32 devices in a mesh: dp: 8 (over z, y), mp: 4 (over x, core).
Axes of the slice: x: 2, y: 2, z: 4, core: 2. Of those that a mesh axis runs over, the one named last changes fastest.
Arguments:
- tokens: bfloat16 [2, 12288, 384], P(None, ('dp', 'mp')), may hold values from -6 to 6
- crop_counts: int32 [2, 16], P(None, 'dp'), may hold values from 2 to 10, as said below
- slot_live: int32 [8], replicated, may hold values from 0 to 1, as said below
- block_w: float32 [2, 384, 4, 1280], P(None, None, 'mp', 'dp')
- block_m: float32 [2, 384, 4, 1280], P(None, None, 'mp', 'dp'), may hold values from -7.1525574e-07 to 7.1525574e-07
- block_v: float32 [2, 384, 4, 1280], P(None, None, 'mp', 'dp'), may hold values from 2.5268668e-14 to 4.042987e-13
- rotation_bases: float32 [2, 4, 384, 384], replicated, as said below
- precond_stats: float32 [2, 4, 384, 384], replicated, as said below
- head_w: float32 [2688, 2048], P('dp')
- head_m: float32 [2688, 2048], P('dp'), may hold values from -1.66893e-06 to 1.66893e-06
- head_v: float32 [2688, 2048], P('dp'), may hold values from 4.767673e-16 to 7.628277e-15
- proto_w: float32 [256, 65536], P('dp', 'mp'), may hold values from -2 to 2
- proto_m: float32 [256, 65536], P('dp', 'mp'), may hold values from -1.66893e-06 to 1.66893e-06
- proto_v: float32 [256, 65536], P('dp', 'mp'), may hold values from 4.767673e-16 to 7.628277e-15
- norm_params: float32 [10, 384], replicated
- norm_m: float32 [10, 384], replicated, may hold values from -1.5258789e-05 to 1.5258789e-05
- norm_v: float32 [10, 384], replicated, may hold values from 4.7676733e-14 to 7.6282774e-13
- teacher_block: float32 [2, 384, 4, 1280], P(None, None, 'mp', 'dp')
- teacher_head: float32 [2688, 2048], P('dp')
- teacher_proto: float32 [256, 65536], P('dp', 'mp'), may hold values from -2 to 2
- teacher_norm: float32 [10, 384], replicated
- center: float32 [65536], P('mp'), may hold values from -0.75 to 0.75
Outputs:
- distill_loss: float32 [], replicated
- grad_norm: float32 [], replicated
- new_block_w: float32 [2, 384, 4, 1280], P(None, None, 'mp', 'dp')
- new_block_m: float32 [2, 384, 4, 1280], P(None, None, 'mp', 'dp')
- new_block_v: float32 [2, 384, 4, 1280], P(None, None, 'mp', 'dp')
- new_bases: float32 [2, 4, 384, 384], replicated
- new_stats: float32 [2, 4, 384, 384], replicated
- new_head_w: float32 [2688, 2048], P('dp')
- new_head_m: float32 [2688, 2048], P('dp')
- new_head_v: float32 [2688, 2048], P('dp')
- new_proto_w: float32 [256, 65536], P('dp', 'mp')
- new_proto_m: float32 [256, 65536], P('dp', 'mp')
- new_proto_v: float32 [256, 65536], P('dp', 'mp')
- new_norm: float32 [10, 384], replicated
- new_norm_m: float32 [10, 384], replicated
- new_norm_v: float32 [10, 384], replicated
- new_teacher_block: float32 [2, 384, 4, 1280], P(None, None, 'mp', 'dp')
- new_teacher_head: float32 [2688, 2048], P('dp')
- new_teacher_proto: float32 [256, 65536], P('dp', 'mp')
- new_teacher_norm: float32 [10, 384], replicated
- new_center: float32 [65536], P('mp')
The draws below stay inside these ranges and needn't reach their ends.
Inputs may be any that keep to these rules, and one draw needn't show every extreme that they name: `crop_counts`: local crops of each image; both 2 and 10 occur in every draw. `slot_live`: 1 marks a slot that holds a head; exactly 6 ones, each group of 2 slots of one index of mp holding one or two. `rotation_bases`: each of the matrices is orthonormal. `precond_stats`: each of the matrices is symmetric positive definite.
All inputs are finite; a program needn't handle non-finite values.
Results may differ from the reference program's by a relative error of at most 0.0085.
The reference program's roundings to bfloat16 on the way count: a program that leaves them out, or rounds other values in their place, can miss the bound.
Values may be sent and summed in bfloat16 or wider, within the bound.
No kernel may reach another device: no remote copies, remote signals or barrier semaphores. Data moves between devices by JAX's collectives and lax.ppermute only.
A program may use at most 384 MiB of HBM per device.

```python
import math
import jax
import jax.numpy as jnp
import numpy as np
from jax import lax

D = 384
HEADS = 6
HD = 64
FF = 1536
HID = 2048
BOT = 256
PROTO = 65536
LAYERS = 2
SLOT_DEV = 2
GLOBAL_TOK = 197
LOCAL_TOK = 37
MAX_LOCAL = 10
IMG_ROWS = 768
STEP = 10
MICRO = 2
IMG_DEV = 4
CROPS = 12
IMAGES = 32
NORM_ROWS = 10
COLS = 1280
HEAD_ROWS = 2688
PARAMS = 26218240
N_DP = 8
N_MP = 4


def draw_crop_counts(key, part):
    key_one, key_two, key_three = jax.random.split(jax.random.fold_in(key, 1), 3)
    counts = jax.random.randint(key_one, (IMAGES,), 2, MAX_LOCAL + 1)
    high_at = jax.random.randint(key_two, (), 0, IMAGES)
    low_at = (high_at + 1 + jax.random.randint(key_three, (), 0, IMAGES - 1)) % IMAGES
    counts = counts.at[high_at].set(MAX_LOCAL).at[low_at].set(2)
    return counts.reshape(MICRO, IMAGES // MICRO).astype(jnp.int32)


def draw_slot_live(key, part):
    key_one, key_two = jax.random.split(jax.random.fold_in(key, 2))
    shuffled = jax.random.permutation(key_one, N_MP)
    dead_count = SLOT_DEV * N_MP - HEADS
    dead_device = jnp.zeros((N_MP,), jnp.int32).at[shuffled[:dead_count]].set(1)
    which_slot = jax.random.randint(key_two, (N_MP,), 0, SLOT_DEV)
    slot_ids = jnp.arange(SLOT_DEV)
    dead_slot = dead_device[:, None] * (slot_ids[None, :] == which_slot[:, None]).astype(jnp.int32)
    return (1 - dead_slot).reshape(-1).astype(jnp.int32)


def block_scales():
    col_ids = jnp.arange(COLS)
    width = SLOT_DEV * HD
    ff_shard = FF // N_MP
    return jnp.where(col_ids < 3 * width, D ** (-0.5), jnp.where(col_ids < 4 * width, 8.0 * (N_MP * width) ** (-0.5), jnp.where(col_ids < 4 * width + ff_shard, D ** (-0.5), FF ** (-0.5))))


def draw_block_w(key, part):
    return jax.random.normal(jax.random.fold_in(key, 3), (LAYERS, D, N_MP, COLS), jnp.float32) * block_scales()


def draw_teacher_block(key, part):
    return jax.random.normal(jax.random.fold_in(key, 4), (LAYERS, D, N_MP, COLS), jnp.float32) * block_scales()


def head_draw(key):
    row_ids = jnp.arange(HEAD_ROWS)[:, None]
    factor = jnp.where(row_ids < D, D ** (-0.5), HID ** (-0.5))
    return jax.random.normal(key, (HEAD_ROWS, HID), jnp.float32) * factor


def draw_head_w(key, part):
    return head_draw(jax.random.fold_in(key, 5))


def draw_teacher_head(key, part):
    return head_draw(jax.random.fold_in(key, 6))


def norm_draw(key):
    key_one, key_two = jax.random.split(key)
    gains_part = 1.0 + 0.2 * jax.random.uniform(key_one, (NORM_ROWS, D), jnp.float32, -1.0, 1.0)
    biases_part = 0.2 * jax.random.normal(key_two, (NORM_ROWS, D), jnp.float32)
    even_row = (jnp.arange(NORM_ROWS) % 2 == 0)[:, None]
    return jnp.where(even_row, gains_part, biases_part)


def draw_norm_params(key, part):
    return norm_draw(jax.random.fold_in(key, 7))


def draw_teacher_norm(key, part):
    return norm_draw(jax.random.fold_in(key, 8))


def draw_rotation_bases(key, part):
    angles = jax.random.uniform(jax.random.fold_in(key, 9), (LAYERS, 4, D // 2), jnp.float32, -math.pi, math.pi)
    row_ids = jnp.arange(D)[:, None]
    col_ids = jnp.arange(D)[None, :]
    angle = angles[:, :, row_ids // 2]
    cosine = jnp.cos(angle)
    sine = jnp.sin(angle)
    upper_pair = (row_ids % 2 == 0) & (col_ids == row_ids + 1)
    lower_pair = (row_ids % 2 == 1) & (col_ids == row_ids - 1)
    return jnp.where(row_ids == col_ids, cosine, jnp.where(upper_pair, -sine, jnp.where(lower_pair, sine, 0.0))).astype(jnp.float32)


def draw_precond_stats(key, part):
    key_one, key_two = jax.random.split(jax.random.fold_in(key, 10))
    gaussian = jax.random.normal(key_one, (LAYERS, 4, D, D), jnp.float32)
    symmetric = (gaussian + jnp.swapaxes(gaussian, 2, 3)) * (0.2 / math.sqrt(2.0 * D))
    magnitude = 2.5e-05 * 0.05 * 4 * D / PARAMS * jax.random.uniform(key_two, (LAYERS, 4, 1, 1), jnp.float32, 1.0, 4.0)
    return (jnp.eye(D, dtype=jnp.float32)[None, None] + symmetric) * magnitude


def steps_of(key, extent, pieces, smallest, largest):
    loudness, own = 1.0, jax.random.fold_in(key, 6)
    for position, blocks in pieces:
        draws = jnp.exp(jax.random.uniform(jax.random.fold_in(own, position), (blocks,), jnp.float32, smallest / len(pieces), largest / len(pieces)))
        loudness = loudness * jnp.repeat(draws, extent[position] // blocks).reshape([-1 if axis == position else 1 for axis in range(len(extent))])
    return loudness


def noise(own_key, dims, scale, most, cuts=(), kind=jnp.bfloat16):
    drawn = scale * jax.random.normal(own_key, dims, jnp.float32)
    if cuts:
        drawn = drawn * steps_of(own_key, dims, cuts, -0.22, 0.18)
    return jnp.clip(drawn, -most, most).astype(kind)


def setup_inputs(seed: int = 0) -> dict:
    seeds = jax.random.split(jax.random.key(seed), 23)
    tokens = noise(seeds[0], (MICRO, IMAGES // MICRO * IMG_ROWS, D), 1.0, 6.0, ((1, 32),))
    crop_counts = draw_crop_counts(jax.random.fold_in(seeds[22], 71), 0)
    slot_live = draw_slot_live(jax.random.fold_in(seeds[22], 71), 0)
    block_w = draw_block_w(jax.random.fold_in(seeds[22], 71), 0)
    block_m = noise(seeds[4], (LAYERS, D, N_MP, COLS), (0.053 * 0.005 / PARAMS ** 0.5), 7.152557373046875e-07, ((2, 4), (3, 8)), jnp.float32)
    block_v = jnp.clip(jnp.exp(math.log(4.0429869196424717e-13) - 2.7725887 * jax.random.uniform(seeds[5], (LAYERS, D, N_MP, COLS), jnp.float32) ** steps_of(seeds[5], (LAYERS, D, N_MP, COLS), ((2, 4), (3, 8)), -0.2, 0.2)), 2.5268668247765448e-14, 4.0429869196424717e-13)
    rotation_bases = draw_rotation_bases(jax.random.fold_in(seeds[22], 71), 0)
    precond_stats = draw_precond_stats(jax.random.fold_in(seeds[22], 71), 0)
    head_w = draw_head_w(jax.random.fold_in(seeds[22], 71), 0)
    head_m = noise(seeds[9], (HEAD_ROWS, HID), (0.11 * 0.005 / PARAMS ** 0.5), 1.6689300537109375e-06, ((0, 8),), jnp.float32)
    head_v = jnp.clip(jnp.exp(math.log(7.628277079018558e-15) - 2.7725887 * jax.random.uniform(seeds[10], (HEAD_ROWS, HID), jnp.float32) ** steps_of(seeds[10], (HEAD_ROWS, HID), ((0, 8),), -0.2, 0.2)), 4.767673174386599e-16, 7.628277079018558e-15)
    proto_w = noise(seeds[11], (BOT, PROTO), 0.15, 2.0, ((0, 8), (1, 4)), jnp.float32)
    proto_m = noise(seeds[12], (BOT, PROTO), (0.11 * 0.005 / PARAMS ** 0.5), 1.6689300537109375e-06, ((0, 8), (1, 4)), jnp.float32)
    proto_v = jnp.clip(jnp.exp(math.log(7.628277079018558e-15) - 2.7725887 * jax.random.uniform(seeds[13], (BOT, PROTO), jnp.float32) ** steps_of(seeds[13], (BOT, PROTO), ((0, 8), (1, 4)), -0.2, 0.2)), 4.767673174386599e-16, 7.628277079018558e-15)
    norm_params = draw_norm_params(jax.random.fold_in(seeds[22], 71), 0)
    norm_m = noise(seeds[15], (NORM_ROWS, D), (0.11 * 0.05 / PARAMS ** 0.5), 1.52587890625e-05, (), jnp.float32)
    norm_v = jnp.clip(jnp.exp(jax.random.uniform(seeds[16], (NORM_ROWS, D), jnp.float32, math.log(4.7676733437931884e-14), math.log(7.628277350069101e-13))), 4.7676733437931884e-14, 7.628277350069101e-13)
    teacher_block = draw_teacher_block(jax.random.fold_in(seeds[22], 71), 0)
    teacher_head = draw_teacher_head(jax.random.fold_in(seeds[22], 71), 0)
    teacher_proto = noise(seeds[19], (BOT, PROTO), 0.15, 2.0, ((0, 8), (1, 4)), jnp.float32)
    teacher_norm = draw_teacher_norm(jax.random.fold_in(seeds[22], 71), 0)
    center = noise(seeds[21], (PROTO,), 0.05, 0.75, ((0, 4),), jnp.float32)
    return {"tokens": tokens, "crop_counts": crop_counts, "slot_live": slot_live, "block_w": block_w, "block_m": block_m, "block_v": block_v, "rotation_bases": rotation_bases, "precond_stats": precond_stats, "head_w": head_w, "head_m": head_m, "head_v": head_v, "proto_w": proto_w, "proto_m": proto_m, "proto_v": proto_v, "norm_params": norm_params, "norm_m": norm_m, "norm_v": norm_v, "teacher_block": teacher_block, "teacher_head": teacher_head, "teacher_proto": teacher_proto, "teacher_norm": teacher_norm, "center": center}


precise = lax.Precision.HIGHEST
TAU_S = 0.1
TAU_T = 0.07
CLIP_NORM = 0.005
BETA_ONE = 0.9
BETA_TWO = 0.999
ROT_ONE = 0.95
ROT_TWO = 0.95
SHAMPOO_BETA = 0.95
ADAM_EPS = 1e-08
WEIGHT_DECAY = 0.04
LR_BLOCK = 0.05
LR_HEAD = 0.03
LR_PROTO = 0.1
LR_NORM = 0.2
TEACHER_MOM = 0.7
CENTER_MOM = 0.9

@jax.custom_vjp
def low(v):
    return lax.optimization_barrier(v.astype(jnp.bfloat16)).astype(jnp.float32)

@jax.custom_vjp
def low_back(v):
    return v

def low_keep(v):
    return (low(v), None)

def low_pass(kept, grad):
    return (grad,)

def back_keep(v):
    return (v, None)

def back_low(kept, grad):
    return (low(grad),)
low.defvjp(low_keep, low_pass)
low_back.defvjp(back_keep, back_low)

def norm_rows(inputs, gain_vec, bias_vec):
    row_mean = lax.optimization_barrier(jnp.mean(inputs, axis=-1, keepdims=True))
    centred = inputs - row_mean
    spread = lax.optimization_barrier(jnp.mean(centred * centred, axis=-1, keepdims=True))
    return centred * lax.rsqrt(spread + 1e-06) * gain_vec + bias_vec

def gelu_exact(inputs):
    return jax.nn.gelu(inputs, approximate=False)

def unit_rows(inputs):
    return inputs * lax.rsqrt(lax.optimization_barrier(jnp.sum(inputs * inputs, axis=-1, keepdims=True)) + 1e-06)

def crop_mask(crop_count):
    row_ids = jnp.arange(IMG_ROWS)
    segment = jnp.where(row_ids < 2 * GLOBAL_TOK, row_ids // GLOBAL_TOK, 2 + (row_ids - 2 * GLOBAL_TOK) // LOCAL_TOK)
    segment = jnp.minimum(segment, 2 + MAX_LOCAL)
    alive_row = segment < 2 + crop_count
    same_crop = (segment[:, None] == segment[None, :]) & alive_row[:, None]
    return same_crop | jnp.eye(IMG_ROWS, dtype=bool)

def cls_starts():
    return np.array([0, GLOBAL_TOK] + [2 * GLOBAL_TOK + local_id * LOCAL_TOK for local_id in range(MAX_LOCAL)], np.int32)

def split_block(weights):
    width = SLOT_DEV * HD
    ff_shard = FF // N_MP
    qkv_w = weights[:, :, :3 * width].reshape(D, N_MP, 3, SLOT_DEV, HD)
    qkv_w = jnp.transpose(qkv_w, (0, 2, 1, 3, 4)).reshape(D, 3, N_MP * SLOT_DEV, HD)
    proj_t = weights[:, :, 3 * width:4 * width].reshape(D, N_MP * SLOT_DEV, HD)
    up_w = weights[:, :, 4 * width:4 * width + ff_shard].reshape(D, N_MP * ff_shard)
    down_t = weights[:, :, 4 * width + ff_shard:].reshape(D, N_MP * ff_shard)
    return (qkv_w, proj_t, up_w, down_t)

def run_block(layer_w, gains, inputs, allowed, slot_alive):
    qkv_w, proj_t, up_w, down_t = split_block(low(layer_w))
    normed = low(norm_rows(inputs, gains[0], gains[1]))
    qkv_all = low_back(low(jnp.einsum('rd,dcnh->crnh', normed, qkv_w, precision=precise)))
    scores = low_back(jnp.einsum('qnh,knh->nqk', qkv_all[0], qkv_all[1], precision=precise) * HD ** (-0.5))
    expd_scores = jnp.where(allowed[None], jnp.exp(scores), 0.0)
    attn_probs = expd_scores / lax.optimization_barrier(jnp.sum(expd_scores, axis=-1, keepdims=True))
    attn_mix = jnp.einsum('nqk,knh->qnh', low(attn_probs), qkv_all[2], precision=precise)
    attn_mix = low_back(low(attn_mix * slot_alive[None, :, None]))
    attended = low_back(jnp.einsum('qnh,dnh->qd', attn_mix, proj_t, precision=precise))
    middle = inputs + attended
    hidden_in = low(norm_rows(middle, gains[2], gains[3]))
    up_proj = low_back(jnp.dot(hidden_in, up_w, precision=precise))
    hidden = low(gelu_exact(up_proj))
    return middle + low_back(jnp.dot(hidden, down_t.T, precision=precise))

def image_logits(params, tokens_img, crop_count, slot_alive):
    block_w, head_w, proto_w, norm_params = params
    allowed = crop_mask(crop_count)
    output = tokens_img
    for layer in range(LAYERS):
        output = run_block(block_w[layer], norm_params[4 * layer:4 * layer + 4], output, allowed, slot_alive)
    cls_rows = output[cls_starts()]
    features = low(norm_rows(cls_rows, norm_params[4 * LAYERS], norm_params[4 * LAYERS + 1]))
    head_full = low(head_w)
    first_out = low_back(jnp.dot(features, head_full[:D], precision=precise))
    act_one = low(gelu_exact(first_out))
    second = low_back(jnp.dot(act_one, head_full[D:D + HID], precision=precise))
    act_two = low(gelu_exact(second))
    third_out = low_back(jnp.dot(act_two, head_full[D + HID:].T, precision=precise))
    unit_out = low(unit_rows(third_out))
    return low_back(jnp.dot(unit_out, low(proto_w), precision=precise))

def image_loss(params, tokens_img, crop_count, teacher_out, center, slot_alive):
    student = image_logits(params, tokens_img, crop_count, slot_alive) / TAU_S
    targets = jax.nn.softmax((teacher_out - center) / TAU_T, axis=-1)
    log_probs = jax.nn.log_softmax(student, axis=-1)
    cross = -jnp.dot(targets, log_probs.T, precision=precise)
    crop_ids = jnp.arange(CROPS)
    pairs = (crop_ids[None, :] != jnp.arange(2)[:, None]) & (crop_ids[None, :] < 2 + crop_count)
    return jnp.sum(jnp.where(pairs, cross, 0.0)) / (2.0 * crop_count + 2.0)

def adam_direction(first_mom, second_mom, beta_one, beta_two):
    return first_mom / (1 - beta_one ** STEP) / (jnp.sqrt(second_mom / (1 - beta_two ** STEP)) + ADAM_EPS)

def adamw(weight, grad_in, first_mom, second_mom, rate, decay):
    first_mom = BETA_ONE * first_mom + (1 - BETA_ONE) * grad_in
    second_mom = BETA_TWO * second_mom + (1 - BETA_TWO) * grad_in * grad_in
    weight = weight - rate * (adam_direction(first_mom, second_mom, BETA_ONE, BETA_TWO) + decay * weight)
    return (weight, first_mom, second_mom)

def renew_basis(stat_new, basis):
    turned = jnp.dot(stat_new, basis, precision=precise)
    gram = jnp.dot(turned.T, turned, precision=precise)
    lower = jnp.linalg.cholesky(gram)
    return jax.scipy.linalg.solve_triangular(lower, turned.T, lower=True).T

def take_cols(array, lower_col, upper_col):
    return array[:, :, lower_col:upper_col].reshape(D, -1)

def reference(tokens, crop_counts, slot_live, block_w, block_m, block_v, rotation_bases, precond_stats, head_w, head_m, head_v, proto_w, proto_m, proto_v, norm_params, norm_m, norm_v, teacher_block, teacher_head, teacher_proto, teacher_norm, center):
    slot_alive = slot_live.astype(jnp.float32)
    images_x = tokens.astype(jnp.float32).reshape(N_DP * IMG_DEV, IMG_ROWS, D)
    counts_flat = crop_counts.reshape(N_DP * IMG_DEV)
    teacher_params = (teacher_block, teacher_head, teacher_proto, teacher_norm)

    def teach(carry, block_item):
        tokens_img, crop_count = block_item
        teacher_out = image_logits(teacher_params, tokens_img, crop_count, slot_alive)[:2]
        return (carry + lax.optimization_barrier(jnp.sum(teacher_out, axis=0)), teacher_out)
    center_sum, teacher_glob = lax.scan(teach, jnp.zeros((PROTO,), jnp.float32), (images_x, counts_flat))

    def objective(params):

        def step_one(carry, block_item):
            tokens_img, crop_count, teacher_out = block_item
            return (carry + image_loss(params, tokens_img, crop_count, teacher_out, center, slot_alive), None)
        loss_sum, unused = lax.scan(jax.checkpoint(step_one), jnp.zeros((), jnp.float32), (images_x, counts_flat, teacher_glob))
        return loss_sum
    params = (block_w, head_w, proto_w, norm_params)
    distill_loss, pullback = jax.vjp(objective, params)
    grad_block, grad_head, grad_proto, grad_norm_params = pullback(jnp.ones((), jnp.float32))[0]
    grad_norm = jnp.sqrt(jnp.sum(grad_block * grad_block) + jnp.sum(grad_head * grad_head) + jnp.sum(grad_proto * grad_proto) + jnp.sum(grad_norm_params * grad_norm_params))
    clip_factor = jnp.minimum(1.0, CLIP_NORM / (grad_norm + 1e-06))
    width = SLOT_DEV * HD
    ff_shard = FF // N_MP
    bounds = [0, 3 * width, 4 * width, 4 * width + ff_shard, 4 * width + 2 * ff_shard]
    layer_w, layer_m, layer_v, layer_bases, layer_stats = ([], [], [], [], [])
    for layer in range(LAYERS):
        new_w, new_m, new_v, new_bases, new_stats = ([], [], [], [], [])
        for matrix_id in range(4):
            lower_col, upper_col = (bounds[matrix_id], bounds[matrix_id + 1])
            grad_cols = clip_factor * take_cols(grad_block[layer], lower_col, upper_col)
            stat_new = SHAMPOO_BETA * precond_stats[layer, matrix_id] + (1 - SHAMPOO_BETA) * jnp.dot(grad_cols, grad_cols.T, precision=precise)
            basis = renew_basis(stat_new, rotation_bases[layer, matrix_id])
            rotated = jnp.dot(basis.T, grad_cols, precision=precise)
            first_mom = ROT_ONE * take_cols(block_m[layer], lower_col, upper_col) + (1 - ROT_ONE) * rotated
            second_mom = ROT_TWO * take_cols(block_v[layer], lower_col, upper_col) + (1 - ROT_TWO) * rotated * rotated
            direction = adam_direction(first_mom, second_mom, ROT_ONE, ROT_TWO)
            weight = take_cols(block_w[layer], lower_col, upper_col)
            weight = weight - LR_BLOCK * (jnp.dot(basis, direction, precision=precise) + WEIGHT_DECAY * weight)
            shape_back = (D, N_MP, upper_col - lower_col)
            new_w.append(weight.reshape(shape_back))
            new_m.append(first_mom.reshape(shape_back))
            new_v.append(second_mom.reshape(shape_back))
            new_bases.append(basis)
            new_stats.append(stat_new)
        layer_w.append(jnp.concatenate(new_w, axis=2))
        layer_m.append(jnp.concatenate(new_m, axis=2))
        layer_v.append(jnp.concatenate(new_v, axis=2))
        layer_bases.append(jnp.stack(new_bases))
        layer_stats.append(jnp.stack(new_stats))
    new_block_w = jnp.stack(layer_w)
    new_block_m = jnp.stack(layer_m)
    new_block_v = jnp.stack(layer_v)
    new_head_w, new_head_m, new_head_v = adamw(head_w, clip_factor * grad_head, head_m, head_v, LR_HEAD, WEIGHT_DECAY)
    new_proto_w, new_proto_m, new_proto_v = adamw(proto_w, clip_factor * grad_proto, proto_m, proto_v, LR_PROTO, WEIGHT_DECAY)
    new_norm, new_norm_m, new_norm_v = adamw(norm_params, clip_factor * grad_norm_params, norm_m, norm_v, LR_NORM, 0.0)
    new_teacher_block = TEACHER_MOM * teacher_block + (1 - TEACHER_MOM) * new_block_w
    new_teacher_head = TEACHER_MOM * teacher_head + (1 - TEACHER_MOM) * new_head_w
    new_teacher_proto = TEACHER_MOM * teacher_proto + (1 - TEACHER_MOM) * new_proto_w
    new_teacher_norm = TEACHER_MOM * teacher_norm + (1 - TEACHER_MOM) * new_norm
    new_center = CENTER_MOM * center + (1 - CENTER_MOM) * center_sum / (2.0 * N_DP * IMG_DEV)
    return (distill_loss, grad_norm, new_block_w, new_block_m, new_block_v, jnp.stack(layer_bases), jnp.stack(layer_stats), new_head_w, new_head_m, new_head_v, new_proto_w, new_proto_m, new_proto_v, new_norm, new_norm_m, new_norm_v, new_teacher_block, new_teacher_head, new_teacher_proto, new_teacher_norm, new_center)
```

```python
import functools

import jax
import jax.numpy as jnp
from jax import lax
from jax.experimental import pallas as pl
from jax.experimental.pallas import tpu as pltpu
from jax.sharding import PartitionSpec as P

D = 384
HD = 64
HID = 2048
LAYERS = 2
SLOT_DEV = 2
GLOBAL_TOK = 197
LOCAL_TOK = 37
MAX_LOCAL = 10
IMG_ROWS = 768
STEP = 10
MICRO = 2
CROPS = 12
GLOBAL_PAD = 200
LOCAL_PAD = 40
CHUNK = 400
CLS = 16

precise = lax.Precision.HIGHEST
TAU_S = 0.1
TAU_T = 0.07
CLIP_NORM = 0.005
BETA_ONE = 0.9
BETA_TWO = 0.999
ROT_ONE = 0.95
ROT_TWO = 0.95
SHAMPOO_BETA = 0.95
ADAM_EPS = 1e-08
WEIGHT_DECAY = 0.04
LR_BLOCK = 0.05
LR_HEAD = 0.03
LR_PROTO = 0.1
LR_NORM = 0.2
TEACHER_MOM = 0.7
CENTER_MOM = 0.9
NN = (((1,), (0,)), ((), ()))
NT = (((1,), (1,)), ((), ()))
TN = (((0,), (0,)), ((), ()))
bf16 = jnp.bfloat16
f32 = jnp.float32
VMEM_LIMIT = 58 * 1024 * 1024


def mm(lhs, rhs, dims=NN, precision=None):
    return lax.dot_general(lhs, rhs, dims, precision=precision, preferred_element_type=f32)


def normalize(inputs):
    centred = inputs - jnp.mean(inputs, axis=-1, keepdims=True)
    spread = jnp.mean(centred * centred, axis=-1, keepdims=True)
    inv = lax.rsqrt(spread + 1e-06)
    return centred * inv, inv


def norm_rows(inputs, gain, bias):
    return normalize(inputs)[0] * gain + bias


def norm_back(inputs, gain, grad_out):
    unit, inv = normalize(inputs)
    scaled = grad_out * gain
    grad = inv * (
        scaled
        - jnp.mean(scaled, axis=-1, keepdims=True)
        - unit * jnp.mean(scaled * unit, axis=-1, keepdims=True)
    )
    return (
        grad,
        jnp.sum(grad_out * unit, axis=0, keepdims=True),
        jnp.sum(grad_out, axis=0, keepdims=True),
    )


def gelu_cdf(inputs):
    return 0.5 + 0.5 * lax.erf(inputs * (0.5**0.5))


def gelu_exact(inputs):
    return inputs * gelu_cdf(inputs)


def gelu_slope(inputs):
    return gelu_cdf(inputs) + inputs * (jnp.exp(-0.5 * inputs * inputs) * 0.3989422804014327)


def low_half(shape):
    return lax.broadcasted_iota(jnp.int32, shape, 1) < HD


def halves(array):
    low = low_half(array.shape)
    zero = jnp.zeros_like(array)
    return jnp.where(low, array, zero), jnp.where(low, zero, array)


def block_fwd_kernel(
    x_ref, wt_ref, gains_ref, seg_col_ref, seg_row_ref, slot_ref,
    out_ref, h1_ref, qkv_ref, o_ref, x2_ref,
):
    x = x_ref[...]
    h1 = norm_rows(x, gains_ref[0:1], gains_ref[1:2]).astype(bf16)
    h1_ref[...] = h1
    allowed = seg_col_ref[0] == seg_row_ref[0]

    def heads(group, att):
        qkv = mm(h1, wt_ref[group, 0:384], NT).astype(bf16)
        qkv_ref[group] = qkv
        keys, values = qkv[:, 128:256], qkv[:, 256:384]
        mixes = []
        for query in halves(qkv[:, 0:128]):
            expd = jnp.where(allowed, jnp.exp(mm(query, keys, NT) * HD ** (-0.5)), 0.0)
            prob = expd / jnp.sum(expd, axis=-1, keepdims=True)
            mixes.append(mm(prob.astype(bf16), values))
        mix = jnp.where(low_half(mixes[0].shape), mixes[0], mixes[1])
        mix = (mix * slot_ref[group]).astype(bf16)
        o_ref[group] = mix
        return att + mm(mix, wt_ref[group, 384:512])

    att = lax.fori_loop(0, wt_ref.shape[0], heads, jnp.zeros(x.shape, f32))
    x2 = x + att
    x2_ref[...] = x2
    h2 = norm_rows(x2, gains_ref[2:3], gains_ref[3:4]).astype(bf16)

    def units(group, total):
        hidden = gelu_exact(mm(h2, wt_ref[group, 512:896], NT)).astype(bf16)
        return total + mm(hidden, wt_ref[group, 896:1280])

    out_ref[...] = x2 + lax.fori_loop(0, wt_ref.shape[0], units, jnp.zeros(x.shape, f32))


def block_bwd_kernel(
    x_ref, wt_ref, gains_ref, seg_col_ref, seg_row_ref, slot_ref,
    h1_ref, qkv_ref, o_ref, x2_ref, grad_ref,
    dwt_ref, dgains_ref,
):
    @pl.when(pl.program_id(0) == 0)
    def _():
        dwt_ref[...] = jnp.zeros_like(dwt_ref)
        dgains_ref[...] = jnp.zeros_like(dgains_ref)

    grad = grad_ref[...]
    grad_low = grad.astype(bf16)
    x2 = x2_ref[...]
    h2 = norm_rows(x2, gains_ref[2:3], gains_ref[3:4]).astype(bf16)

    def units(group, total):
        up = mm(h2, wt_ref[group, 512:896], NT)
        hidden = gelu_exact(up).astype(bf16)
        grad_up = (mm(grad_low, wt_ref[group, 896:1280], NT) * gelu_slope(up)).astype(bf16)
        dwt_ref[group, 512:896] += mm(grad_up, h2, TN)
        dwt_ref[group, 896:1280] += mm(hidden, grad_low, TN)
        return total + mm(grad_up, wt_ref[group, 512:896])

    groups = wt_ref.shape[0]
    grad_h2 = lax.fori_loop(0, groups, units, jnp.zeros(grad.shape, f32))
    grad_x2, gain_two, bias_two = norm_back(x2, gains_ref[2:3], grad_h2)
    grad_att = (grad + grad_x2).astype(bf16)
    allowed = seg_col_ref[0] == seg_row_ref[0]
    h1 = h1_ref[...]

    def heads(group, total):
        grad_mix = mm(grad_att, wt_ref[group, 384:512], NT).astype(bf16)
        grad_mix = grad_mix * slot_ref[group].astype(bf16)
        dwt_ref[group, 384:512] += mm(o_ref[group], grad_att, TN)
        qkv = qkv_ref[group]
        keys, values = qkv[:, 128:256], qkv[:, 256:384]
        grad_values = jnp.zeros(values.shape, f32)
        grad_keys = jnp.zeros(values.shape, f32)
        grad_queries = []
        for query, gmix in zip(halves(qkv[:, 0:128]), halves(grad_mix)):
            expd = jnp.where(allowed, jnp.exp(mm(query, keys, NT) * HD ** (-0.5)), 0.0)
            prob = expd / jnp.sum(expd, axis=-1, keepdims=True)
            grad_values = grad_values + mm(prob.astype(bf16), gmix, TN)
            grad_prob = mm(gmix, values, NT)
            scored = prob * (grad_prob - jnp.sum(prob * grad_prob, axis=-1, keepdims=True))
            scored = scored.astype(bf16)
            grad_queries.append(mm(scored, keys))
            grad_keys = grad_keys + mm(scored, query, TN)
        low = low_half(grad_queries[0].shape)
        grad_query = jnp.where(low, grad_queries[0], grad_queries[1]) * HD ** (-0.5)
        grad_qkv = jnp.concatenate(
            [grad_query.astype(bf16), (grad_keys * HD ** (-0.5)).astype(bf16), grad_values.astype(bf16)],
            axis=1,
        )
        dwt_ref[group, 0:384] += mm(grad_qkv, h1, TN)
        return total + mm(grad_qkv, wt_ref[group, 0:384])

    grad_h1 = lax.fori_loop(0, groups, heads, jnp.zeros(grad.shape, f32))
    _, gain_one, bias_one = norm_back(x_ref[...], gains_ref[0:1], grad_h1)
    dgains_ref[...] += jnp.concatenate([gain_one, bias_one, gain_two, bias_two], axis=0)


def whole_spec(shape):
    return pl.BlockSpec(shape, lambda *_: (0,) * len(shape))


def block_specs(groups, layer):
    row = pl.BlockSpec((CHUNK, D), lambda c: (c, 0))
    return dict(
        row=row,
        wt=pl.BlockSpec((groups, 1280, D), lambda c: (0, 0, layer)),
        gains=whole_spec((4, D)),
        seg_col=pl.BlockSpec((1, CHUNK, 1), lambda c: (c, 0, 0)),
        seg_row=pl.BlockSpec((1, 1, CHUNK), lambda c: (c, 0, 0)),
        slot=whole_spec((groups, 1, 128)),
        qkv=pl.BlockSpec((groups, CHUNK, 384), lambda c: (0, c, 0)),
        mix=pl.BlockSpec((groups, CHUNK, 128), lambda c: (0, c, 0)),
    )


def block_fwd(x, weights, layer, gains, seg_col, seg_row, slot):
    rows, groups = x.shape[0], weights.shape[0]
    s = block_specs(groups, layer)
    return pl.pallas_call(
        block_fwd_kernel,
        grid=(rows // CHUNK,),
        in_specs=[s["row"], s["wt"], s["gains"], s["seg_col"], s["seg_row"], s["slot"]],
        out_specs=[s["row"], s["row"], s["qkv"], s["mix"], s["row"]],
        out_shape=[
            jax.ShapeDtypeStruct((rows, D), f32),
            jax.ShapeDtypeStruct((rows, D), bf16),
            jax.ShapeDtypeStruct((groups, rows, 384), bf16),
            jax.ShapeDtypeStruct((groups, rows, 128), bf16),
            jax.ShapeDtypeStruct((rows, D), f32),
        ],
        compiler_params=pltpu.CompilerParams(vmem_limit_bytes=VMEM_LIMIT),
        cost_estimate=pl.CostEstimate(
            flops=rows * 9_000_000, bytes_accessed=8_000_000, transcendentals=rows * 4000
        ),
    )(x, weights, gains, seg_col, seg_row, slot)


def block_bwd(x, weights, layer, gains, seg_col, seg_row, slot, saved, grad):
    rows, groups = x.shape[0], weights.shape[0]
    s = block_specs(groups, layer)
    h1, qkv, mix, x2 = saved
    return pl.pallas_call(
        block_bwd_kernel,
        grid=(rows // CHUNK,),
        in_specs=[
            s["row"], s["wt"], s["gains"], s["seg_col"], s["seg_row"], s["slot"],
            s["row"], s["qkv"], s["mix"], s["row"], s["row"],
        ],
        out_specs=[whole_spec((groups, 1280, D)), whole_spec((4, D))],
        out_shape=[
            jax.ShapeDtypeStruct((groups, 1280, D), f32),
            jax.ShapeDtypeStruct((4, D), f32),
        ],
        compiler_params=pltpu.CompilerParams(vmem_limit_bytes=VMEM_LIMIT),
        cost_estimate=pl.CostEstimate(
            flops=rows * 22_000_000, bytes_accessed=16_000_000, transcendentals=rows * 6000
        ),
    )(x, weights, gains, seg_col, seg_row, slot, h1, qkv, mix, x2, grad)


def crop_starts(crops):
    return [
        crop * GLOBAL_PAD if crop < 2 else 2 * GLOBAL_PAD + (crop - 2) * LOCAL_PAD
        for crop in range(crops)
    ]


def take_cls(ref, crops):
    rows = [ref[start : start + 1, :] for start in crop_starts(crops)]
    return jnp.concatenate(rows + [jnp.zeros((CLS - crops, ref.shape[1]), f32)], axis=0)


def last_fwd_kernel(
    crops, x_ref, wt_ref, gains_ref, seg_cls_ref, seg_row_ref, slot_ref,
    out_ref, h1_ref, kv_ref, q_ref, o_ref, x2_ref,
):
    gain, bias = gains_ref[0:1], gains_ref[1:2]
    h1 = norm_rows(x_ref[...], gain, bias).astype(bf16)
    h1_ref[...] = h1
    x_cls = take_cls(x_ref, crops)
    h1_cls = norm_rows(x_cls, gain, bias).astype(bf16)
    allowed = seg_cls_ref[...] == seg_row_ref[...]

    def heads(group, att):
        kv = mm(h1, wt_ref[group, 128:384], NT).astype(bf16)
        kv_ref[group] = kv
        query = mm(h1_cls, wt_ref[group, 0:128], NT).astype(bf16)
        q_ref[group] = query
        both = jnp.concatenate(halves(query), axis=0)
        scores = mm(both, kv[:, 0:128], NT) * HD ** (-0.5)
        expd = jnp.where(allowed, jnp.exp(scores), 0.0)
        prob = expd / jnp.sum(expd, axis=-1, keepdims=True)
        mix = mm(prob.astype(bf16), kv[:, 128:256])
        mix = jnp.where(low_half((CLS, 128)), mix[0:CLS], mix[CLS:])
        mix = (mix * slot_ref[group]).astype(bf16)
        o_ref[group] = mix
        return att + mm(mix, wt_ref[group, 384:512])

    att = lax.fori_loop(0, wt_ref.shape[0], heads, jnp.zeros((CLS, D), f32))
    x2 = x_cls + att
    x2_ref[...] = x2
    h2 = norm_rows(x2, gains_ref[2:3], gains_ref[3:4]).astype(bf16)

    def units(group, total):
        hidden = gelu_exact(mm(h2, wt_ref[group, 512:896], NT)).astype(bf16)
        return total + mm(hidden, wt_ref[group, 896:1280])

    out_ref[...] = x2 + lax.fori_loop(0, wt_ref.shape[0], units, jnp.zeros((CLS, D), f32))


def last_bwd_kernel(
    crops, x_ref, wt_ref, gains_ref, seg_cls_ref, seg_row_ref, slot_ref,
    h1_ref, kv_ref, q_ref, o_ref, x2_ref, grad_ref,
    dwt_ref, dgains_ref, dx_ref,
):
    grad = grad_ref[...]
    grad_low = grad.astype(bf16)
    x2 = x2_ref[...]
    h2 = norm_rows(x2, gains_ref[2:3], gains_ref[3:4]).astype(bf16)
    groups = wt_ref.shape[0]

    def units(group, total):
        up = mm(h2, wt_ref[group, 512:896], NT)
        hidden = gelu_exact(up).astype(bf16)
        grad_up = (mm(grad_low, wt_ref[group, 896:1280], NT) * gelu_slope(up)).astype(bf16)
        dwt_ref[group, 512:896] = mm(grad_up, h2, TN)
        dwt_ref[group, 896:1280] = mm(hidden, grad_low, TN)
        return total + mm(grad_up, wt_ref[group, 512:896])

    grad_h2 = lax.fori_loop(0, groups, units, jnp.zeros((CLS, D), f32))
    grad_x2, gain_two, bias_two = norm_back(x2, gains_ref[2:3], grad_h2)
    grad_x2 = grad + grad_x2
    grad_att = grad_x2.astype(bf16)
    allowed = seg_cls_ref[...] == seg_row_ref[...]
    h1 = h1_ref[...]
    h1_cls = norm_rows(take_cls(x_ref, crops), gains_ref[0:1], gains_ref[1:2]).astype(bf16)

    def heads(group, carry):
        total, total_cls = carry
        grad_mix = mm(grad_att, wt_ref[group, 384:512], NT).astype(bf16)
        grad_mix = grad_mix * slot_ref[group].astype(bf16)
        dwt_ref[group, 384:512] = mm(o_ref[group], grad_att, TN)
        kv = kv_ref[group]
        keys, values = kv[:, 0:128], kv[:, 128:256]
        both = jnp.concatenate(halves(q_ref[group]), axis=0)
        gboth = jnp.concatenate(halves(grad_mix), axis=0)
        expd = jnp.where(allowed, jnp.exp(mm(both, keys, NT) * HD ** (-0.5)), 0.0)
        prob = expd / jnp.sum(expd, axis=-1, keepdims=True)
        grad_prob = mm(gboth, values, NT)
        scored = prob * (grad_prob - jnp.sum(prob * grad_prob, axis=-1, keepdims=True))
        scored = scored.astype(bf16)
        grad_values = mm(prob.astype(bf16), gboth, TN)
        grad_keys = mm(scored, both, TN) * HD ** (-0.5)
        grad_query = mm(scored, keys)
        low = low_half((CLS, 128))
        grad_query = jnp.where(low, grad_query[0:CLS], grad_query[CLS:]) * HD ** (-0.5)
        grad_query = grad_query.astype(bf16)
        grad_kv = jnp.concatenate([grad_keys.astype(bf16), grad_values.astype(bf16)], axis=1)
        dwt_ref[group, 0:128] = mm(grad_query, h1_cls, TN)
        dwt_ref[group, 128:384] = mm(grad_kv, h1, TN)
        return (
            total + mm(grad_kv, wt_ref[group, 128:384]),
            total_cls + mm(grad_query, wt_ref[group, 0:128]),
        )

    grad_h1, grad_cls = lax.fori_loop(
        0, groups, heads, (jnp.zeros(h1.shape, f32), jnp.zeros((CLS, D), f32))
    )
    dx_ref[...] = grad_h1
    starts = crop_starts(crops)
    for crop, start in enumerate(starts):
        dx_ref[start : start + 1, :] += grad_cls[crop : crop + 1, :]
    grad_x, gain_one, bias_one = norm_back(x_ref[...], gains_ref[0:1], dx_ref[...])
    dx_ref[...] = grad_x
    for crop, start in enumerate(starts):
        dx_ref[start : start + 1, :] += grad_x2[crop : crop + 1, :]
    dgains_ref[...] = jnp.concatenate([gain_one, bias_one, gain_two, bias_two], axis=0)


def last_in_specs(rows, groups, layer):
    return [
        whole_spec((rows, D)),
        pl.BlockSpec((groups, 1280, D), lambda i: (0, 0, layer)),
        whole_spec((4, D)),
        whole_spec((2 * CLS, 1)),
        whole_spec((1, rows)),
        whole_spec((groups, 1, 128)),
    ]


def last_saved(rows, groups):
    return [
        jax.ShapeDtypeStruct((rows, D), bf16),
        jax.ShapeDtypeStruct((groups, rows, 256), bf16),
        jax.ShapeDtypeStruct((groups, CLS, 128), bf16),
        jax.ShapeDtypeStruct((groups, CLS, 128), bf16),
        jax.ShapeDtypeStruct((CLS, D), f32),
    ]


def last_fwd(crops, x, weights, layer, gains, seg_cls, seg_row, slot):
    rows, groups = x.shape[0], weights.shape[0]
    out_shape = [jax.ShapeDtypeStruct((CLS, D), f32)] + last_saved(rows, groups)
    return pl.pallas_call(
        functools.partial(last_fwd_kernel, crops),
        grid=(1,),
        in_specs=last_in_specs(rows, groups, layer),
        out_specs=[whole_spec(a.shape) for a in out_shape],
        out_shape=out_shape,
        compiler_params=pltpu.CompilerParams(vmem_limit_bytes=VMEM_LIMIT),
        cost_estimate=pl.CostEstimate(
            flops=rows * 1_600_000, bytes_accessed=8_000_000, transcendentals=rows * 200
        ),
    )(x, weights, gains, seg_cls, seg_row, slot)


def last_bwd(crops, x, weights, layer, gains, seg_cls, seg_row, slot, saved, grad):
    rows, groups = x.shape[0], weights.shape[0]
    out_shape = [
        jax.ShapeDtypeStruct((groups, 1280, D), f32),
        jax.ShapeDtypeStruct((4, D), f32),
        jax.ShapeDtypeStruct((rows, D), f32),
    ]
    return pl.pallas_call(
        functools.partial(last_bwd_kernel, crops),
        grid=(1,),
        in_specs=last_in_specs(rows, groups, layer)
        + [whole_spec(a.shape) for a in last_saved(rows, groups)]
        + [whole_spec((CLS, D))],
        out_specs=[whole_spec(a.shape) for a in out_shape],
        out_shape=out_shape,
        compiler_params=pltpu.CompilerParams(vmem_limit_bytes=VMEM_LIMIT),
        cost_estimate=pl.CostEstimate(
            flops=rows * 4_000_000, bytes_accessed=16_000_000, transcendentals=rows * 400
        ),
    )(x, weights, gains, seg_cls, seg_row, slot, *saved, grad)


def basis_kernel(clip_ref, grads_ref, stats_ref, bases_ref, new_stats_ref, new_bases_ref, s_ref):
    layers, kinds = stats_ref.shape[0] // 4, 4
    mats = layers * kinds
    groups = grads_ref.shape[0]
    clip = clip_ref[0]
    bounds = (0, 384, 512, 896, 1280)
    for layer in range(layers):
        for kind in range(kinds):
            mat = layer * kinds + kind

            def outer(group, total, layer=layer, kind=kind):
                part = grads_ref[group, bounds[kind] : bounds[kind + 1], layer * D : layer * D + D]
                return total + mm(part, part, TN)

            stat = lax.fori_loop(0, groups, outer, jnp.zeros((D, D), f32))
            new_stats_ref[mat] = (
                SHAMPOO_BETA * stats_ref[mat] + (1 - SHAMPOO_BETA) * (clip * clip) * stat
            )

    def turn(mat, carry):
        new_bases_ref[mat] = mm(new_stats_ref[mat], bases_ref[mat], precision=precise)
        return carry

    lax.fori_loop(0, mats, turn, 0)
    lanes = lax.broadcasted_iota(jnp.int32, (mats, 128), 1)
    for block in range(D // 128):
        low, high = block * 128, block * 128 + 128
        for mat in range(mats):
            part = new_bases_ref[mat, :, low:high]
            s_ref[:, mat, :] = mm(part, part, TN, precise)
        pivots = jnp.zeros((mats, 128), f32)
        for first in range(0, 128, 32):

            def eliminate(step, pivots, first=first):
                row = s_ref[step]
                here = lanes == step
                pivot = jnp.sum(jnp.where(here, row, 0.0), axis=-1, keepdims=True)
                factors = jnp.where(lanes > step, row / pivot, 0.0)
                source = jnp.where(here, 1.0, row)
                for other in range(first, 128):
                    s_ref[other] = (
                        jnp.where(here, 0.0, s_ref[other]) - factors[:, other : other + 1] * source
                    )
                return jnp.where(here, pivot, pivots)

            pivots = lax.fori_loop(first, first + 32, eliminate, pivots)
        scale = lax.rsqrt(pivots)
        for other in range(128):
            row = jnp.where(lanes < other, s_ref[other], jnp.where(lanes == other, 1.0, 0.0))
            s_ref[other] = row * scale[:, other : other + 1]
        for mat in range(mats):
            part = mm(new_bases_ref[mat, :, low:high], s_ref[:, mat, :], NT, precise)
            new_bases_ref[mat, :, low:high] = part
            if high < D:
                rest = new_bases_ref[mat, :, high:]
                cross = mm(part, rest, TN, precise)
                new_bases_ref[mat, :, high:] = rest - mm(part, cross, NN, precise)


def renew_bases(clip_factor, grads, stats, bases):
    shape = stats.shape
    mats = shape[0] * shape[1]
    new_stats, new_bases = pl.pallas_call(
        basis_kernel,
        in_specs=[pl.BlockSpec(memory_space=pltpu.SMEM)]
        + [pl.BlockSpec(memory_space=pltpu.VMEM)] * 3,
        out_specs=[pl.BlockSpec(memory_space=pltpu.VMEM)] * 2,
        out_shape=[jax.ShapeDtypeStruct((mats, D, D), f32)] * 2,
        scratch_shapes=[pltpu.VMEM((128, mats, 128), f32)],
        compiler_params=pltpu.CompilerParams(vmem_limit_bytes=VMEM_LIMIT),
    )(clip_factor.reshape(1), grads, stats.reshape(mats, D, D), bases.reshape(mats, D, D))
    return new_stats.reshape(shape), new_bases.reshape(shape)


def flip_perm(count, bit):
    return [(i, i ^ bit) for i in range(count)]


def flips(axis):
    count = lax.axis_size(axis)
    bits, bit = [], 1
    while bit < count:
        bits.append(bit)
        bit *= 2
    return count, bits


def sum_over(array, axes):
    for axis in axes:
        count, bits = flips(axis)
        for bit in bits:
            array = array + lax.ppermute(array, axis, flip_perm(count, bit))
    return array


def shift_perm(count, step):
    return [(i, (i + step) % count) for i in range(count)]


def gather_over(array, axis):
    count = lax.axis_size(axis)
    if count > 8:
        return lax.all_gather(array, axis, axis=0)
    me = lax.axis_index(axis)
    out = jnp.zeros((count, *array.shape), array.dtype)
    out = lax.dynamic_update_index_in_dim(out, array, me, 0)
    for step in range(1, count):
        got = lax.ppermute(array, axis, shift_perm(count, step))
        out = lax.dynamic_update_index_in_dim(out, got, (me - step) % count, 0)
    return out


def swap_over(pick, axis):
    count = lax.axis_size(axis)
    me = lax.axis_index(axis)
    if count > 8:
        return lax.all_to_all(jnp.stack([pick(i) for i in range(count)]), axis, 0, 0)
    own = pick(me)
    out = jnp.zeros((count, *own.shape), own.dtype)
    out = lax.dynamic_update_index_in_dim(out, own, me, 0)
    for step in range(1, count):
        got = lax.ppermute(pick((me + step) % count), axis, shift_perm(count, step))
        out = lax.dynamic_update_index_in_dim(out, got, (me - step) % count, 0)
    return out


def adam_direction(first_mom, second_mom, beta_one, beta_two):
    return (
        first_mom / (1 - beta_one**STEP) / (jnp.sqrt(second_mom / (1 - beta_two**STEP)) + ADAM_EPS)
    )


def adamw(weight, grad_in, first_mom, second_mom, rate, decay):
    first_mom = BETA_ONE * first_mom + (1 - BETA_ONE) * grad_in
    second_mom = BETA_TWO * second_mom + (1 - BETA_TWO) * grad_in * grad_in
    weight = weight - rate * (
        adam_direction(first_mom, second_mom, BETA_ONE, BETA_TWO) + decay * weight
    )
    return (weight, first_mom, second_mom)


def row_layout(crop_count):
    rows = jnp.arange(2 * CHUNK)
    is_global = rows < 2 * GLOBAL_PAD
    local = rows - 2 * GLOBAL_PAD
    crop = jnp.where(is_global, rows // GLOBAL_PAD, 2 + local // LOCAL_PAD)
    offset = jnp.where(is_global, rows % GLOBAL_PAD, local % LOCAL_PAD)
    real = offset < jnp.where(is_global, GLOBAL_TOK, LOCAL_TOK)
    source = jnp.where(
        is_global, crop * GLOBAL_TOK + offset, 2 * GLOBAL_TOK + (crop - 2) * LOCAL_TOK + offset
    )
    source = jnp.where(real, source, -1)
    segment = jnp.where(real & (crop < 2 + crop_count), crop, 1000 + rows)
    return source, segment.astype(jnp.int32)


def shards(
    tokens, crop_counts, slot_live, block_w, block_m, block_v, rotation_bases, precond_stats,
    head_w, head_m, head_v, proto_w, proto_m, proto_v, norm_params, norm_m, norm_v,
    teacher_block, teacher_head, teacher_proto, teacher_norm, center,
):
    mp_index = lax.axis_index("mp")
    dp_index = lax.axis_index("dp")
    mp_count = lax.axis_size("mp")
    dp_count = lax.axis_size("dp")
    col_width = block_w.shape[3]
    micro, place = mp_index % MICRO, mp_index // MICRO
    crop_count = crop_counts[micro, place]
    own_t = jnp.concatenate(
        [
            part[layer, :, 0].astype(bf16).T
            for part in (teacher_block, block_w)
            for layer in range(LAYERS)
        ],
        axis=1,
    )
    weights = lax.all_gather(own_t, ("mp", "dp"), axis=0, tiled=True)
    weights = weights.reshape(mp_count, dp_count * col_width, 2 * LAYERS * D)
    head_cols = head_w.shape[1] // mp_count
    proto_cols = proto_w.shape[1] // dp_count

    def take_head(part):
        part = lax.dynamic_slice_in_dim(part, mp_index * head_cols, head_cols, 1).astype(bf16)
        return lax.all_gather(part, "dp", axis=0, tiled=True)

    def take_proto(part):
        def pick(i):
            return lax.dynamic_slice_in_dim(part, i * proto_cols, proto_cols, 1).astype(bf16)

        return swap_over(pick, "dp").reshape(-1, proto_cols)

    head_t, head_s = take_head(teacher_head), take_head(head_w)
    proto_t, proto_s = take_proto(teacher_proto), take_proto(proto_w)
    counts_own = jnp.stack([crop_counts[i % MICRO, i // MICRO] for i in range(mp_count)])
    counts = gather_over(counts_own[None], "dp").reshape(-1)
    other = lax.ppermute(
        lax.dynamic_index_in_dim(tokens, 1 - micro, 0, keepdims=False), "mp", flip_perm(mp_count, 1)
    )
    mine = lax.dynamic_index_in_dim(tokens, micro, 0, keepdims=False)
    first = micro == 0
    image = jnp.concatenate([jnp.where(first, mine, other), jnp.where(first, other, mine)], axis=0)
    source, segment = row_layout(crop_count)
    spread = (source[:, None] == jnp.arange(IMG_ROWS)[None, :]).astype(bf16)
    x0 = mm(spread, image)
    seg_col, seg_row = segment.reshape(2, CHUNK, 1), segment.reshape(2, 1, CHUNK)
    starts = crop_starts(CROPS)
    seg_cls = jnp.concatenate([segment[jnp.array(starts)], jnp.zeros((CLS - CROPS,), jnp.int32)])
    seg_cls = jnp.concatenate([seg_cls, seg_cls])[:, None]
    slot = jnp.repeat(slot_live.astype(f32).reshape(mp_count, SLOT_DEV), HD, axis=1)[:, None, :]
    x0_t = x0[:CHUNK]
    x1_t = block_fwd(x0_t, weights, 0, teacher_norm[0:4], seg_col, seg_row, slot)[0]
    y_t = last_fwd(
        2, x1_t, weights, 1, teacher_norm[4:8], seg_cls, segment[None, :CHUNK], slot
    )[0]
    x1, *saved0 = block_fwd(x0, weights, 2, norm_params[0:4], seg_col, seg_row, slot)
    y_s, *saved1 = last_fwd(
        CROPS, x1, weights, 3, norm_params[4:8], seg_cls, segment[None], slot
    )
    y_all = lax.all_gather(jnp.concatenate([y_s[:CROPS], y_t[:4]], axis=0), "mp", axis=0)
    cls_s = y_all[:, :CROPS].reshape(mp_count * CROPS, D)
    cls_t = y_all[:, CROPS : CROPS + 2].reshape(mp_count * 2, D)
    n_s, n_t = cls_s.shape[0], cls_t.shape[0]
    h1_s, h2_s, h3_s = head_s[:D], head_s[D : D + HID], head_s[D + HID :]
    h1_t, h2_t, h3_t = head_t[:D], head_t[D : D + HID], head_t[D + HID :]
    gain_s, bias_s = norm_params[8:9], norm_params[9:10]
    feats_s = norm_rows(cls_s, gain_s, bias_s).astype(bf16)
    feats_t = norm_rows(cls_t, teacher_norm[8:9], teacher_norm[9:10]).astype(bf16)
    a1_s, a1_t = mm(feats_s, h1_s), mm(feats_t, h1_t)
    b1_own = jnp.concatenate([gelu_exact(a1_s), gelu_exact(a1_t)], axis=0).astype(bf16)
    b1 = lax.all_gather(b1_own, "mp", axis=1, tiled=True)
    a2_s, a2_t = mm(b1[:n_s], h2_s), mm(b1[n_s:], h2_t)
    b2_s = gelu_exact(a2_s).astype(bf16)
    b2_t = gelu_exact(a2_t).astype(bf16)
    third = sum_over(jnp.concatenate([mm(b2_s, h3_s, NT), mm(b2_t, h3_t, NT)], axis=0), ("mp",))
    inv = lax.rsqrt(jnp.sum(third * third, axis=-1, keepdims=True) + 1e-06)
    unit = (third * inv).astype(bf16)
    unit_all = gather_over(unit, "dp")
    z_s = unit_all[:, :n_s].reshape(dp_count * n_s, -1)
    z_t = unit_all[:, n_s:].reshape(dp_count * n_t, -1)
    images = dp_count * mp_count
    scaled_s = mm(z_s, proto_s) / TAU_S
    glob = mm(z_t, proto_t)
    center_own = lax.dynamic_slice_in_dim(center, dp_index * proto_cols, proto_cols)
    scaled_t = (glob - center_own) / TAU_T
    center_part = jnp.sum(glob, axis=0)
    max_s = jnp.max(scaled_s, axis=-1, keepdims=True)
    max_t = jnp.max(scaled_t, axis=-1, keepdims=True)
    exp_s, exp_t = jnp.exp(scaled_s - max_s), jnp.exp(scaled_t - max_t)
    cross = mm(exp_t, scaled_s, NT, precise)
    same = jnp.arange(images * 2)[:, None] // 2 == jnp.arange(images * CROPS)[None, :] // CROPS
    cross = jnp.sum(
        jnp.where(same, cross, 0.0).reshape(images * 2, images, CROPS), axis=1
    )
    stats = jnp.concatenate(
        [
            max_s.reshape(-1),
            jnp.sum(exp_s, axis=-1),
            max_t.reshape(-1),
            jnp.sum(exp_t, axis=-1),
            cross.reshape(-1),
        ]
    )
    stats = gather_over(lax.all_gather(stats[None], "mp", axis=0, tiled=True), "dp")
    stats = stats.reshape(images, -1)
    r_s, r_t = images * CROPS, images * 2
    maxes_s, sums_s = stats[:, :r_s], stats[:, r_s : 2 * r_s]
    maxes_t, sums_t = stats[:, 2 * r_s : 2 * r_s + r_t], stats[:, 2 * r_s + r_t : 2 * (r_s + r_t)]
    crosses = stats[:, 2 * (r_s + r_t) :].reshape(images, r_t, CROPS)
    top_s, top_t = jnp.max(maxes_s, axis=0), jnp.max(maxes_t, axis=0)
    total_s = jnp.sum(sums_s * jnp.exp(maxes_s - top_s), axis=0)
    shrink_t = jnp.exp(maxes_t - top_t)
    total_t = jnp.sum(sums_t * shrink_t, axis=0)
    cross_total = jnp.sum(crosses * shrink_t[:, :, None], axis=0) / total_t[:, None]
    log_norm = (jnp.log(total_s) + top_s).reshape(images, 1, CROPS)
    crop_ids = jnp.arange(CROPS)
    pairs = (
        (crop_ids[None, None, :] != jnp.arange(2)[None, :, None])
        & (crop_ids[None, None, :] < 2 + counts[:, None, None])
    ).astype(f32)
    image_weight = 1.0 / (2.0 * counts.astype(f32) + 2.0)
    pair_weight = pairs * image_weight[:, None, None]
    entropy = log_norm - cross_total.reshape(images, 2, CROPS)
    loss_total = jnp.sum(entropy * pair_weight)
    coef_s = jnp.sum(pair_weight, axis=1).reshape(-1, 1) / total_s[:, None]
    coef_s = coef_s * jnp.exp(max_s - top_s[:, None])
    coef_t = jnp.exp(max_t[:, 0] - top_t) / total_t
    coef_t = pair_weight.reshape(r_t, CROPS) * coef_t[:, None]
    mix = jnp.where(same, jnp.tile(coef_t, (1, images)), 0.0)
    grad_scaled = (coef_s * exp_s - mm(mix, exp_t, TN, precise)) / TAU_S
    grad_logits = grad_scaled.astype(bf16)
    grad_unit_part = mm(grad_logits, proto_s, NT)
    grad_proto = mm(z_s, grad_logits, TN)

    def pick_unit(i):
        return lax.dynamic_slice_in_dim(grad_unit_part, i * n_s, n_s, 0)

    grad_unit = sum_over(jnp.sum(swap_over(pick_unit, "dp"), axis=0), ("mp",))
    third_s, inv_s = third[:n_s], inv[:n_s]
    along = jnp.sum(grad_unit * third_s, axis=-1, keepdims=True)
    grad_third = (inv_s * grad_unit - third_s * (inv_s * inv_s * inv_s * along)).astype(bf16)
    grad_a2 = (mm(grad_third, h3_s) * gelu_slope(a2_s)).astype(bf16)
    grad_b1 = lax.psum_scatter(mm(grad_a2, h2_s, NT), "mp", scatter_dimension=1, tiled=True)
    grad_a1 = (grad_b1 * gelu_slope(a1_s)).astype(bf16)
    grad_feats = sum_over(mm(grad_a1, h1_s, NT), ("mp",))
    grad_cls, head_gain, head_bias = norm_back(cls_s, gain_s, grad_feats)
    grad_y = lax.dynamic_slice_in_dim(grad_cls, mp_index * CROPS, CROPS, 0)
    grad_y = jnp.concatenate([grad_y, jnp.zeros((CLS - CROPS, D), f32)], axis=0)
    dwt1, dgains1, grad_x1 = last_bwd(
        CROPS, x1, weights, 3, norm_params[4:8], seg_cls, segment[None], slot, saved1, grad_y
    )
    dwt0, dgains0 = block_bwd(
        x0, weights, 2, norm_params[0:4], seg_col, seg_row, slot, saved0, grad_x1
    )
    block_g = jnp.concatenate(
        [
            lax.psum_scatter(
                dwt.reshape(-1, D), ("mp", "dp"), scatter_dimension=0, tiled=True
            )
            for dwt in (dwt0, dwt1)
        ],
        axis=1,
    )
    rows_left = jnp.concatenate([feats_s, b1[:n_s], grad_third], axis=1)
    head_rows = head_w.shape[0]

    def pick_left(i):
        return lax.dynamic_slice_in_dim(rows_left, i * head_rows, head_rows, 1)

    left = swap_over(pick_left, "dp").reshape(dp_count * n_s, head_rows)
    right = gather_over(jnp.concatenate([grad_a1, grad_a2, b2_s], axis=1), "dp")
    right = right.reshape(dp_count * n_s, 3 * head_cols)
    stack_ids = dp_index * head_rows + jnp.arange(head_rows)[None, :]
    edges = (0, D, D + HID, D + HID + third.shape[1])
    head_g = sum(
        mm(
            jnp.where((stack_ids >= edges[i]) & (stack_ids < edges[i + 1]), left, 0).astype(bf16),
            right[:, i * head_cols : (i + 1) * head_cols],
            TN,
        )
        for i in range(3)
    )
    head_square = jnp.sum(head_g * head_g)
    head_g = lax.all_gather(head_g, "mp", axis=1, tiled=True)
    proto_square = jnp.sum(grad_proto * grad_proto)
    proto_rows = proto_w.shape[0]

    def pick_proto(i):
        return lax.dynamic_slice_in_dim(grad_proto, i * proto_rows, proto_rows, 0)

    proto_g = swap_over(pick_proto, "dp")
    proto_g = proto_g.transpose(1, 0, 2).reshape(proto_rows, -1)
    center_total = gather_over(center_part, "dp").reshape(-1)
    head_first = (mp_index == 0).astype(f32)
    square = jnp.sum(block_g * block_g) + head_square + proto_square
    norm_part = jnp.concatenate(
        [
            dgains0,
            dgains1,
            head_first * head_gain,
            head_first * head_bias,
            jnp.full((1, D), square),
        ],
        axis=0,
    )
    norm_sum = sum_over(norm_part, ("mp", "dp"))
    norm_total = norm_sum[:10]
    grad_norm = jnp.sqrt(norm_sum[10, 0] + jnp.sum(norm_total * norm_total))
    clip_factor = jnp.minimum(1.0, CLIP_NORM / (grad_norm + 1e-06))
    grads_all = lax.all_gather(block_g.astype(bf16), ("mp", "dp"), axis=0, tiled=True)
    grads_all = grads_all.reshape(mp_count, dp_count * col_width, LAYERS * D)
    new_stats, new_bases = renew_bases(clip_factor, grads_all, precond_stats, rotation_bases)
    col_ids = dp_index * col_width + jnp.arange(col_width)
    bounds = (0, 384, 512, 896, 1280)
    col_masks = jnp.stack(
        [((col_ids >= bounds[k]) & (col_ids < bounds[k + 1])).astype(f32) for k in range(4)]
    )
    grad_cols = (clip_factor * block_g).reshape(col_width, LAYERS, D)
    rotated = jnp.einsum("lkde,cld,kc->lec", new_bases, grad_cols, col_masks, precision=precise)
    first_mom = ROT_ONE * block_m[:, :, 0] + (1 - ROT_ONE) * rotated
    second_mom = ROT_TWO * block_v[:, :, 0] + (1 - ROT_TWO) * rotated * rotated
    direction = adam_direction(first_mom, second_mom, ROT_ONE, ROT_TWO)
    turned_back = jnp.einsum("lkde,lec,kc->ldc", new_bases, direction, col_masks, precision=precise)
    master = block_w[:, :, 0]
    new_block_w = (master - LR_BLOCK * (turned_back + WEIGHT_DECAY * master))[:, :, None]
    new_head_w, new_head_m, new_head_v = adamw(
        head_w, clip_factor * head_g, head_m, head_v, LR_HEAD, WEIGHT_DECAY
    )
    new_proto_w, new_proto_m, new_proto_v = adamw(
        proto_w, clip_factor * proto_g, proto_m, proto_v, LR_PROTO, WEIGHT_DECAY
    )
    new_norm, new_norm_m, new_norm_v = adamw(
        norm_params, clip_factor * norm_total, norm_m, norm_v, LR_NORM, 0.0
    )
    new_teacher_block = TEACHER_MOM * teacher_block + (1 - TEACHER_MOM) * new_block_w
    new_teacher_head = TEACHER_MOM * teacher_head + (1 - TEACHER_MOM) * new_head_w
    new_teacher_proto = TEACHER_MOM * teacher_proto + (1 - TEACHER_MOM) * new_proto_w
    new_teacher_norm = TEACHER_MOM * teacher_norm + (1 - TEACHER_MOM) * new_norm
    new_center = CENTER_MOM * center + (1 - CENTER_MOM) * center_total / (2.0 * images)
    return (
        loss_total, grad_norm, new_block_w, first_mom[:, :, None], second_mom[:, :, None],
        new_bases, new_stats, new_head_w, new_head_m, new_head_v,
        new_proto_w, new_proto_m, new_proto_v, new_norm, new_norm_m, new_norm_v,
        new_teacher_block, new_teacher_head, new_teacher_proto, new_teacher_norm, new_center,
    )


def solution(mesh):
    block, head, proto, rep = P(None, None, "mp", "dp"), P("dp", None), P("dp", "mp"), P()
    in_specs = (
        P(None, ("dp", "mp"), None), P(None, "dp"), rep, block, block, block, rep, rep,
        head, head, head, proto, proto, proto, rep, rep, rep, block, head, proto, rep, P("mp"),
    )
    out_specs = (
        rep, rep, block, block, block, rep, rep, head, head, head, proto, proto, proto,
        rep, rep, rep, block, head, proto, rep, P("mp"),
    )
    return jax.shard_map(shards, mesh=mesh, in_specs=in_specs, out_specs=out_specs, check_vma=False)
```

```python
import functools

import jax
import jax.numpy as jnp
from jax import lax
from jax.experimental import pallas as pl
from jax.experimental.pallas import tpu as pltpu
from jax.sharding import PartitionSpec as P

D = 384
HD = 64
HID = 2048
LAYERS = 2
SLOT_DEV = 2
GLOBAL_TOK = 197
LOCAL_TOK = 37
MAX_LOCAL = 10
IMG_ROWS = 768
STEP = 10
MICRO = 2
CROPS = 12
GLOBAL_PAD = 200
LOCAL_PAD = 40
CHUNK = 400
CLS = 16

precise = lax.Precision.HIGHEST
TAU_S = 0.1
TAU_T = 0.07
CLIP_NORM = 0.005
BETA_ONE = 0.9
BETA_TWO = 0.999
ROT_ONE = 0.95
ROT_TWO = 0.95
SHAMPOO_BETA = 0.95
ADAM_EPS = 1e-08
WEIGHT_DECAY = 0.04
LR_BLOCK = 0.05
LR_HEAD = 0.03
LR_PROTO = 0.1
LR_NORM = 0.2
TEACHER_MOM = 0.7
CENTER_MOM = 0.9
NN = (((1,), (0,)), ((), ()))
NT = (((1,), (1,)), ((), ()))
TN = (((0,), (0,)), ((), ()))
bf16 = jnp.bfloat16
f32 = jnp.float32
VMEM_LIMIT = 58 * 1024 * 1024


def mm(lhs, rhs, dims=NN, precision=None):
    return lax.dot_general(lhs, rhs, dims, precision=precision, preferred_element_type=f32)


def normalize(inputs):
    centred = inputs - jnp.mean(inputs, axis=-1, keepdims=True)
    spread = jnp.mean(centred * centred, axis=-1, keepdims=True)
    inv = lax.rsqrt(spread + 1e-06)
    return centred * inv, inv


def norm_rows(inputs, gain, bias):
    return normalize(inputs)[0] * gain + bias


def norm_back(inputs, gain, grad_out):
    unit, inv = normalize(inputs)
    scaled = grad_out * gain
    grad = inv * (
        scaled
        - jnp.mean(scaled, axis=-1, keepdims=True)
        - unit * jnp.mean(scaled * unit, axis=-1, keepdims=True)
    )
    return (
        grad,
        jnp.sum(grad_out * unit, axis=0, keepdims=True),
        jnp.sum(grad_out, axis=0, keepdims=True),
    )


def gelu_cdf(inputs):
    return 0.5 + 0.5 * lax.erf(inputs * (0.5**0.5))


def gelu_exact(inputs):
    return inputs * gelu_cdf(inputs)


def gelu_slope(inputs):
    return gelu_cdf(inputs) + inputs * (jnp.exp(-0.5 * inputs * inputs) * 0.3989422804014327)


def low_half(shape):
    return lax.broadcasted_iota(jnp.int32, shape, 1) < HD


def halves(array):
    low = low_half(array.shape)
    zero = jnp.zeros_like(array)
    return jnp.where(low, array, zero), jnp.where(low, zero, array)


def block_fwd_kernel(
    x_ref, wt_ref, gains_ref, seg_col_ref, seg_row_ref, slot_ref,
    out_ref, h1_ref, qkv_ref, o_ref, x2_ref,
):
    x = x_ref[...]
    h1 = norm_rows(x, gains_ref[0:1], gains_ref[1:2]).astype(bf16)
    h1_ref[...] = h1
    allowed = seg_col_ref[0] == seg_row_ref[0]

    def heads(group, att):
        qkv = mm(h1, wt_ref[group, 0:384], NT).astype(bf16)
        qkv_ref[group] = qkv
        keys, values = qkv[:, 128:256], qkv[:, 256:384]
        mixes = []
        for query in halves(qkv[:, 0:128]):
            expd = jnp.where(allowed, jnp.exp(mm(query, keys, NT) * HD ** (-0.5)), 0.0)
            prob = expd / jnp.sum(expd, axis=-1, keepdims=True)
            mixes.append(mm(prob.astype(bf16), values))
        mix = jnp.where(low_half(mixes[0].shape), mixes[0], mixes[1])
        mix = (mix * slot_ref[group]).astype(bf16)
        o_ref[group] = mix
        return att + mm(mix, wt_ref[group, 384:512])

    att = lax.fori_loop(0, wt_ref.shape[0], heads, jnp.zeros(x.shape, f32))
    x2 = x + att
    x2_ref[...] = x2
    h2 = norm_rows(x2, gains_ref[2:3], gains_ref[3:4]).astype(bf16)

    def units(group, total):
        hidden = gelu_exact(mm(h2, wt_ref[group, 512:896], NT)).astype(bf16)
        return total + mm(hidden, wt_ref[group, 896:1280])

    out_ref[...] = x2 + lax.fori_loop(0, wt_ref.shape[0], units, jnp.zeros(x.shape, f32))


def mlp_bwd_kernel(wt_ref, gains_ref, x2_ref, grad_ref, dwt_ref, dgains_ref, dx2_ref):
    @pl.when(pl.program_id(0) == 0)
    def _():
        dwt_ref[...] = jnp.zeros_like(dwt_ref)
        dgains_ref[...] = jnp.zeros_like(dgains_ref)

    grad = grad_ref[...]
    grad_low = grad.astype(bf16)
    x2 = x2_ref[...]
    h2 = norm_rows(x2, gains_ref[2:3], gains_ref[3:4]).astype(bf16)

    def units(group, total):
        up = mm(h2, wt_ref[group, 512:896], NT)
        cdf = gelu_cdf(up)
        hidden = (up * cdf).astype(bf16)
        slope = cdf + up * (jnp.exp(-0.5 * up * up) * 0.3989422804014327)
        grad_up = (mm(grad_low, wt_ref[group, 896:1280], NT) * slope).astype(bf16)
        dwt_ref[group, 512:896] += mm(grad_up, h2, TN)
        dwt_ref[group, 896:1280] += mm(hidden, grad_low, TN)
        return total + mm(grad_up, wt_ref[group, 512:896])

    grad_h2 = lax.fori_loop(0, wt_ref.shape[0], units, jnp.zeros(grad.shape, f32))
    grad_x2, gain_two, bias_two = norm_back(x2, gains_ref[2:3], grad_h2)
    dx2_ref[...] = grad + grad_x2
    dgains_ref[...] += jnp.concatenate([gain_two, bias_two], axis=0)


def attention_bwd_kernel(
    last, wt_ref, gains_ref, seg_col_ref, seg_row_ref, slot_ref, h1_ref, qkv_ref, o_ref, dx2_ref,
    *refs,
):
    if last:
        x_ref, partial_ref, _, dwt_ref, dgains_ref = refs
    else:
        _, dwt_ref, dh1_ref = refs

    @pl.when(pl.program_id(0) == 0)
    def _():
        dwt_ref[...] = jnp.zeros_like(dwt_ref)
        if last:
            dgains_ref[...] = jnp.zeros_like(dgains_ref)

    grad_att = dx2_ref[...].astype(bf16)
    allowed = seg_col_ref[0] == seg_row_ref[0]
    h1 = h1_ref[...]

    def heads(group, total):
        grad_mix = mm(grad_att, wt_ref[group, 384:512], NT).astype(bf16)
        grad_mix = grad_mix * slot_ref[group].astype(bf16)
        dwt_ref[group, 384:512] += mm(o_ref[group], grad_att, TN)
        qkv = qkv_ref[group]
        keys, values = qkv[:, 128:256], qkv[:, 256:384]
        grad_values = jnp.zeros(values.shape, f32)
        grad_keys = jnp.zeros(values.shape, f32)
        grad_queries = []
        for query, gmix in zip(halves(qkv[:, 0:128]), halves(grad_mix)):
            expd = jnp.where(allowed, jnp.exp(mm(query, keys, NT) * HD ** (-0.5)), 0.0)
            prob = expd * (1.0 / jnp.sum(expd, axis=-1, keepdims=True))
            grad_values = grad_values + mm(prob.astype(bf16), gmix, TN)
            grad_prob = mm(gmix, values, NT)
            scored = prob * (grad_prob - jnp.sum(prob * grad_prob, axis=-1, keepdims=True))
            scored = scored.astype(bf16)
            grad_queries.append(mm(scored, keys))
            grad_keys = grad_keys + mm(scored, query, TN)
        low = low_half(grad_queries[0].shape)
        grad_query = jnp.where(low, grad_queries[0], grad_queries[1]) * HD ** (-0.5)
        grad_qkv = jnp.concatenate(
            [grad_query.astype(bf16), (grad_keys * HD ** (-0.5)).astype(bf16), grad_values.astype(bf16)],
            axis=1,
        )
        dwt_ref[group, 0:384] += mm(grad_qkv, h1, TN)
        return total + mm(grad_qkv, wt_ref[group, 0:384])

    start = partial_ref[...] if last else jnp.zeros(h1.shape, f32)
    grad_h1 = lax.fori_loop(0, wt_ref.shape[0], heads, start)
    if last:
        _, gain_one, bias_one = norm_back(x_ref[...], gains_ref[0:1], grad_h1)
        dgains_ref[...] += jnp.concatenate([gain_one, bias_one], axis=0)
    else:
        dh1_ref[...] = grad_h1


def whole_spec(shape):
    return pl.BlockSpec(shape, lambda *_: (0,) * len(shape))


def block_specs(groups, layer):
    row = pl.BlockSpec((CHUNK, D), lambda c: (c, 0))
    return dict(
        row=row,
        wt=pl.BlockSpec((groups, 1280, D), lambda c: (0, 0, layer)),
        gains=whole_spec((4, D)),
        seg_col=pl.BlockSpec((1, CHUNK, 1), lambda c: (c, 0, 0)),
        seg_row=pl.BlockSpec((1, 1, CHUNK), lambda c: (c, 0, 0)),
        slot=whole_spec((groups, 1, 128)),
        qkv=pl.BlockSpec((groups, CHUNK, 384), lambda c: (0, c, 0)),
        mix=pl.BlockSpec((groups, CHUNK, 128), lambda c: (0, c, 0)),
    )


def block_fwd(x, weights, layer, gains, seg_col, seg_row, slot):
    rows, groups = x.shape[0], weights.shape[0]
    s = block_specs(groups, layer)
    return pl.pallas_call(
        block_fwd_kernel,
        grid=(rows // CHUNK,),
        in_specs=[s["row"], s["wt"], s["gains"], s["seg_col"], s["seg_row"], s["slot"]],
        out_specs=[s["row"], s["row"], s["qkv"], s["mix"], s["row"]],
        out_shape=[
            jax.ShapeDtypeStruct((rows, D), f32),
            jax.ShapeDtypeStruct((rows, D), bf16),
            jax.ShapeDtypeStruct((groups, rows, 384), bf16),
            jax.ShapeDtypeStruct((groups, rows, 128), bf16),
            jax.ShapeDtypeStruct((rows, D), f32),
        ],
        compiler_params=pltpu.CompilerParams(vmem_limit_bytes=VMEM_LIMIT),
        cost_estimate=pl.CostEstimate(
            flops=rows * 30_000_000, bytes_accessed=8_000_000, transcendentals=rows * 4000
        ),
    )(x, weights, gains, seg_col, seg_row, slot)


def mlp_bwd(weights, layer, gains, x2, grad):
    rows, groups = x2.shape[0], weights.shape[0]
    s = block_specs(groups, layer)
    return pl.pallas_call(
        mlp_bwd_kernel,
        grid=(rows // CHUNK,),
        in_specs=[s["wt"], s["gains"], s["row"], s["row"]],
        out_specs=[whole_spec((groups, 1280, D)), whole_spec((2, D)), s["row"]],
        out_shape=[
            jax.ShapeDtypeStruct((groups, 1280, D), f32),
            jax.ShapeDtypeStruct((2, D), f32),
            jax.ShapeDtypeStruct((rows, D), f32),
        ],
        compiler_params=pltpu.CompilerParams(vmem_limit_bytes=VMEM_LIMIT),
        cost_estimate=pl.CostEstimate(
            flops=rows * 24_000_000, bytes_accessed=16_000_000, transcendentals=rows * 6000
        ),
    )(weights, gains, x2, grad)


def attention_bwd(part, weights, layer, gains, seg_col, seg_row, slot, saved, grad_x2, dwt, last=()):
    h1, qkv, mix, _ = saved
    rows, groups = h1.shape[0], weights.shape[0] // 2
    s = block_specs(groups, layer)
    heads = pl.BlockSpec((groups, 512, D), lambda c: (part, 0, 0))
    in_specs = [
        pl.BlockSpec((groups, 512, D), lambda c: (part, 0, layer)),
        s["gains"], s["seg_col"], s["seg_row"],
        pl.BlockSpec((groups, 1, 128), lambda c: (part, 0, 0)),
        s["row"],
        pl.BlockSpec((groups, CHUNK, 384), lambda c: (part, c, 0)),
        pl.BlockSpec((groups, CHUNK, 128), lambda c: (part, c, 0)),
        s["row"],
    ] + [s["row"]] * len(last)
    args = (weights, gains, seg_col, seg_row, slot, h1, qkv, mix, grad_x2, *last, dwt)
    return pl.pallas_call(
        functools.partial(attention_bwd_kernel, bool(last)),
        grid=(rows // CHUNK,),
        in_specs=in_specs + [pl.BlockSpec(memory_space=pl.ANY)],
        out_specs=[heads, whole_spec((2, D)) if last else s["row"]],
        out_shape=[
            jax.ShapeDtypeStruct(dwt.shape, f32),
            jax.ShapeDtypeStruct((2, D) if last else (rows, D), f32),
        ],
        input_output_aliases={len(args) - 1: 0},
        compiler_params=pltpu.CompilerParams(vmem_limit_bytes=VMEM_LIMIT),
        cost_estimate=pl.CostEstimate(
            flops=rows * 19_000_000, bytes_accessed=8_000_000, transcendentals=rows * 3000
        ),
    )(*args)


def crop_starts(crops):
    return [
        crop * GLOBAL_PAD if crop < 2 else 2 * GLOBAL_PAD + (crop - 2) * LOCAL_PAD
        for crop in range(crops)
    ]


def take_cls(ref, crops):
    rows = [ref[start : start + 1, :] for start in crop_starts(crops)]
    return jnp.concatenate(rows + [jnp.zeros((CLS - crops, ref.shape[1]), f32)], axis=0)


def last_fwd_kernel(
    crops, x_ref, wt_ref, gains_ref, seg_cls_ref, seg_row_ref, slot_ref,
    out_ref, h1_ref, kv_ref, q_ref, o_ref, x2_ref,
):
    gain, bias = gains_ref[0:1], gains_ref[1:2]
    h1 = norm_rows(x_ref[...], gain, bias).astype(bf16)
    h1_ref[...] = h1
    x_cls = take_cls(x_ref, crops)
    h1_cls = norm_rows(x_cls, gain, bias).astype(bf16)
    allowed = seg_cls_ref[...] == seg_row_ref[...]

    def heads(group, att):
        kv = mm(h1, wt_ref[group, 128:384], NT).astype(bf16)
        kv_ref[group] = kv
        query = mm(h1_cls, wt_ref[group, 0:128], NT).astype(bf16)
        q_ref[group] = query
        both = jnp.concatenate(halves(query), axis=0)
        scores = mm(both, kv[:, 0:128], NT) * HD ** (-0.5)
        expd = jnp.where(allowed, jnp.exp(scores), 0.0)
        prob = expd / jnp.sum(expd, axis=-1, keepdims=True)
        mix = mm(prob.astype(bf16), kv[:, 128:256])
        mix = jnp.where(low_half((CLS, 128)), mix[0:CLS], mix[CLS:])
        mix = (mix * slot_ref[group]).astype(bf16)
        o_ref[group] = mix
        return att + mm(mix, wt_ref[group, 384:512])

    att = lax.fori_loop(0, wt_ref.shape[0], heads, jnp.zeros((CLS, D), f32))
    x2 = x_cls + att
    x2_ref[...] = x2
    h2 = norm_rows(x2, gains_ref[2:3], gains_ref[3:4]).astype(bf16)

    def units(group, total):
        hidden = gelu_exact(mm(h2, wt_ref[group, 512:896], NT)).astype(bf16)
        return total + mm(hidden, wt_ref[group, 896:1280])

    out_ref[...] = x2 + lax.fori_loop(0, wt_ref.shape[0], units, jnp.zeros((CLS, D), f32))


def last_bwd_kernel(
    crops, x_ref, wt_ref, gains_ref, seg_cls_ref, seg_row_ref, slot_ref,
    h1_ref, kv_ref, q_ref, o_ref, x2_ref, grad_ref,
    dwt_ref, dgains_ref, dx_ref,
):
    grad = grad_ref[...]
    grad_low = grad.astype(bf16)
    x2 = x2_ref[...]
    h2 = norm_rows(x2, gains_ref[2:3], gains_ref[3:4]).astype(bf16)
    groups = wt_ref.shape[0]

    def units(group, total):
        up = mm(h2, wt_ref[group, 512:896], NT)
        hidden = gelu_exact(up).astype(bf16)
        grad_up = (mm(grad_low, wt_ref[group, 896:1280], NT) * gelu_slope(up)).astype(bf16)
        dwt_ref[group, 512:896] = mm(grad_up, h2, TN)
        dwt_ref[group, 896:1280] = mm(hidden, grad_low, TN)
        return total + mm(grad_up, wt_ref[group, 512:896])

    grad_h2 = lax.fori_loop(0, groups, units, jnp.zeros((CLS, D), f32))
    grad_x2, gain_two, bias_two = norm_back(x2, gains_ref[2:3], grad_h2)
    grad_x2 = grad + grad_x2
    grad_att = grad_x2.astype(bf16)
    allowed = seg_cls_ref[...] == seg_row_ref[...]
    h1 = h1_ref[...]
    h1_cls = norm_rows(take_cls(x_ref, crops), gains_ref[0:1], gains_ref[1:2]).astype(bf16)

    def heads(group, carry):
        total, total_cls = carry
        grad_mix = mm(grad_att, wt_ref[group, 384:512], NT).astype(bf16)
        grad_mix = grad_mix * slot_ref[group].astype(bf16)
        dwt_ref[group, 384:512] = mm(o_ref[group], grad_att, TN)
        kv = kv_ref[group]
        keys, values = kv[:, 0:128], kv[:, 128:256]
        both = jnp.concatenate(halves(q_ref[group]), axis=0)
        gboth = jnp.concatenate(halves(grad_mix), axis=0)
        expd = jnp.where(allowed, jnp.exp(mm(both, keys, NT) * HD ** (-0.5)), 0.0)
        prob = expd / jnp.sum(expd, axis=-1, keepdims=True)
        grad_prob = mm(gboth, values, NT)
        scored = prob * (grad_prob - jnp.sum(prob * grad_prob, axis=-1, keepdims=True))
        scored = scored.astype(bf16)
        grad_values = mm(prob.astype(bf16), gboth, TN)
        grad_keys = mm(scored, both, TN) * HD ** (-0.5)
        grad_query = mm(scored, keys)
        low = low_half((CLS, 128))
        grad_query = jnp.where(low, grad_query[0:CLS], grad_query[CLS:]) * HD ** (-0.5)
        grad_query = grad_query.astype(bf16)
        grad_kv = jnp.concatenate([grad_keys.astype(bf16), grad_values.astype(bf16)], axis=1)
        dwt_ref[group, 0:128] = mm(grad_query, h1_cls, TN)
        dwt_ref[group, 128:384] = mm(grad_kv, h1, TN)
        return (
            total + mm(grad_kv, wt_ref[group, 128:384]),
            total_cls + mm(grad_query, wt_ref[group, 0:128]),
        )

    grad_h1, grad_cls = lax.fori_loop(
        0, groups, heads, (jnp.zeros(h1.shape, f32), jnp.zeros((CLS, D), f32))
    )
    dx_ref[...] = grad_h1
    starts = crop_starts(crops)
    for crop, start in enumerate(starts):
        dx_ref[start : start + 1, :] += grad_cls[crop : crop + 1, :]
    grad_x, gain_one, bias_one = norm_back(x_ref[...], gains_ref[0:1], dx_ref[...])
    dx_ref[...] = grad_x
    for crop, start in enumerate(starts):
        dx_ref[start : start + 1, :] += grad_x2[crop : crop + 1, :]
    dgains_ref[...] = jnp.concatenate([gain_one, bias_one, gain_two, bias_two], axis=0)


def last_in_specs(rows, groups, layer):
    return [
        whole_spec((rows, D)),
        pl.BlockSpec((groups, 1280, D), lambda i: (0, 0, layer)),
        whole_spec((4, D)),
        whole_spec((2 * CLS, 1)),
        whole_spec((1, rows)),
        whole_spec((groups, 1, 128)),
    ]


def last_saved(rows, groups):
    return [
        jax.ShapeDtypeStruct((rows, D), bf16),
        jax.ShapeDtypeStruct((groups, rows, 256), bf16),
        jax.ShapeDtypeStruct((groups, CLS, 128), bf16),
        jax.ShapeDtypeStruct((groups, CLS, 128), bf16),
        jax.ShapeDtypeStruct((CLS, D), f32),
    ]


def last_fwd(crops, x, weights, layer, gains, seg_cls, seg_row, slot):
    rows, groups = x.shape[0], weights.shape[0]
    out_shape = [jax.ShapeDtypeStruct((CLS, D), f32)] + last_saved(rows, groups)
    return pl.pallas_call(
        functools.partial(last_fwd_kernel, crops),
        grid=(1,),
        in_specs=last_in_specs(rows, groups, layer),
        out_specs=[whole_spec(a.shape) for a in out_shape],
        out_shape=out_shape,
        compiler_params=pltpu.CompilerParams(vmem_limit_bytes=VMEM_LIMIT),
        cost_estimate=pl.CostEstimate(
            flops=rows * 15_000_000, bytes_accessed=8_000_000, transcendentals=rows * 200
        ),
    )(x, weights, gains, seg_cls, seg_row, slot)


def last_bwd(crops, x, weights, layer, gains, seg_cls, seg_row, slot, saved, grad):
    rows, groups = x.shape[0], weights.shape[0]
    out_shape = [
        jax.ShapeDtypeStruct((groups, 1280, D), f32),
        jax.ShapeDtypeStruct((4, D), f32),
        jax.ShapeDtypeStruct((rows, D), f32),
    ]
    return pl.pallas_call(
        functools.partial(last_bwd_kernel, crops),
        grid=(1,),
        in_specs=last_in_specs(rows, groups, layer)
        + [whole_spec(a.shape) for a in last_saved(rows, groups)]
        + [whole_spec((CLS, D))],
        out_specs=[whole_spec(a.shape) for a in out_shape],
        out_shape=out_shape,
        compiler_params=pltpu.CompilerParams(vmem_limit_bytes=VMEM_LIMIT),
        cost_estimate=pl.CostEstimate(
            flops=rows * 20_000_000, bytes_accessed=16_000_000, transcendentals=rows * 400
        ),
    )(x, weights, gains, seg_cls, seg_row, slot, *saved, grad)


PANEL = 32


def panel_steps(panels):
    lanes = lax.broadcasted_iota(jnp.int32, (PANEL, 128), 1)
    ids = lax.broadcasted_iota(jnp.int32, (PANEL, 1), 0)
    panels = list(panels)
    pivots = [jnp.zeros((PANEL, 1), f32) for _ in panels]
    for step in range(PANEL):
        here = lanes == step
        for i, panel in enumerate(panels):
            row = panel[step : step + 1]
            pivot = row[:, step : step + 1]
            column = jnp.where(ids > step, panel[:, step : step + 1], 0.0)
            source = jnp.where(here[0:1], 1.0, row) * (1.0 / pivot)
            cleared = jnp.where(here & (ids > step), 0.0, panel)
            panels[i] = cleared - column * source
            pivots[i] = jnp.where(ids == step, pivot, pivots[i])
    return panels, pivots


def basis_kernel(stats_ref, bases_ref, out_ref, gram_ref, inverse_ref):
    mats = stats_ref.shape[0]
    lanes = lax.broadcasted_iota(jnp.int32, (128, 128), 1)
    rows = lax.broadcasted_iota(jnp.int32, (128, 128), 0)
    near_lanes, near_rows = lanes[:PANEL], rows[:PANEL]
    for mat in range(mats):
        out_ref[mat] = mm(stats_ref[mat], bases_ref[mat], precision=precise)
    for block in range(D // 128):
        low, high = block * 128, block * 128 + 128
        for mat in range(mats):
            part = out_ref[mat, :, low:high]
            gram_ref[mat] = mm(part, part, TN, precise)

        def panels(index, carry):
            first = pl.multiple_of(index * PANEL, PANEL)
            last = first + PANEL
            started = [
                pltpu.roll(gram_ref[mat, pl.ds(first, PANEL), :], 128 - first, 1)
                for mat in range(mats)
            ]
            for mat, (panel, pivots) in enumerate(zip(*panel_steps(started))):
                panel = pltpu.roll(panel, first, 1)
                own = near_lanes - first
                unit = jnp.where(own < near_rows, panel, jnp.where(own == near_rows, 1.0, 0.0))
                inverse_ref[mat, pl.ds(first, PANEL), :] = unit * lax.rsqrt(pivots)
                source = jnp.where(near_lanes < last, unit, panel)
                factors = jnp.where(near_lanes < last, 0.0, panel / pivots)
                gram = gram_ref[mat]
                gram = jnp.where((lanes >= first) & (lanes < last) & (rows >= last), 0.0, gram)
                gram_ref[mat] = gram - mm(factors, source, TN, precise)
            return carry

        lax.fori_loop(0, 128 // PANEL, panels, 0)
        for mat in range(mats):
            part = mm(out_ref[mat, :, low:high], inverse_ref[mat], NT, precise)
            out_ref[mat, :, low:high] = part
            if high < D:
                rest = out_ref[mat, :, high:]
                cross = mm(part, rest, TN, precise)
                out_ref[mat, :, high:] = rest - mm(part, cross, NN, precise)


def renew_bases(new_stats, bases):
    mats = new_stats.shape[0]
    return pl.pallas_call(
        basis_kernel,
        in_specs=[pl.BlockSpec(memory_space=pltpu.VMEM)] * 2,
        out_specs=pl.BlockSpec(memory_space=pltpu.VMEM),
        out_shape=jax.ShapeDtypeStruct((mats, D, D), f32),
        scratch_shapes=[pltpu.VMEM((mats, 128, 128), f32), pltpu.VMEM((mats, 128, 128), f32)],
        compiler_params=pltpu.CompilerParams(vmem_limit_bytes=VMEM_LIMIT),
        cost_estimate=pl.CostEstimate(
            flops=60_000_000_000, bytes_accessed=6_000_000, transcendentals=1000
        ),
    )(new_stats, bases)


def flip_perm(count, bit):
    return [(i, i ^ bit) for i in range(count)]


def flips(axis):
    count = lax.axis_size(axis)
    bits, bit = [], 1
    while bit < count:
        bits.append(bit)
        bit *= 2
    return count, bits


def thirds(array):
    high = lax.optimization_barrier(array.astype(bf16))
    rest = array - high.astype(f32)
    middle = lax.optimization_barrier(rest.astype(bf16))
    return jnp.stack([high, middle, (rest - middle.astype(f32)).astype(bf16)])


def whole_of(parts):
    layers, count = parts.shape[:2]
    parts = parts.transpose(1, 0, 2, 3).reshape(count, 3, -1, parts.shape[-1]).astype(f32)
    return jnp.sum(parts[:, 0] + (parts[:, 1] + parts[:, 2]), axis=0)


def sum_over(array, axes):
    for axis in axes:
        count, bits = flips(axis)
        for bit in bits:
            array = array + lax.ppermute(array, axis, flip_perm(count, bit))
    return array


def shift_perm(count, step):
    return [(i, (i + step) % count) for i in range(count)]


def gather_over(array, axis):
    count = lax.axis_size(axis)
    if lax.axis_size("dp") > 8:
        return lax.all_gather(array, axis, axis=0)
    return lax.all_to_all(jnp.broadcast_to(array[None], (count, *array.shape)), axis, 0, 0)


def swap_over(pick, axis, after=None):
    count = lax.axis_size(axis)
    me = lax.axis_index(axis)
    if count > 8:
        return lax.all_to_all(jnp.stack([pick(i) for i in range(count)]), axis, 0, 0)
    own = pick(me)
    picks = [pick(lax.rem(me + step, count)) for step in range(1, count)]
    if after is not None:
        picks, _ = lax.optimization_barrier((picks, after))
    out = jnp.zeros((count, *own.shape), own.dtype)
    out = put(out, own, me)
    for step in range(1, count):
        got = lax.ppermute(picks[step - 1], axis, shift_perm(count, step))
        out = put(out, got, lax.rem(me + (count - step), count))
    return out


RING = (0, 2, 4, 6, 7, 5, 3, 1)


def unsigned(index):
    return lax.convert_element_type(index, jnp.uint32)


def put(out, piece, index):
    return lax.dynamic_update_index_in_dim(out, piece, unsigned(index), 0)


def ring_at(offset):
    count = len(RING)
    table = [RING[(RING.index(i) + offset) % count] for i in range(count)]
    return lax.dynamic_slice(
        jnp.array(table, jnp.uint32), (lax.axis_index("dp").astype(jnp.uint32),), (1,)
    )[0]


def ring_perm(step):
    count = len(RING)
    return [(RING[i], RING[(i + step) % count]) for i in range(count)]


def ring_gather(piece):
    count = lax.axis_size("dp")
    if count != len(RING):
        return lax.all_gather(piece, "dp", axis=0)
    out = put(jnp.zeros((count, *piece.shape), piece.dtype), piece, lax.axis_index("dp"))
    right = left = piece
    for step in range(1, count // 2):
        right = lax.ppermute(right, "dp", ring_perm(1))
        left = lax.ppermute(left, "dp", ring_perm(-1))
        out = put(out, right, ring_at(-step))
        out = put(out, left, ring_at(step))
    half = piece.shape[-2] // 2
    right = lax.ppermute(right[..., :half, :], "dp", ring_perm(1))
    left = lax.ppermute(left[..., half:, :], "dp", ring_perm(-1))
    return put(out, jnp.concatenate([right, left], axis=-2), ring_at(count // 2))


class RingScatter:
    steps = len(RING) // 2

    def __init__(self, parts):
        self.parts = parts
        self.ringed = lax.axis_size("dp") == len(RING)
        self.right = self.left = None
        if self.ringed:
            far = self.own(self.steps)
            self.send_right, self.send_left = far[0:1], far[1:2]

    def own(self, offset):
        return lax.dynamic_index_in_dim(self.parts, ring_at(offset), 1, keepdims=False)

    def step(self, index):
        if not self.ringed:
            return
        if index > 0:
            right, left = self.own(self.steps - index), self.own(index - self.steps)
            if index == 1:
                right = jnp.concatenate([right[0:1] + self.right, right[1:2]])
                left = jnp.concatenate([left[0:1], left[1:2] + self.left])
            else:
                right, left = right + self.right, left + self.left
            self.send_right, self.send_left = right, left
        self.right = lax.ppermute(self.send_right, "dp", ring_perm(1))
        self.left = lax.ppermute(self.send_left, "dp", ring_perm(-1))

    def tie(self, other):
        if self.ringed:
            other, self.right, self.left = lax.optimization_barrier((other, self.right, self.left))
        return other

    def total(self):
        if not self.ringed:
            return lax.psum_scatter(self.parts, "dp", scatter_dimension=1, tiled=True)[:, 0]
        return self.own(0) + self.right + self.left


def core_halves(grad, dp_count, core):
    parts = grad.reshape(2, 2, dp_count, -1, D)
    send = lax.dynamic_index_in_dim(parts, unsigned(1 - core), 1, keepdims=False)
    return send, lax.dynamic_index_in_dim(parts, unsigned(core), 1, keepdims=False)


def across_sum(parts, across):
    send = lax.dynamic_index_in_dim(parts, unsigned(1 - across), 0, keepdims=False)
    own = lax.dynamic_index_in_dim(parts, unsigned(across), 0, keepdims=False)
    return own + lax.ppermute(send, "mp", flip_perm(4, 2))


def gather_mats(own, far, across, core):
    pair = put(jnp.stack([own, own]), far, 1 - across)
    other = lax.ppermute(pair, "mp", flip_perm(4, 1))
    whole = jnp.zeros((2, 2, *own.shape), own.dtype)
    whole = lax.dynamic_update_index_in_dim(whole, pair, unsigned(core), 1)
    whole = lax.dynamic_update_index_in_dim(whole, other, unsigned(1 - core), 1)
    return whole.reshape(4, *own.shape)


def adam_direction(first_mom, second_mom, beta_one, beta_two):
    return (
        first_mom / (1 - beta_one**STEP) / (jnp.sqrt(second_mom / (1 - beta_two**STEP)) + ADAM_EPS)
    )


def adamw(weight, grad_in, first_mom, second_mom, rate, decay):
    first_mom = BETA_ONE * first_mom + (1 - BETA_ONE) * grad_in
    second_mom = BETA_TWO * second_mom + (1 - BETA_TWO) * grad_in * grad_in
    weight = weight - rate * (
        adam_direction(first_mom, second_mom, BETA_ONE, BETA_TWO) + decay * weight
    )
    return (weight, first_mom, second_mom)


def row_layout(crop_count):
    rows = jnp.arange(2 * CHUNK)
    is_global = rows < 2 * GLOBAL_PAD
    local = rows - 2 * GLOBAL_PAD
    crop = jnp.where(is_global, rows // GLOBAL_PAD, 2 + local // LOCAL_PAD)
    offset = jnp.where(is_global, rows % GLOBAL_PAD, local % LOCAL_PAD)
    real = offset < jnp.where(is_global, GLOBAL_TOK, LOCAL_TOK)
    source = jnp.where(
        is_global, crop * GLOBAL_TOK + offset, 2 * GLOBAL_TOK + (crop - 2) * LOCAL_TOK + offset
    )
    source = jnp.where(real, source, -1)
    segment = jnp.where(real & (crop < 2 + crop_count), crop, 1000 + rows)
    return source, segment.astype(jnp.int32)


def shards(
    tokens, crop_counts, slot_live, block_w, block_m, block_v, rotation_bases, precond_stats,
    head_w, head_m, head_v, proto_w, proto_m, proto_v, norm_params, norm_m, norm_v,
    teacher_block, teacher_head, teacher_proto, teacher_norm, center,
):
    mp_index = lax.axis_index("mp")
    dp_index = lax.axis_index("dp")
    mp_count = lax.axis_size("mp")
    dp_count = lax.axis_size("dp")
    col_width = block_w.shape[3]
    micro, place = mp_index % MICRO, mp_index // MICRO
    crop_count = crop_counts[micro, place]
    across, core = mp_index // 2, mp_index % 2
    own_t = [teacher_block[layer, :, 0].astype(bf16).T for layer in range(LAYERS)]
    own_s = [block_w[layer, :, 0].astype(bf16).T for layer in range(LAYERS)]
    weights = lax.all_gather(
        jnp.concatenate([*own_t, *own_s], axis=1), ("mp", "dp"), axis=0, tiled=True
    ).reshape(mp_count, -1, 2 * LAYERS * D)
    head_cols = head_w.shape[1] // mp_count
    proto_cols = proto_w.shape[1] // dp_count
    heads = jnp.concatenate(
        [
            lax.dynamic_slice_in_dim(part, unsigned(mp_index * head_cols), head_cols, 1)
            for part in (teacher_head, head_w)
        ],
        axis=1,
    ).astype(bf16)

    def pick_cols(i):
        return jnp.stack(
            [
                lax.dynamic_slice_in_dim(part, unsigned(i * proto_cols), proto_cols, 1).astype(bf16)
                for part in (teacher_proto, proto_w)
            ]
        )

    counts_own = jnp.stack([crop_counts[i % MICRO, i // MICRO] for i in range(mp_count)])
    counts = gather_over(counts_own[None], "dp").reshape(-1)
    other = lax.ppermute(
        lax.dynamic_index_in_dim(tokens, 1 - micro, 0, keepdims=False), "mp", flip_perm(mp_count, 1)
    )
    mine = lax.dynamic_index_in_dim(tokens, micro, 0, keepdims=False)
    first = micro == 0
    image = jnp.concatenate([jnp.where(first, mine, other), jnp.where(first, other, mine)], axis=0)
    source, segment = row_layout(crop_count)
    spread = (source[:, None] == jnp.arange(IMG_ROWS)[None, :]).astype(bf16)
    x0 = mm(spread, image)
    seg_col, seg_row = segment.reshape(2, CHUNK, 1), segment.reshape(2, 1, CHUNK)
    starts = crop_starts(CROPS)
    seg_cls = jnp.concatenate([segment[jnp.array(starts)], jnp.zeros((CLS - CROPS,), jnp.int32)])
    seg_cls = jnp.concatenate([seg_cls, seg_cls])[:, None]
    slot = jnp.repeat(slot_live.astype(f32).reshape(mp_count, SLOT_DEV), HD, axis=1)[:, None, :]
    protos = swap_over(pick_cols, "dp")
    x0, weights, heads, protos, counts, seg_col, seg_row, seg_cls, slot = lax.optimization_barrier(
        (x0, weights, heads, protos, counts, seg_col, seg_row, seg_cls, slot)
    )
    heads = lax.all_gather(heads, "dp", axis=0, tiled=True)
    head_t, head_s = heads[:, :head_cols], heads[:, head_cols:]
    protos = protos.transpose(1, 0, 2, 3).reshape(2, -1, proto_cols)
    proto_t, proto_s = protos[0], protos[1]
    x0_t = x0[:CHUNK]
    x1_t = block_fwd(x0_t, weights, 0, teacher_norm[0:4], seg_col, seg_row, slot)[0]
    x1, *saved0 = block_fwd(x0, weights, 2, norm_params[0:4], seg_col, seg_row, slot)
    y_t = last_fwd(
        2, x1_t, weights, 1, teacher_norm[4:8], seg_cls, segment[None, :CHUNK], slot
    )[0]
    y_s, *saved1 = last_fwd(
        CROPS, x1, weights, 3, norm_params[4:8], seg_cls, segment[None], slot
    )
    y_all = lax.all_gather(jnp.concatenate([y_s[:CROPS], y_t[:4]], axis=0), "mp", axis=0)
    cls_s = y_all[:, :CROPS].reshape(mp_count * CROPS, D)
    cls_t = y_all[:, CROPS : CROPS + 2].reshape(mp_count * 2, D)
    n_s, n_t = cls_s.shape[0], cls_t.shape[0]
    h1_s, h2_s, h3_s = head_s[:D], head_s[D : D + HID], head_s[D + HID :]
    h1_t, h2_t, h3_t = head_t[:D], head_t[D : D + HID], head_t[D + HID :]
    gain_s, bias_s = norm_params[8:9], norm_params[9:10]
    feats_s = norm_rows(cls_s, gain_s, bias_s).astype(bf16)
    feats_t = norm_rows(cls_t, teacher_norm[8:9], teacher_norm[9:10]).astype(bf16)
    a1_s, a1_t = mm(feats_s, h1_s), mm(feats_t, h1_t)
    b1_own = jnp.concatenate([gelu_exact(a1_s), gelu_exact(a1_t)], axis=0).astype(bf16)
    b1 = lax.all_gather(b1_own, "mp", axis=1, tiled=True)
    a2_s, a2_t = mm(b1[:n_s], h2_s), mm(b1[n_s:], h2_t)
    b2_s = gelu_exact(a2_s).astype(bf16)
    b2_t = gelu_exact(a2_t).astype(bf16)
    third = sum_over(jnp.concatenate([mm(b2_s, h3_s, NT), mm(b2_t, h3_t, NT)], axis=0), ("mp",))
    inv = lax.rsqrt(jnp.sum(third * third, axis=-1, keepdims=True) + 1e-06)
    unit = (third * inv).astype(bf16)
    unit_all = gather_over(unit, "dp")
    z_s = unit_all[:, :n_s].reshape(dp_count * n_s, -1)
    z_t = unit_all[:, n_s:].reshape(dp_count * n_t, -1)
    images = dp_count * mp_count
    scaled_s = mm(z_s, proto_s) / TAU_S
    glob = mm(z_t, proto_t)
    center_own = lax.dynamic_slice_in_dim(center, dp_index * proto_cols, proto_cols)
    scaled_t = (glob - center_own) / TAU_T
    center_part = jnp.sum(glob, axis=0)
    max_s = jnp.max(scaled_s, axis=-1, keepdims=True)
    max_t = jnp.max(scaled_t, axis=-1, keepdims=True)
    exp_s, exp_t = jnp.exp(scaled_s - max_s), jnp.exp(scaled_t - max_t)
    cross = mm(exp_t, scaled_s, NT, precise)
    same = jnp.arange(images * 2)[:, None] // 2 == jnp.arange(images * CROPS)[None, :] // CROPS
    cross = jnp.sum(
        jnp.where(same, cross, 0.0).reshape(images * 2, images, CROPS), axis=1
    )
    stats = jnp.concatenate(
        [
            max_s.reshape(-1),
            jnp.sum(exp_s, axis=-1),
            max_t.reshape(-1),
            jnp.sum(exp_t, axis=-1),
            cross.reshape(-1),
        ]
    )
    stats = gather_over(stats, ("dp", "mp"))
    r_s, r_t = images * CROPS, images * 2
    maxes_s, sums_s = stats[:, :r_s], stats[:, r_s : 2 * r_s]
    maxes_t, sums_t = stats[:, 2 * r_s : 2 * r_s + r_t], stats[:, 2 * r_s + r_t : 2 * (r_s + r_t)]
    crosses = stats[:, 2 * (r_s + r_t) :].reshape(images, r_t, CROPS)
    top_s, top_t = jnp.max(maxes_s, axis=0), jnp.max(maxes_t, axis=0)
    total_s = jnp.sum(sums_s * jnp.exp(maxes_s - top_s), axis=0)
    shrink_t = jnp.exp(maxes_t - top_t)
    total_t = jnp.sum(sums_t * shrink_t, axis=0)
    cross_total = jnp.sum(crosses * shrink_t[:, :, None], axis=0) / total_t[:, None]
    log_norm = (jnp.log(total_s) + top_s).reshape(images, 1, CROPS)
    crop_ids = jnp.arange(CROPS)
    pairs = (
        (crop_ids[None, None, :] != jnp.arange(2)[None, :, None])
        & (crop_ids[None, None, :] < 2 + counts[:, None, None])
    ).astype(f32)
    image_weight = 1.0 / (2.0 * counts.astype(f32) + 2.0)
    pair_weight = pairs * image_weight[:, None, None]
    entropy = log_norm - cross_total.reshape(images, 2, CROPS)
    loss_total = jnp.sum(entropy * pair_weight)
    coef_s = jnp.sum(pair_weight, axis=1).reshape(-1, 1) / total_s[:, None]
    coef_s = coef_s * jnp.exp(max_s - top_s[:, None])
    coef_t = jnp.exp(max_t[:, 0] - top_t) / total_t
    coef_t = pair_weight.reshape(r_t, CROPS) * coef_t[:, None]
    mix = jnp.where(same, jnp.tile(coef_t, (1, images)), 0.0)
    grad_scaled = (coef_s * exp_s - mm(mix, exp_t, TN, precise)) / TAU_S
    grad_logits = grad_scaled.astype(bf16)
    grad_unit_part = mm(grad_logits, proto_s, NT)
    grad_proto = mm(z_s, grad_logits, TN)

    grad_unit = lax.all_to_all(grad_unit_part.reshape(dp_count, n_s, -1), "dp", 0, 0)
    grad_unit = sum_over(jnp.sum(grad_unit, axis=0), ("mp",))
    third_s, inv_s = third[:n_s], inv[:n_s]
    along = jnp.sum(grad_unit * third_s, axis=-1, keepdims=True)
    grad_third = (inv_s * grad_unit - third_s * (inv_s * inv_s * inv_s * along)).astype(bf16)
    grad_a2 = (mm(grad_third, h3_s) * gelu_slope(a2_s)).astype(bf16)
    grad_b1 = mm(grad_a2, h2_s, NT).reshape(n_s, mp_count, head_cols).transpose(1, 0, 2)
    grad_b1 = jnp.sum(lax.all_to_all(grad_b1, "mp", 0, 0), axis=0)
    grad_a1 = (grad_b1 * gelu_slope(a1_s)).astype(bf16)
    grad_feats = sum_over(mm(grad_a1, h1_s, NT), ("mp",))
    grad_cls, head_gain, head_bias = norm_back(cls_s, gain_s, grad_feats)
    grad_y = lax.dynamic_slice_in_dim(grad_cls, mp_index * CROPS, CROPS, 0)
    grad_y = jnp.concatenate([grad_y, jnp.zeros((CLS - CROPS, D), f32)], axis=0)
    proto_square = jnp.sum(grad_proto * grad_proto)
    proto_rows = proto_w.shape[0]

    def pick_proto(i):
        return lax.dynamic_slice_in_dim(grad_proto, unsigned(i * proto_rows), proto_rows, 0)

    proto_g = swap_over(pick_proto, "dp", grad_unit)
    proto_g = proto_g.transpose(1, 0, 2).reshape(proto_rows, -1)
    rows_left = jnp.concatenate([feats_s, b1[:n_s], grad_third], axis=1)
    head_rows = head_w.shape[0]

    left = rows_left.reshape(n_s, dp_count, head_rows).transpose(1, 0, 2)
    left = lax.all_to_all(left, "dp", 0, 0).reshape(dp_count * n_s, head_rows)
    right = lax.all_gather(jnp.concatenate([grad_a1, grad_a2, b2_s], axis=1), "dp", axis=0)
    right = right.reshape(dp_count * n_s, 3 * head_cols)
    dwt1, dgains1, grad_x1 = last_bwd(
        CROPS, x1, weights, 3, norm_params[4:8], seg_cls, segment[None], slot, saved1, grad_y
    )
    send1, own1 = core_halves(dwt1, dp_count, core)
    grad_x1, send1 = lax.optimization_barrier((grad_x1, send1))
    got1 = lax.ppermute(send1, "mp", flip_perm(4, 1))
    dwt0, dgains0b, grad_x2 = mlp_bwd(weights, 2, norm_params[0:4], saved0[3], grad_x1)
    grad_x2, got1 = lax.optimization_barrier((grad_x2, got1))
    ring1 = RingScatter(own1 + got1)
    ring1.step(0)
    block_args = (weights, 2, norm_params[0:4], seg_col, seg_row, slot, saved0)
    dwt0, grad_h1 = attention_bwd(0, *block_args, grad_x2, dwt0)
    grad_h1 = ring1.tie(grad_h1)
    ring1.step(1)
    dwt0, dgains0a = attention_bwd(1, *block_args, grad_x2, dwt0, (x0, grad_h1))
    send0, own0 = core_halves(dwt0, dp_count, core)
    send0, proto_g, left, right = lax.optimization_barrier(
        (ring1.tie(send0), proto_g, left, right)
    )
    stack_ids = dp_index * head_rows + jnp.arange(head_rows)[None, :]
    edges = (0, D, D + HID, D + HID + third.shape[1])
    head_own = sum(
        mm(
            jnp.where((stack_ids >= edges[i]) & (stack_ids < edges[i + 1]), left, 0).astype(bf16),
            right[:, i * head_cols : (i + 1) * head_cols],
            TN,
        )
        for i in range(3)
    )
    ring1.step(2)
    ring0 = RingScatter(own0 + lax.ppermute(send0, "mp", flip_perm(4, 1)))
    ring0.step(0)
    ring1.step(3)
    block_g1 = across_sum(ring1.total(), across)
    for index in range(1, RingScatter.steps):
        ring0.step(index)
    block_g = jnp.stack([across_sum(ring0.total(), across), block_g1])
    head_square = jnp.sum(head_own * head_own)
    center_total = gather_over(center_part, "dp").reshape(-1)
    head_first = (mp_index == 0).astype(f32)
    square = head_square + proto_square
    norm_part = jnp.concatenate(
        [
            dgains0a,
            dgains0b,
            dgains1,
            head_first * head_gain,
            head_first * head_bias,
            jnp.full((1, D), square),
            jnp.zeros((5, D), f32),
        ],
        axis=0,
    )
    norm_part = sum_over(norm_part, ("mp",))
    norm_rows_sent = thirds(norm_part).reshape(LAYERS, -1, D)
    columns = jnp.concatenate([block_g.astype(bf16), norm_rows_sent], axis=1)
    columns = ring_gather(columns).transpose(1, 0, 2, 3)
    norm_sum = whole_of(columns[:, :, col_width:])
    norm_total = norm_sum[:10]
    columns = columns[:, :, :col_width].reshape(LAYERS, dp_count * col_width, D)
    wide = columns.astype(f32)
    block_square = sum_over(jnp.full((1, 128), jnp.sum(wide * wide)), ("mp",))[0, 0]
    grad_norm = jnp.sqrt(norm_sum[10, 0] + block_square + jnp.sum(norm_total * norm_total))
    clip_factor = jnp.minimum(1.0, CLIP_NORM / (grad_norm + 1e-06))
    bounds = (0, 384, 512, 896, 1280)
    longest = 384

    def kind_rows(kind):
        start = jnp.array(bounds[:4])[kind]
        rows = lax.dynamic_slice_in_dim(columns, start, longest, 1)
        inside = start + jnp.arange(longest) < jnp.array(bounds[1:])[kind]
        return jnp.where(inside[None, :, None], rows, 0).astype(bf16)

    kinds = [kind_rows(mp_index)] + [
        lax.ppermute(kind_rows(mp_index ^ flip), "mp", flip_perm(mp_count, flip))
        for flip in (1, 2, 3)
    ]
    kinds = jnp.concatenate(kinds, axis=1)
    stat = lax.dot_general(
        kinds, kinds, (((1,), (1,)), ((0,), (0,))), preferred_element_type=f32
    )
    stats_own = lax.dynamic_index_in_dim(precond_stats, mp_index, 1, keepdims=False)
    bases_own = lax.dynamic_index_in_dim(rotation_bases, mp_index, 1, keepdims=False)
    stats_own = SHAMPOO_BETA * stats_own + (1 - SHAMPOO_BETA) * (clip_factor * clip_factor) * stat
    far_stats = lax.ppermute(stats_own, "mp", flip_perm(4, 2))
    stats_own, head_own = lax.optimization_barrier((stats_own, head_own))
    far_head = lax.ppermute(head_own, "mp", flip_perm(4, 2))
    basis_own, late_clip, far_head = lax.optimization_barrier(
        (renew_bases(stats_own, bases_own), clip_factor, far_head)
    )
    head_g = gather_mats(head_own, far_head, across, core).transpose(1, 0, 2)
    head_g = head_g.reshape(head_rows, -1)
    new_head_w, new_head_m, new_head_v = adamw(
        head_w, late_clip * head_g, head_m, head_v, LR_HEAD, WEIGHT_DECAY
    )
    new_proto_w, new_proto_m, new_proto_v = adamw(
        proto_w, late_clip * proto_g, proto_m, proto_v, LR_PROTO, WEIGHT_DECAY
    )
    new_teacher_head = TEACHER_MOM * teacher_head + (1 - TEACHER_MOM) * new_head_w
    new_teacher_proto = TEACHER_MOM * teacher_proto + (1 - TEACHER_MOM) * new_proto_w
    beside = (
        new_head_w, new_head_m, new_head_v, new_proto_w, new_proto_m, new_proto_v,
        new_teacher_head, new_teacher_proto,
    )
    far_bases = lax.ppermute(basis_own, "mp", flip_perm(4, 2))
    far_stats, far_bases, beside = lax.optimization_barrier((far_stats, far_bases, beside))
    new_bases = gather_mats(basis_own, far_bases, across, core)
    new_stats = gather_mats(stats_own, far_stats, across, core).transpose(1, 0, 2, 3)
    (
        new_head_w, new_head_m, new_head_v, new_proto_w, new_proto_m, new_proto_v,
        new_teacher_head, new_teacher_proto,
    ) = beside
    new_bases = new_bases.transpose(1, 0, 2, 3)
    col_ids = dp_index * col_width + jnp.arange(col_width)
    col_masks = jnp.stack(
        [((col_ids >= bounds[k]) & (col_ids < bounds[k + 1])).astype(f32) for k in range(4)]
    )
    grad_cols = clip_factor * block_g
    rotated = jnp.einsum("lkde,lcd,kc->lec", new_bases, grad_cols, col_masks, precision=precise)
    first_mom = ROT_ONE * block_m[:, :, 0] + (1 - ROT_ONE) * rotated
    second_mom = ROT_TWO * block_v[:, :, 0] + (1 - ROT_TWO) * rotated * rotated
    direction = adam_direction(first_mom, second_mom, ROT_ONE, ROT_TWO)
    turned_back = jnp.einsum("lkde,lec,kc->ldc", new_bases, direction, col_masks, precision=precise)
    master = block_w[:, :, 0]
    new_block_w = (master - LR_BLOCK * (turned_back + WEIGHT_DECAY * master))[:, :, None]
    new_norm, new_norm_m, new_norm_v = adamw(
        norm_params, clip_factor * norm_total, norm_m, norm_v, LR_NORM, 0.0
    )
    new_teacher_block = TEACHER_MOM * teacher_block + (1 - TEACHER_MOM) * new_block_w
    new_teacher_norm = TEACHER_MOM * teacher_norm + (1 - TEACHER_MOM) * new_norm
    new_center = CENTER_MOM * center + (1 - CENTER_MOM) * center_total / (2.0 * images)
    return (
        loss_total, grad_norm, new_block_w, first_mom[:, :, None], second_mom[:, :, None],
        new_bases, new_stats, new_head_w, new_head_m, new_head_v,
        new_proto_w, new_proto_m, new_proto_v, new_norm, new_norm_m, new_norm_v,
        new_teacher_block, new_teacher_head, new_teacher_proto, new_teacher_norm, new_center,
    )


def solution(mesh):
    block, head, proto, rep = P(None, None, "mp", "dp"), P("dp", None), P("dp", "mp"), P()
    in_specs = (
        P(None, ("dp", "mp"), None), P(None, "dp"), rep, block, block, block, rep, rep,
        head, head, head, proto, proto, proto, rep, rep, rep, block, head, proto, rep, P("mp"),
    )
    out_specs = (
        rep, rep, block, block, block, rep, rep, head, head, head, proto, proto, proto,
        rep, rep, rep, block, head, proto, rep, P("mp"),
    )
    return jax.shard_map(shards, mesh=mesh, in_specs=in_specs, out_specs=out_specs, check_vma=False)
```

```python
import functools

import jax
import jax.numpy as jnp
from jax import lax
from jax.experimental import pallas as pl
from jax.experimental.pallas import tpu as pltpu
from jax.sharding import PartitionSpec as P

D = 384
HD = 64
HID = 2048
LAYERS = 2
SLOT_DEV = 2
GLOBAL_TOK = 197
LOCAL_TOK = 37
MAX_LOCAL = 10
IMG_ROWS = 768
STEP = 10
MICRO = 2
CROPS = 12
GLOBAL_PAD = 200
LOCAL_PAD = 40
CHUNK = 400
CLS = 16

precise = lax.Precision.HIGHEST
TAU_S = 0.1
TAU_T = 0.07
CLIP_NORM = 0.005
BETA_ONE = 0.9
BETA_TWO = 0.999
ROT_ONE = 0.95
ROT_TWO = 0.95
SHAMPOO_BETA = 0.95
ADAM_EPS = 1e-08
WEIGHT_DECAY = 0.04
LR_BLOCK = 0.05
LR_HEAD = 0.03
LR_PROTO = 0.1
LR_NORM = 0.2
TEACHER_MOM = 0.7
CENTER_MOM = 0.9
NN = (((1,), (0,)), ((), ()))
NT = (((1,), (1,)), ((), ()))
TN = (((0,), (0,)), ((), ()))
bf16 = jnp.bfloat16
f32 = jnp.float32
VMEM_LIMIT = 58 * 1024 * 1024


def mm(lhs, rhs, dims=NN, precision=None):
    return lax.dot_general(lhs, rhs, dims, precision=precision, preferred_element_type=f32)


def normalize(inputs):
    centred = inputs - jnp.mean(inputs, axis=-1, keepdims=True)
    spread = jnp.mean(centred * centred, axis=-1, keepdims=True)
    inv = lax.rsqrt(spread + 1e-06)
    return centred * inv, inv


def norm_rows(inputs, gain, bias):
    return normalize(inputs)[0] * gain + bias


def norm_back(inputs, gain, grad_out):
    unit, inv = normalize(inputs)
    scaled = grad_out * gain
    grad = inv * (
        scaled
        - jnp.mean(scaled, axis=-1, keepdims=True)
        - unit * jnp.mean(scaled * unit, axis=-1, keepdims=True)
    )
    return (
        grad,
        jnp.sum(grad_out * unit, axis=0, keepdims=True),
        jnp.sum(grad_out, axis=0, keepdims=True),
    )


def gelu_cdf(inputs):
    return 0.5 + 0.5 * lax.erf(inputs * (0.5**0.5))


def gelu_exact(inputs):
    return inputs * gelu_cdf(inputs)


def gelu_slope(inputs):
    return gelu_cdf(inputs) + inputs * (jnp.exp(-0.5 * inputs * inputs) * 0.3989422804014327)


def low_half(shape):
    return lax.broadcasted_iota(jnp.int32, shape, 1) < HD


def halves(array):
    low = low_half(array.shape)
    zero = jnp.zeros_like(array)
    return jnp.where(low, array, zero), jnp.where(low, zero, array)


def block_fwd_kernel(
    x_ref, wt_ref, gains_ref, seg_col_ref, seg_row_ref, slot_ref,
    out_ref, h1_ref, qkv_ref, o_ref, x2_ref,
):
    x = x_ref[...]
    h1 = norm_rows(x, gains_ref[0:1], gains_ref[1:2]).astype(bf16)
    h1_ref[...] = h1
    allowed = seg_col_ref[0] == seg_row_ref[0]

    def heads(group, att):
        qkv = mm(h1, wt_ref[group, 0:384], NT).astype(bf16)
        qkv_ref[group] = qkv
        keys, values = qkv[:, 128:256], qkv[:, 256:384]
        mixes = []
        for query in halves(qkv[:, 0:128]):
            expd = jnp.where(allowed, jnp.exp(mm(query, keys, NT) * HD ** (-0.5)), 0.0)
            prob = expd / jnp.sum(expd, axis=-1, keepdims=True)
            mixes.append(mm(prob.astype(bf16), values))
        mix = jnp.where(low_half(mixes[0].shape), mixes[0], mixes[1])
        mix = (mix * slot_ref[group]).astype(bf16)
        o_ref[group] = mix
        return att + mm(mix, wt_ref[group, 384:512])

    att = lax.fori_loop(0, wt_ref.shape[0], heads, jnp.zeros(x.shape, f32))
    x2 = x + att
    x2_ref[...] = x2
    h2 = norm_rows(x2, gains_ref[2:3], gains_ref[3:4]).astype(bf16)

    def units(group, total):
        hidden = gelu_exact(mm(h2, wt_ref[group, 512:896], NT)).astype(bf16)
        return total + mm(hidden, wt_ref[group, 896:1280])

    out_ref[...] = x2 + lax.fori_loop(0, wt_ref.shape[0], units, jnp.zeros(x.shape, f32))


def mlp_bwd_kernel(last, wt_ref, gains_ref, x2_ref, grad_ref, *refs):
    if last:
        partial_ref, _, dwt_ref, dx2_ref, dgains_ref = refs
    else:
        dwt_ref, dx2_ref = refs

    @pl.when(pl.program_id(0) == 0)
    def _():
        dwt_ref[...] = jnp.zeros_like(dwt_ref)
        if last:
            dgains_ref[...] = jnp.zeros_like(dgains_ref)

    grad = grad_ref[...]
    grad_low = grad.astype(bf16)
    x2 = x2_ref[...]
    h2 = norm_rows(x2, gains_ref[2:3], gains_ref[3:4]).astype(bf16)

    def units(group, total):
        up = mm(h2, wt_ref[group, 512:896], NT)
        cdf = gelu_cdf(up)
        hidden = (up * cdf).astype(bf16)
        slope = cdf + up * (jnp.exp(-0.5 * up * up) * 0.3989422804014327)
        grad_up = (mm(grad_low, wt_ref[group, 896:1280], NT) * slope).astype(bf16)
        dwt_ref[group, 512:896] += mm(grad_up, h2, TN)
        dwt_ref[group, 896:1280] += mm(hidden, grad_low, TN)
        return total + mm(grad_up, wt_ref[group, 512:896])

    start = partial_ref[...] if last else jnp.zeros(grad.shape, f32)
    grad_h2 = lax.fori_loop(0, wt_ref.shape[0], units, start)
    if last:
        grad_x2, gain_two, bias_two = norm_back(x2, gains_ref[2:3], grad_h2)
        dx2_ref[...] = grad + grad_x2
        dgains_ref[...] += jnp.concatenate([gain_two, bias_two], axis=0)
    else:
        dx2_ref[...] = grad_h2


def attention_bwd_kernel(
    last, wt_ref, gains_ref, seg_col_ref, seg_row_ref, slot_ref, h1_ref, qkv_ref, o_ref, dx2_ref,
    *refs,
):
    if last:
        x_ref, partial_ref, _, dwt_ref, dgains_ref = refs
    else:
        _, dwt_ref, dh1_ref = refs

    @pl.when(pl.program_id(0) == 0)
    def _():
        dwt_ref[...] = jnp.zeros_like(dwt_ref)
        if last:
            dgains_ref[...] = jnp.zeros_like(dgains_ref)

    grad_att = dx2_ref[...].astype(bf16)
    allowed = seg_col_ref[0] == seg_row_ref[0]
    h1 = h1_ref[...]

    def heads(group, total):
        grad_mix = mm(grad_att, wt_ref[group, 384:512], NT).astype(bf16)
        grad_mix = grad_mix * slot_ref[group].astype(bf16)
        dwt_ref[group, 384:512] += mm(o_ref[group], grad_att, TN)
        qkv = qkv_ref[group]
        keys, values = qkv[:, 128:256], qkv[:, 256:384]
        grad_values = jnp.zeros(values.shape, f32)
        grad_keys = jnp.zeros(values.shape, f32)
        grad_queries = []
        for query, gmix in zip(halves(qkv[:, 0:128]), halves(grad_mix)):
            expd = jnp.where(allowed, jnp.exp(mm(query, keys, NT) * HD ** (-0.5)), 0.0)
            prob = expd * (1.0 / jnp.sum(expd, axis=-1, keepdims=True))
            grad_values = grad_values + mm(prob.astype(bf16), gmix, TN)
            grad_prob = mm(gmix, values, NT)
            scored = prob * (grad_prob - jnp.sum(prob * grad_prob, axis=-1, keepdims=True))
            scored = scored.astype(bf16)
            grad_queries.append(mm(scored, keys))
            grad_keys = grad_keys + mm(scored, query, TN)
        low = low_half(grad_queries[0].shape)
        grad_query = jnp.where(low, grad_queries[0], grad_queries[1]) * HD ** (-0.5)
        grad_qkv = jnp.concatenate(
            [grad_query.astype(bf16), (grad_keys * HD ** (-0.5)).astype(bf16), grad_values.astype(bf16)],
            axis=1,
        )
        dwt_ref[group, 0:384] += mm(grad_qkv, h1, TN)
        return total + mm(grad_qkv, wt_ref[group, 0:384])

    start = partial_ref[...] if last else jnp.zeros(h1.shape, f32)
    grad_h1 = lax.fori_loop(0, wt_ref.shape[0], heads, start)
    if last:
        _, gain_one, bias_one = norm_back(x_ref[...], gains_ref[0:1], grad_h1)
        dgains_ref[...] += jnp.concatenate([gain_one, bias_one], axis=0)
    else:
        dh1_ref[...] = grad_h1


def whole_spec(shape):
    return pl.BlockSpec(shape, lambda *_: (0,) * len(shape))


def block_specs(groups, layer):
    row = pl.BlockSpec((CHUNK, D), lambda c: (c, 0))
    return dict(
        row=row,
        wt=pl.BlockSpec((groups, 1280, D), lambda c: (0, 0, layer)),
        gains=whole_spec((4, D)),
        seg_col=pl.BlockSpec((1, CHUNK, 1), lambda c: (c, 0, 0)),
        seg_row=pl.BlockSpec((1, 1, CHUNK), lambda c: (c, 0, 0)),
        slot=whole_spec((groups, 1, 128)),
        qkv=pl.BlockSpec((groups, CHUNK, 384), lambda c: (0, c, 0)),
        mix=pl.BlockSpec((groups, CHUNK, 128), lambda c: (0, c, 0)),
    )


def block_fwd(x, weights, layer, gains, seg_col, seg_row, slot):
    rows, groups = x.shape[0], weights.shape[0]
    s = block_specs(groups, layer)
    return pl.pallas_call(
        block_fwd_kernel,
        grid=(rows // CHUNK,),
        in_specs=[s["row"], s["wt"], s["gains"], s["seg_col"], s["seg_row"], s["slot"]],
        out_specs=[s["row"], s["row"], s["qkv"], s["mix"], s["row"]],
        out_shape=[
            jax.ShapeDtypeStruct((rows, D), f32),
            jax.ShapeDtypeStruct((rows, D), bf16),
            jax.ShapeDtypeStruct((groups, rows, 384), bf16),
            jax.ShapeDtypeStruct((groups, rows, 128), bf16),
            jax.ShapeDtypeStruct((rows, D), f32),
        ],
        compiler_params=pltpu.CompilerParams(vmem_limit_bytes=VMEM_LIMIT),
        cost_estimate=pl.CostEstimate(
            flops=rows * 30_000_000, bytes_accessed=8_000_000, transcendentals=rows * 4000
        ),
    )(x, weights, gains, seg_col, seg_row, slot)


def mlp_bwd(part, weights, layer, gains, x2, grad, last=()):
    rows, groups = x2.shape[0], weights.shape[0] // 2
    s = block_specs(groups, layer)
    half = pl.BlockSpec((groups, 1280, D), lambda c: (part, 0, layer))
    any_spec = [pl.BlockSpec(memory_space=pl.ANY)] if last else []
    args = (weights, gains, x2, grad, *last)
    return pl.pallas_call(
        functools.partial(mlp_bwd_kernel, bool(last)),
        grid=(rows // CHUNK,),
        in_specs=[half, s["gains"], s["row"], s["row"]] + [s["row"]] * len(last[:1]) + any_spec,
        out_specs=[pl.BlockSpec((groups, 1280, D), lambda c: (part, 0, 0)), s["row"]]
        + [whole_spec((2, D))] * len(last[:1]),
        out_shape=[
            jax.ShapeDtypeStruct((2 * groups, 1280, D), f32),
            jax.ShapeDtypeStruct((rows, D), f32),
        ]
        + [jax.ShapeDtypeStruct((2, D), f32)] * len(last[:1]),
        input_output_aliases={len(args) - 1: 0} if last else {},
        compiler_params=pltpu.CompilerParams(vmem_limit_bytes=VMEM_LIMIT),
        cost_estimate=pl.CostEstimate(
            flops=rows * 13_000_000, bytes_accessed=8_000_000, transcendentals=rows * 3000
        ),
    )(*args)


def attention_bwd(part, weights, layer, gains, seg_col, seg_row, slot, saved, grad_x2, dwt, last=()):
    h1, qkv, mix, _ = saved
    rows, groups = h1.shape[0], weights.shape[0] // 2
    s = block_specs(groups, layer)
    heads = pl.BlockSpec((groups, 512, D), lambda c: (part, 0, 0))
    in_specs = [
        pl.BlockSpec((groups, 512, D), lambda c: (part, 0, layer)),
        s["gains"], s["seg_col"], s["seg_row"],
        pl.BlockSpec((groups, 1, 128), lambda c: (part, 0, 0)),
        s["row"],
        pl.BlockSpec((groups, CHUNK, 384), lambda c: (part, c, 0)),
        pl.BlockSpec((groups, CHUNK, 128), lambda c: (part, c, 0)),
        s["row"],
    ] + [s["row"]] * len(last)
    args = (weights, gains, seg_col, seg_row, slot, h1, qkv, mix, grad_x2, *last, dwt)
    return pl.pallas_call(
        functools.partial(attention_bwd_kernel, bool(last)),
        grid=(rows // CHUNK,),
        in_specs=in_specs + [pl.BlockSpec(memory_space=pl.ANY)],
        out_specs=[heads, whole_spec((2, D)) if last else s["row"]],
        out_shape=[
            jax.ShapeDtypeStruct(dwt.shape, f32),
            jax.ShapeDtypeStruct((2, D) if last else (rows, D), f32),
        ],
        input_output_aliases={len(args) - 1: 0},
        compiler_params=pltpu.CompilerParams(vmem_limit_bytes=VMEM_LIMIT),
        cost_estimate=pl.CostEstimate(
            flops=rows * 19_000_000, bytes_accessed=8_000_000, transcendentals=rows * 3000
        ),
    )(*args)


def crop_starts(crops):
    return [
        crop * GLOBAL_PAD if crop < 2 else 2 * GLOBAL_PAD + (crop - 2) * LOCAL_PAD
        for crop in range(crops)
    ]


def take_cls(ref, crops):
    rows = [ref[start : start + 1, :] for start in crop_starts(crops)]
    return jnp.concatenate(rows + [jnp.zeros((CLS - crops, ref.shape[1]), f32)], axis=0)


def last_fwd_kernel(
    crops, x_ref, wt_ref, gains_ref, seg_cls_ref, seg_row_ref, slot_ref,
    out_ref, h1_ref, kv_ref, q_ref, o_ref, x2_ref,
):
    gain, bias = gains_ref[0:1], gains_ref[1:2]
    h1 = norm_rows(x_ref[...], gain, bias).astype(bf16)
    h1_ref[...] = h1
    x_cls = take_cls(x_ref, crops)
    h1_cls = norm_rows(x_cls, gain, bias).astype(bf16)
    allowed = seg_cls_ref[...] == seg_row_ref[...]

    def heads(group, att):
        kv = mm(h1, wt_ref[group, 128:384], NT).astype(bf16)
        kv_ref[group] = kv
        query = mm(h1_cls, wt_ref[group, 0:128], NT).astype(bf16)
        q_ref[group] = query
        both = jnp.concatenate(halves(query), axis=0)
        scores = mm(both, kv[:, 0:128], NT) * HD ** (-0.5)
        expd = jnp.where(allowed, jnp.exp(scores), 0.0)
        prob = expd / jnp.sum(expd, axis=-1, keepdims=True)
        mix = mm(prob.astype(bf16), kv[:, 128:256])
        mix = jnp.where(low_half((CLS, 128)), mix[0:CLS], mix[CLS:])
        mix = (mix * slot_ref[group]).astype(bf16)
        o_ref[group] = mix
        return att + mm(mix, wt_ref[group, 384:512])

    att = lax.fori_loop(0, wt_ref.shape[0], heads, jnp.zeros((CLS, D), f32))
    x2 = x_cls + att
    x2_ref[...] = x2
    h2 = norm_rows(x2, gains_ref[2:3], gains_ref[3:4]).astype(bf16)

    def units(group, total):
        hidden = gelu_exact(mm(h2, wt_ref[group, 512:896], NT)).astype(bf16)
        return total + mm(hidden, wt_ref[group, 896:1280])

    out_ref[...] = x2 + lax.fori_loop(0, wt_ref.shape[0], units, jnp.zeros((CLS, D), f32))


def last_bwd_kernel(
    crops, x_ref, wt_ref, gains_ref, seg_cls_ref, seg_row_ref, slot_ref,
    h1_ref, kv_ref, q_ref, o_ref, x2_ref, grad_ref,
    dwt_ref, dgains_ref, dx_ref,
):
    grad = grad_ref[...]
    grad_low = grad.astype(bf16)
    x2 = x2_ref[...]
    h2 = norm_rows(x2, gains_ref[2:3], gains_ref[3:4]).astype(bf16)
    groups = wt_ref.shape[0]

    def units(group, total):
        up = mm(h2, wt_ref[group, 512:896], NT)
        hidden = gelu_exact(up).astype(bf16)
        grad_up = (mm(grad_low, wt_ref[group, 896:1280], NT) * gelu_slope(up)).astype(bf16)
        dwt_ref[group, 512:896] = mm(grad_up, h2, TN)
        dwt_ref[group, 896:1280] = mm(hidden, grad_low, TN)
        return total + mm(grad_up, wt_ref[group, 512:896])

    grad_h2 = lax.fori_loop(0, groups, units, jnp.zeros((CLS, D), f32))
    grad_x2, gain_two, bias_two = norm_back(x2, gains_ref[2:3], grad_h2)
    grad_x2 = grad + grad_x2
    grad_att = grad_x2.astype(bf16)
    allowed = seg_cls_ref[...] == seg_row_ref[...]
    h1 = h1_ref[...]
    h1_cls = norm_rows(take_cls(x_ref, crops), gains_ref[0:1], gains_ref[1:2]).astype(bf16)

    def heads(group, carry):
        total, total_cls = carry
        grad_mix = mm(grad_att, wt_ref[group, 384:512], NT).astype(bf16)
        grad_mix = grad_mix * slot_ref[group].astype(bf16)
        dwt_ref[group, 384:512] = mm(o_ref[group], grad_att, TN)
        kv = kv_ref[group]
        keys, values = kv[:, 0:128], kv[:, 128:256]
        both = jnp.concatenate(halves(q_ref[group]), axis=0)
        gboth = jnp.concatenate(halves(grad_mix), axis=0)
        expd = jnp.where(allowed, jnp.exp(mm(both, keys, NT) * HD ** (-0.5)), 0.0)
        prob = expd / jnp.sum(expd, axis=-1, keepdims=True)
        grad_prob = mm(gboth, values, NT)
        scored = prob * (grad_prob - jnp.sum(prob * grad_prob, axis=-1, keepdims=True))
        scored = scored.astype(bf16)
        grad_values = mm(prob.astype(bf16), gboth, TN)
        grad_keys = mm(scored, both, TN) * HD ** (-0.5)
        grad_query = mm(scored, keys)
        low = low_half((CLS, 128))
        grad_query = jnp.where(low, grad_query[0:CLS], grad_query[CLS:]) * HD ** (-0.5)
        grad_query = grad_query.astype(bf16)
        grad_kv = jnp.concatenate([grad_keys.astype(bf16), grad_values.astype(bf16)], axis=1)
        dwt_ref[group, 0:128] = mm(grad_query, h1_cls, TN)
        dwt_ref[group, 128:384] = mm(grad_kv, h1, TN)
        return (
            total + mm(grad_kv, wt_ref[group, 128:384]),
            total_cls + mm(grad_query, wt_ref[group, 0:128]),
        )

    grad_h1, grad_cls = lax.fori_loop(
        0, groups, heads, (jnp.zeros(h1.shape, f32), jnp.zeros((CLS, D), f32))
    )
    dx_ref[...] = grad_h1
    starts = crop_starts(crops)
    for crop, start in enumerate(starts):
        dx_ref[start : start + 1, :] += grad_cls[crop : crop + 1, :]
    grad_x, gain_one, bias_one = norm_back(x_ref[...], gains_ref[0:1], dx_ref[...])
    dx_ref[...] = grad_x
    for crop, start in enumerate(starts):
        dx_ref[start : start + 1, :] += grad_x2[crop : crop + 1, :]
    dgains_ref[...] = jnp.concatenate([gain_one, bias_one, gain_two, bias_two], axis=0)


def last_in_specs(rows, groups, layer):
    return [
        whole_spec((rows, D)),
        pl.BlockSpec((groups, 1280, D), lambda i: (0, 0, layer)),
        whole_spec((4, D)),
        whole_spec((2 * CLS, 1)),
        whole_spec((1, rows)),
        whole_spec((groups, 1, 128)),
    ]


def last_saved(rows, groups):
    return [
        jax.ShapeDtypeStruct((rows, D), bf16),
        jax.ShapeDtypeStruct((groups, rows, 256), bf16),
        jax.ShapeDtypeStruct((groups, CLS, 128), bf16),
        jax.ShapeDtypeStruct((groups, CLS, 128), bf16),
        jax.ShapeDtypeStruct((CLS, D), f32),
    ]


def last_fwd(crops, x, weights, layer, gains, seg_cls, seg_row, slot):
    rows, groups = x.shape[0], weights.shape[0]
    out_shape = [jax.ShapeDtypeStruct((CLS, D), f32)] + last_saved(rows, groups)
    return pl.pallas_call(
        functools.partial(last_fwd_kernel, crops),
        grid=(1,),
        in_specs=last_in_specs(rows, groups, layer),
        out_specs=[whole_spec(a.shape) for a in out_shape],
        out_shape=out_shape,
        compiler_params=pltpu.CompilerParams(vmem_limit_bytes=VMEM_LIMIT),
        cost_estimate=pl.CostEstimate(
            flops=rows * 15_000_000, bytes_accessed=8_000_000, transcendentals=rows * 200
        ),
    )(x, weights, gains, seg_cls, seg_row, slot)


def last_bwd(crops, x, weights, layer, gains, seg_cls, seg_row, slot, saved, grad):
    rows, groups = x.shape[0], weights.shape[0]
    out_shape = [
        jax.ShapeDtypeStruct((groups, 1280, D), f32),
        jax.ShapeDtypeStruct((4, D), f32),
        jax.ShapeDtypeStruct((rows, D), f32),
    ]
    return pl.pallas_call(
        functools.partial(last_bwd_kernel, crops),
        grid=(1,),
        in_specs=last_in_specs(rows, groups, layer)
        + [whole_spec(a.shape) for a in last_saved(rows, groups)]
        + [whole_spec((CLS, D))],
        out_specs=[whole_spec(a.shape) for a in out_shape],
        out_shape=out_shape,
        compiler_params=pltpu.CompilerParams(vmem_limit_bytes=VMEM_LIMIT),
        cost_estimate=pl.CostEstimate(
            flops=rows * 20_000_000, bytes_accessed=16_000_000, transcendentals=rows * 400
        ),
    )(x, weights, gains, seg_cls, seg_row, slot, *saved, grad)


PANEL = 32


def panel_steps(panels):
    lanes = lax.broadcasted_iota(jnp.int32, (PANEL, 128), 1)
    ids = lax.broadcasted_iota(jnp.int32, (PANEL, 1), 0)
    panels = list(panels)
    pivots = [jnp.zeros((PANEL, 1), f32) for _ in panels]
    for step in range(PANEL):
        here = lanes == step
        for i, panel in enumerate(panels):
            row = panel[step : step + 1]
            pivot = row[:, step : step + 1]
            column = jnp.where(ids > step, panel[:, step : step + 1], 0.0)
            source = jnp.where(here[0:1], 1.0, row) * (1.0 / pivot)
            cleared = jnp.where(here & (ids > step), 0.0, panel)
            panels[i] = cleared - column * source
            pivots[i] = jnp.where(ids == step, pivot, pivots[i])
    return panels, pivots


def basis_kernel(stats_ref, bases_ref, out_ref, gram_ref, inverse_ref):
    mats = stats_ref.shape[0]
    lanes = lax.broadcasted_iota(jnp.int32, (128, 128), 1)
    rows = lax.broadcasted_iota(jnp.int32, (128, 128), 0)
    near_lanes, near_rows = lanes[:PANEL], rows[:PANEL]
    for mat in range(mats):
        out_ref[mat] = mm(stats_ref[mat], bases_ref[mat], precision=precise)
    for block in range(D // 128):
        low, high = block * 128, block * 128 + 128
        for mat in range(mats):
            part = out_ref[mat, :, low:high]
            gram_ref[mat] = mm(part, part, TN, precise)

        def panels(index, carry):
            first = pl.multiple_of(index * PANEL, PANEL)
            last = first + PANEL
            started = [
                pltpu.roll(gram_ref[mat, pl.ds(first, PANEL), :], 128 - first, 1)
                for mat in range(mats)
            ]
            for mat, (panel, pivots) in enumerate(zip(*panel_steps(started))):
                panel = pltpu.roll(panel, first, 1)
                own = near_lanes - first
                unit = jnp.where(own < near_rows, panel, jnp.where(own == near_rows, 1.0, 0.0))
                inverse_ref[mat, pl.ds(first, PANEL), :] = unit * lax.rsqrt(pivots)
                source = jnp.where(near_lanes < last, unit, panel)
                factors = jnp.where(near_lanes < last, 0.0, panel / pivots)
                gram = gram_ref[mat]
                gram = jnp.where((lanes >= first) & (lanes < last) & (rows >= last), 0.0, gram)
                gram_ref[mat] = gram - mm(factors, source, TN, precise)
            return carry

        lax.fori_loop(0, 128 // PANEL, panels, 0)
        for mat in range(mats):
            part = mm(out_ref[mat, :, low:high], inverse_ref[mat], NT, precise)
            out_ref[mat, :, low:high] = part
            if high < D:
                rest = out_ref[mat, :, high:]
                cross = mm(part, rest, TN, precise)
                out_ref[mat, :, high:] = rest - mm(part, cross, NN, precise)


def renew_bases(new_stats, bases):
    mats = new_stats.shape[0]
    return pl.pallas_call(
        basis_kernel,
        in_specs=[pl.BlockSpec(memory_space=pltpu.VMEM)] * 2,
        out_specs=pl.BlockSpec(memory_space=pltpu.VMEM),
        out_shape=jax.ShapeDtypeStruct((mats, D, D), f32),
        scratch_shapes=[pltpu.VMEM((mats, 128, 128), f32), pltpu.VMEM((mats, 128, 128), f32)],
        compiler_params=pltpu.CompilerParams(vmem_limit_bytes=VMEM_LIMIT),
        cost_estimate=pl.CostEstimate(
            flops=60_000_000_000, bytes_accessed=6_000_000, transcendentals=1000
        ),
    )(new_stats, bases)


def crop_pairs(r_t, r_s):
    rows = lax.broadcasted_iota(jnp.int32, (r_t, r_s), 0)
    crops = lax.broadcasted_iota(jnp.int32, (r_t, r_s), 1)
    first = (rows // 2) * CROPS
    return (crops >= first) & (crops < first + CROPS), rows % 2 == 0


def spread_pairs(values, same, even):
    first = jnp.where(same & even, 1.0, 0.0)
    second = jnp.where(same & ~even, 1.0, 0.0)
    return mm(values, first, NN, precise), mm(values, second, NN, precise)


def logits_kernel(
    zs_ref, zt_ref, ps_ref, pt_ref, center_ref, exp_s_ref, exp_t_ref, stats_ref, part_ref
):
    scaled_s = mm(ps_ref[...], zs_ref[...], (((0,), (1,)), ((), ()))) / TAU_S
    glob = mm(pt_ref[...], zt_ref[...], (((0,), (1,)), ((), ())))
    part_ref[...] = jnp.sum(glob, axis=1, keepdims=True)
    scaled_t = (glob - center_ref[...]) / TAU_T
    max_s = jnp.max(scaled_s, axis=0, keepdims=True)
    max_t = jnp.max(scaled_t, axis=0, keepdims=True)
    exp_s = jnp.exp(scaled_s - max_s)
    exp_t = jnp.exp(scaled_t - max_t)
    exp_s_ref[...] = exp_s
    exp_t_ref[...] = exp_t
    same, even = crop_pairs(exp_t.shape[1], exp_s.shape[1])
    cross = jnp.where(same, mm(exp_t, scaled_s, TN, precise), 0.0)
    stats_ref[...] = jnp.concatenate(
        [
            max_s,
            jnp.sum(exp_s, axis=0, keepdims=True),
            *spread_pairs(max_t, same, even),
            *spread_pairs(jnp.sum(exp_t, axis=0, keepdims=True), same, even),
            jnp.sum(jnp.where(even, cross, 0.0), axis=0, keepdims=True),
            jnp.sum(jnp.where(even, 0.0, cross), axis=0, keepdims=True),
        ],
        axis=0,
    )


def prototype_logits(z_s, z_t, proto_s, proto_t, center):
    cols, r_s, r_t = proto_s.shape[1], z_s.shape[0], z_t.shape[0]
    return pl.pallas_call(
        logits_kernel,
        in_specs=[pl.BlockSpec(memory_space=pltpu.VMEM)] * 5,
        out_specs=[pl.BlockSpec(memory_space=pltpu.VMEM)] * 4,
        out_shape=[
            jax.ShapeDtypeStruct((cols, r_s), f32),
            jax.ShapeDtypeStruct((cols, r_t), f32),
            jax.ShapeDtypeStruct((8, r_s), f32),
            jax.ShapeDtypeStruct((cols, 1), f32),
        ],
        compiler_params=pltpu.CompilerParams(vmem_limit_bytes=VMEM_LIMIT),
        cost_estimate=pl.CostEstimate(
            flops=8_000_000_000, bytes_accessed=8_000_000, transcendentals=1_000_000
        ),
    )(z_s, z_t, proto_s, proto_t, center)


def join_stats(every):
    tops = jnp.max(every, axis=0)

    def add_up(row, shrink):
        return jnp.sum(every[:, row : row + 1] * shrink, axis=0)

    shrink = [jnp.exp(every[:, row : row + 1] - tops[row : row + 1][None]) for row in (0, 2, 3)]
    sums = [add_up(4, shrink[1]), add_up(5, shrink[2]), add_up(6, shrink[1]), add_up(7, shrink[2])]
    return jnp.concatenate([tops[0:1], add_up(1, shrink[0]), tops[2:4], *sums], axis=0)


def loss_kernel(
    all_ref, own_ref, weight_ref, exp_s_ref, exp_t_ref, zs_ref, ps_ref, dz_ref, dproto_ref, loss_ref
):
    every, own = all_ref[...], own_ref[...]
    every = join_stats(every) if every.ndim == 3 else every
    top_s, total_s, top_0, top_1 = every[0:1], every[1:2], every[2:3], every[3:4]
    total_0, total_1, cross_0, cross_1 = every[4:5], every[5:6], every[6:7], every[7:8]
    weight_0, weight_1 = weight_ref[0:1], weight_ref[1:2]
    log_norm = jnp.log(total_s) + top_s
    loss = weight_0 * (log_norm - cross_0 / total_0) + weight_1 * (log_norm - cross_1 / total_1)
    loss_ref[...] = jnp.broadcast_to(jnp.sum(loss, axis=1, keepdims=True), loss_ref.shape)
    coef_s = (weight_0 + weight_1) / total_s * jnp.exp(own[0:1] - top_s)
    coef_0 = weight_0 / total_0 * jnp.exp(own[2:3] - top_0)
    coef_1 = weight_1 / total_1 * jnp.exp(own[3:4] - top_1)
    same, even = crop_pairs(exp_t_ref.shape[1], exp_s_ref.shape[1])
    mix = jnp.where(same, jnp.where(even, coef_0, coef_1), 0.0)
    target = mm(exp_t_ref[...], mix, NN, precise)
    grad = ((coef_s * exp_s_ref[...] - target) / TAU_S).astype(bf16)
    dz_ref[...] = mm(grad, ps_ref[...], (((0,), (1,)), ((), ())))
    dproto_ref[...] = mm(zs_ref[...], grad, (((0,), (1,)), ((), ())))


def loss_and_grads(every, own, weights, exp_s, exp_t, z_s, proto_s):
    return pl.pallas_call(
        loss_kernel,
        in_specs=[pl.BlockSpec(memory_space=pltpu.VMEM)] * 7,
        out_specs=[pl.BlockSpec(memory_space=pltpu.VMEM)] * 3,
        out_shape=[
            jax.ShapeDtypeStruct(z_s.shape, f32),
            jax.ShapeDtypeStruct(proto_s.shape, f32),
            jax.ShapeDtypeStruct((1, 128), f32),
        ],
        compiler_params=pltpu.CompilerParams(vmem_limit_bytes=VMEM_LIMIT),
        cost_estimate=pl.CostEstimate(
            flops=8_000_000_000, bytes_accessed=8_000_000, transcendentals=10_000
        ),
    )(every, own, weights, exp_s, exp_t, z_s, proto_s)


def flip_perm(count, bit):
    return [(i, i ^ bit) for i in range(count)]


def flips(axis):
    count = lax.axis_size(axis)
    bits, bit = [], 1
    while bit < count:
        bits.append(bit)
        bit *= 2
    return count, bits


def thirds(array):
    high = lax.optimization_barrier(array.astype(bf16))
    rest = array - high.astype(f32)
    middle = lax.optimization_barrier(rest.astype(bf16))
    return jnp.stack([high, middle, (rest - middle.astype(f32)).astype(bf16)])


def whole_of(parts):
    layers, count = parts.shape[:2]
    parts = parts.transpose(1, 0, 2, 3).reshape(count, 3, -1, parts.shape[-1]).astype(f32)
    return jnp.sum(parts[:, 0] + (parts[:, 1] + parts[:, 2]), axis=0)


def sum_over(array, axes):
    for axis in axes:
        count, bits = flips(axis)
        for bit in bits:
            array = array + lax.ppermute(array, axis, flip_perm(count, bit))
    return array


def shift_perm(count, step):
    return [(i, (i + step) % count) for i in range(count)]


def gather_over(array, axis):
    count = lax.axis_size(axis)
    if lax.axis_size("dp") > 8:
        return lax.all_gather(array, axis, axis=0)
    return lax.all_to_all(jnp.broadcast_to(array[None], (count, *array.shape)), axis, 0, 0)


def swap_pieces(pick, after=None):
    count = lax.axis_size("dp")
    me = lax.axis_index("dp")
    if count > 8:
        return [lax.all_to_all(jnp.stack([pick(i) for i in range(count)]), "dp", 0, 0)]
    picks = [pick(lax.rem(me + step, count)) for step in range(1, count)]
    if after is not None:
        picks, _ = lax.optimization_barrier((picks, after))
    got = [
        lax.ppermute(piece, "dp", shift_perm(count, step + 1)) for step, piece in enumerate(picks)
    ]
    return [pick(me), *got]


def swap_joined(pieces):
    if len(pieces) == 1:
        return pieces[0]
    count = lax.axis_size("dp")
    out = jnp.zeros((count, *pieces[0].shape), pieces[0].dtype)
    for step, piece in enumerate(pieces):
        out = put(out, piece, lax.rem(lax.axis_index("dp") + (count - step), count))
    return out


RING = (0, 2, 4, 6, 7, 5, 3, 1)


def unsigned(index):
    return lax.convert_element_type(index, jnp.uint32)


def put(out, piece, index):
    return lax.dynamic_update_index_in_dim(out, piece, unsigned(index), 0)


def ring_at(offset):
    count = len(RING)
    table = [RING[(RING.index(i) + offset) % count] for i in range(count)]
    return lax.dynamic_slice(
        jnp.array(table, jnp.uint32), (lax.axis_index("dp").astype(jnp.uint32),), (1,)
    )[0]


def ring_perm(step):
    count = len(RING)
    return [(RING[i], RING[(i + step) % count]) for i in range(count)]


def ring_gather(piece):
    count = lax.axis_size("dp")
    if count != len(RING):
        return lax.all_gather(piece, "dp", axis=0)
    out = put(jnp.zeros((count, *piece.shape), piece.dtype), piece, lax.axis_index("dp"))
    right = left = piece
    for step in range(1, count // 2):
        right = lax.ppermute(right, "dp", ring_perm(1))
        left = lax.ppermute(left, "dp", ring_perm(-1))
        out = put(out, right, ring_at(-step))
        out = put(out, left, ring_at(step))
    half = piece.shape[-2] // 2
    right = lax.ppermute(right[..., :half, :], "dp", ring_perm(1))
    left = lax.ppermute(left[..., half:, :], "dp", ring_perm(-1))
    return put(out, jnp.concatenate([right, left], axis=-2), ring_at(count // 2))


class RingScatter:
    steps = len(RING) // 2

    def __init__(self, parts):
        self.parts = parts
        self.ringed = lax.axis_size("dp") == len(RING)
        self.right = self.left = None
        if self.ringed:
            far = self.own(self.steps)
            self.send_right, self.send_left = far[0:1], far[1:2]

    def own(self, offset):
        return lax.dynamic_index_in_dim(self.parts, ring_at(offset), 1, keepdims=False)

    def step(self, index):
        if not self.ringed:
            return
        if index > 0:
            right, left = self.own(self.steps - index), self.own(index - self.steps)
            if index == 1:
                right = jnp.concatenate([right[0:1] + self.right, right[1:2]])
                left = jnp.concatenate([left[0:1], left[1:2] + self.left])
            else:
                right, left = right + self.right, left + self.left
            self.send_right, self.send_left = right, left
        self.right = lax.ppermute(self.send_right, "dp", ring_perm(1))
        self.left = lax.ppermute(self.send_left, "dp", ring_perm(-1))

    def tie(self, other):
        if self.ringed:
            other, self.right, self.left = lax.optimization_barrier((other, self.right, self.left))
        return other

    def total(self):
        if not self.ringed:
            return lax.psum_scatter(self.parts, "dp", scatter_dimension=1, tiled=True)[:, 0]
        return self.own(0) + self.right + self.left


def core_halves(grad, dp_count, core):
    parts = grad.reshape(2, 2, dp_count, -1, D)
    send = lax.dynamic_index_in_dim(parts, unsigned(1 - core), 1, keepdims=False)
    return send, lax.dynamic_index_in_dim(parts, unsigned(core), 1, keepdims=False)


def across_sum(parts, across):
    send = lax.dynamic_index_in_dim(parts, unsigned(1 - across), 0, keepdims=False)
    own = lax.dynamic_index_in_dim(parts, unsigned(across), 0, keepdims=False)
    return own + lax.ppermute(send, "mp", flip_perm(4, 2))


def gather_mats(own, far, across, core):
    pair = put(jnp.stack([own, own]), far, 1 - across)
    other = lax.ppermute(pair, "mp", flip_perm(4, 1))
    whole = jnp.zeros((2, 2, *own.shape), own.dtype)
    whole = lax.dynamic_update_index_in_dim(whole, pair, unsigned(core), 1)
    whole = lax.dynamic_update_index_in_dim(whole, other, unsigned(1 - core), 1)
    return whole.reshape(4, *own.shape)


def adam_direction(first_mom, second_mom, beta_one, beta_two):
    return (
        first_mom / (1 - beta_one**STEP) / (jnp.sqrt(second_mom / (1 - beta_two**STEP)) + ADAM_EPS)
    )


def adamw(weight, grad_in, first_mom, second_mom, rate, decay):
    first_mom = BETA_ONE * first_mom + (1 - BETA_ONE) * grad_in
    second_mom = BETA_TWO * second_mom + (1 - BETA_TWO) * grad_in * grad_in
    weight = weight - rate * (
        adam_direction(first_mom, second_mom, BETA_ONE, BETA_TWO) + decay * weight
    )
    return (weight, first_mom, second_mom)


def row_layout(crop_count):
    rows = jnp.arange(2 * CHUNK)
    is_global = rows < 2 * GLOBAL_PAD
    local = rows - 2 * GLOBAL_PAD
    crop = jnp.where(is_global, rows // GLOBAL_PAD, 2 + local // LOCAL_PAD)
    offset = jnp.where(is_global, rows % GLOBAL_PAD, local % LOCAL_PAD)
    real = offset < jnp.where(is_global, GLOBAL_TOK, LOCAL_TOK)
    source = jnp.where(
        is_global, crop * GLOBAL_TOK + offset, 2 * GLOBAL_TOK + (crop - 2) * LOCAL_TOK + offset
    )
    source = jnp.where(real, source, -1)
    segment = jnp.where(real & (crop < 2 + crop_count), crop, 1000 + rows)
    return source, segment.astype(jnp.int32)


def shards(
    tokens, crop_counts, slot_live, block_w, block_m, block_v, rotation_bases, precond_stats,
    head_w, head_m, head_v, proto_w, proto_m, proto_v, norm_params, norm_m, norm_v,
    teacher_block, teacher_head, teacher_proto, teacher_norm, center,
):
    mp_index = lax.axis_index("mp")
    dp_index = lax.axis_index("dp")
    mp_count = lax.axis_size("mp")
    dp_count = lax.axis_size("dp")
    col_width = block_w.shape[3]
    micro, place = mp_index % MICRO, mp_index // MICRO
    crop_count = crop_counts[micro, place]
    across, core = mp_index // 2, mp_index % 2
    own_t = [teacher_block[layer, :, 0].astype(bf16).T for layer in range(LAYERS)]
    own_s = [block_w[layer, :, 0].astype(bf16).T for layer in range(LAYERS)]
    weights = lax.all_gather(
        jnp.concatenate([*own_t, *own_s], axis=1), ("mp", "dp"), axis=0, tiled=True
    ).reshape(mp_count, -1, 2 * LAYERS * D)
    head_cols = head_w.shape[1] // mp_count
    proto_cols = proto_w.shape[1] // dp_count
    heads = jnp.concatenate(
        [
            lax.dynamic_slice_in_dim(part, unsigned(mp_index * head_cols), head_cols, 1)
            for part in (teacher_head, head_w)
        ],
        axis=1,
    ).astype(bf16)

    def pick_cols(i):
        return jnp.stack(
            [
                lax.dynamic_slice_in_dim(part, unsigned(i * proto_cols), proto_cols, 1).astype(bf16)
                for part in (teacher_proto, proto_w)
            ]
        )

    counts_own = jnp.stack([crop_counts[i % MICRO, i // MICRO] for i in range(mp_count)])
    counts = gather_over(counts_own[None], "dp").reshape(-1)
    other = lax.ppermute(
        lax.dynamic_index_in_dim(tokens, 1 - micro, 0, keepdims=False), "mp", flip_perm(mp_count, 1)
    )
    mine = lax.dynamic_index_in_dim(tokens, micro, 0, keepdims=False)
    first = micro == 0
    image = jnp.concatenate([jnp.where(first, mine, other), jnp.where(first, other, mine)], axis=0)
    source, segment = row_layout(crop_count)
    spread = (source[:, None] == jnp.arange(IMG_ROWS)[None, :]).astype(bf16)
    x0 = mm(spread, image)
    seg_col, seg_row = segment.reshape(2, CHUNK, 1), segment.reshape(2, 1, CHUNK)
    starts = crop_starts(CROPS)
    seg_cls = jnp.concatenate([segment[jnp.array(starts)], jnp.zeros((CLS - CROPS,), jnp.int32)])
    seg_cls = jnp.concatenate([seg_cls, seg_cls])[:, None]
    slot = jnp.repeat(slot_live.astype(f32).reshape(mp_count, SLOT_DEV), HD, axis=1)[:, None, :]
    protos = swap_joined(swap_pieces(pick_cols))
    center_own = lax.dynamic_slice_in_dim(center, unsigned(dp_index * proto_cols), proto_cols)
    center_own = center_own[:, None]
    crop_ids = jnp.arange(CROPS)
    pair_weight = (
        (crop_ids[None, None, :] != jnp.arange(2)[:, None, None])
        & (crop_ids[None, None, :] < 2 + counts[None, :, None])
    ).astype(f32) / (2.0 * counts.astype(f32) + 2.0)[None, :, None]
    pair_weight = pair_weight.reshape(2, -1)
    x0, weights, heads, protos, seg_col, seg_row, seg_cls, slot, center_own, pair_weight = (
        lax.optimization_barrier(
            (x0, weights, heads, protos, seg_col, seg_row, seg_cls, slot, center_own, pair_weight)
        )
    )
    heads = lax.all_gather(heads, "dp", axis=0, tiled=True)
    head_t, head_s = heads[:, :head_cols], heads[:, head_cols:]
    protos = protos.transpose(1, 0, 2, 3).reshape(2, -1, proto_cols)
    proto_t, proto_s = protos[0], protos[1]
    x0_t = x0[:CHUNK]
    x1_t = block_fwd(x0_t, weights, 0, teacher_norm[0:4], seg_col, seg_row, slot)[0]
    x1, *saved0 = block_fwd(x0, weights, 2, norm_params[0:4], seg_col, seg_row, slot)
    y_t = last_fwd(
        2, x1_t, weights, 1, teacher_norm[4:8], seg_cls, segment[None, :CHUNK], slot
    )[0]
    y_s, *saved1 = last_fwd(
        CROPS, x1, weights, 3, norm_params[4:8], seg_cls, segment[None], slot
    )
    y_all = lax.all_gather(jnp.concatenate([y_s[:CROPS], y_t[:4]], axis=0), "mp", axis=0)
    cls_s = y_all[:, :CROPS].reshape(mp_count * CROPS, D)
    cls_t = y_all[:, CROPS : CROPS + 2].reshape(mp_count * 2, D)
    n_s, n_t = cls_s.shape[0], cls_t.shape[0]
    h1_s, h2_s, h3_s = head_s[:D], head_s[D : D + HID], head_s[D + HID :]
    h1_t, h2_t, h3_t = head_t[:D], head_t[D : D + HID], head_t[D + HID :]
    gain_s, bias_s = norm_params[8:9], norm_params[9:10]
    feats_s = norm_rows(cls_s, gain_s, bias_s).astype(bf16)
    feats_t = norm_rows(cls_t, teacher_norm[8:9], teacher_norm[9:10]).astype(bf16)
    a1_s, a1_t = mm(feats_s, h1_s), mm(feats_t, h1_t)
    b1_own = jnp.concatenate([gelu_exact(a1_s), gelu_exact(a1_t)], axis=0).astype(bf16)
    b1 = lax.all_gather(b1_own, "mp", axis=1, tiled=True)
    a2_s, a2_t = mm(b1[:n_s], h2_s), mm(b1[n_s:], h2_t)
    b2_s = gelu_exact(a2_s).astype(bf16)
    b2_t = gelu_exact(a2_t).astype(bf16)
    third = sum_over(jnp.concatenate([mm(b2_s, h3_s, NT), mm(b2_t, h3_t, NT)], axis=0), ("mp",))
    inv = lax.rsqrt(jnp.sum(third * third, axis=-1, keepdims=True) + 1e-06)
    unit = (third * inv).astype(bf16)
    unit_all = gather_over(unit, "dp")
    z_s = unit_all[:, :n_s].reshape(dp_count * n_s, -1)
    z_t = unit_all[:, n_s:].reshape(dp_count * n_t, -1)
    images = dp_count * mp_count
    exp_s, exp_t, own_stats, center_part = prototype_logits(z_s, z_t, proto_s, proto_t, center_own)
    center_part = center_part.reshape(-1)
    all_stats = gather_over(own_stats, ("dp", "mp"))
    if dp_count > 8:
        all_stats = join_stats(all_stats)
    grad_unit_part, grad_proto, loss_total = loss_and_grads(
        all_stats, own_stats, pair_weight, exp_s, exp_t, z_s, proto_s
    )
    loss_total = loss_total[0, 0]
    grad_unit = lax.all_to_all(grad_unit_part.reshape(dp_count, n_s, -1), "dp", 0, 0)
    grad_unit = sum_over(jnp.sum(grad_unit, axis=0), ("mp",))
    third_s, inv_s = third[:n_s], inv[:n_s]
    along = jnp.sum(grad_unit * third_s, axis=-1, keepdims=True)
    grad_third = (inv_s * grad_unit - third_s * (inv_s * inv_s * inv_s * along)).astype(bf16)
    grad_a2 = (mm(grad_third, h3_s) * gelu_slope(a2_s)).astype(bf16)
    grad_b1 = mm(grad_a2, h2_s, NT).reshape(n_s, mp_count, head_cols).transpose(1, 0, 2)
    grad_b1 = jnp.sum(lax.all_to_all(grad_b1, "mp", 0, 0), axis=0)
    grad_a1 = (grad_b1 * gelu_slope(a1_s)).astype(bf16)
    grad_feats = sum_over(mm(grad_a1, h1_s, NT), ("mp",))
    grad_cls, head_gain, head_bias = norm_back(cls_s, gain_s, grad_feats)
    grad_y = lax.dynamic_slice_in_dim(grad_cls, mp_index * CROPS, CROPS, 0)
    grad_y = jnp.concatenate([grad_y, jnp.zeros((CLS - CROPS, D), f32)], axis=0)
    proto_square = jnp.sum(grad_proto * grad_proto)
    proto_rows = proto_w.shape[0]

    def pick_proto(i):
        return lax.dynamic_slice_in_dim(grad_proto, unsigned(i * proto_rows), proto_rows, 0)

    proto_g = swap_pieces(pick_proto, grad_unit)
    rows_left = jnp.concatenate([feats_s, b1[:n_s], grad_third], axis=1)
    head_rows = head_w.shape[0]

    left = rows_left.reshape(n_s, dp_count, head_rows).transpose(1, 0, 2)
    left = lax.all_to_all(left, "dp", 0, 0).reshape(dp_count * n_s, head_rows)
    right = lax.all_gather(jnp.concatenate([grad_a1, grad_a2, b2_s], axis=1), "dp", axis=0)
    right = right.reshape(dp_count * n_s, 3 * head_cols)
    dwt1, dgains1, grad_x1 = last_bwd(
        CROPS, x1, weights, 3, norm_params[4:8], seg_cls, segment[None], slot, saved1, grad_y
    )
    send1, own1 = core_halves(dwt1, dp_count, core)
    grad_x1, send1 = lax.optimization_barrier((grad_x1, send1))
    got1 = lax.ppermute(send1, "mp", flip_perm(4, 1))
    mlp_args = (weights, 2, norm_params[0:4], saved0[3], grad_x1)
    dwt0, grad_h2 = mlp_bwd(0, *mlp_args)
    grad_h2, got1, proto_g[1:3] = lax.optimization_barrier((grad_h2, got1, proto_g[1:3]))
    ring1 = RingScatter(own1 + got1)
    ring1.step(0)
    dwt0, grad_x2, dgains0b = mlp_bwd(1, *mlp_args, (grad_h2, dwt0))
    grad_x2, proto_g[3:5] = lax.optimization_barrier((ring1.tie(grad_x2), proto_g[3:5]))
    ring1.step(1)
    block_args = (weights, 2, norm_params[0:4], seg_col, seg_row, slot, saved0)
    dwt0, grad_h1 = attention_bwd(0, *block_args, grad_x2, dwt0)
    grad_h1, proto_g[5:7] = lax.optimization_barrier((ring1.tie(grad_h1), proto_g[5:7]))
    ring1.step(2)
    dwt0, dgains0a = attention_bwd(1, *block_args, grad_x2, dwt0, (x0, grad_h1))
    send0, own0 = core_halves(dwt0, dp_count, core)
    send0, proto_g, left, right = lax.optimization_barrier(
        (ring1.tie(send0), proto_g, left, right)
    )
    stack_ids = dp_index * head_rows + jnp.arange(head_rows)[None, :]
    edges = (0, D, D + HID, D + HID + third.shape[1])
    head_own = sum(
        mm(
            jnp.where((stack_ids >= edges[i]) & (stack_ids < edges[i + 1]), left, 0).astype(bf16),
            right[:, i * head_cols : (i + 1) * head_cols],
            TN,
        )
        for i in range(3)
    )
    ring1.step(3)
    ring0 = RingScatter(own0 + lax.ppermute(send0, "mp", flip_perm(4, 1)))
    ring0.step(0)
    block_g1 = across_sum(ring1.total(), across)
    for index in range(1, RingScatter.steps):
        ring0.step(index)
    block_g = jnp.stack([across_sum(ring0.total(), across), block_g1])
    head_square = jnp.sum(head_own * head_own)
    center_total = gather_over(center_part, "dp").reshape(-1)
    head_first = (mp_index == 0).astype(f32)
    square = head_square + proto_square
    norm_part = jnp.concatenate(
        [
            dgains0a,
            dgains0b,
            dgains1,
            head_first * head_gain,
            head_first * head_bias,
            jnp.full((1, D), square),
            jnp.zeros((5, D), f32),
        ],
        axis=0,
    )
    norm_part = sum_over(norm_part, ("mp",))
    norm_rows_sent = thirds(norm_part).reshape(LAYERS, -1, D)
    columns = jnp.concatenate([block_g.astype(bf16), norm_rows_sent], axis=1)
    columns = ring_gather(columns).transpose(1, 0, 2, 3)
    norm_sum = whole_of(columns[:, :, col_width:])
    norm_total = norm_sum[:10]
    columns, proto_g = lax.optimization_barrier((columns, proto_g))
    proto_g = swap_joined(proto_g).transpose(1, 0, 2).reshape(proto_rows, -1)
    columns = columns[:, :, :col_width].reshape(LAYERS, dp_count * col_width, D)
    wide = columns.astype(f32)
    block_square = sum_over(jnp.full((1, 128), jnp.sum(wide * wide)), ("mp",))[:, :1]
    norm_square = jnp.sum(norm_total * norm_total, axis=(0, 1), keepdims=True)
    grad_norm = jnp.sqrt(norm_sum[10:11, :1] + block_square + norm_square)
    clip_factor = jnp.minimum(1.0, CLIP_NORM / (grad_norm + 1e-06))
    bounds = (0, 384, 512, 896, 1280)
    longest = 384

    own_kind = unsigned(mp_index)
    starts = jnp.array([[bounds[kind ^ flip] for flip in range(4)] for kind in range(4)], jnp.uint32)

    def kind_rows(flip):
        start = lax.dynamic_slice(starts, (own_kind, jnp.uint32(flip)), (1, 1))[0, 0]
        rows = lax.dynamic_slice_in_dim(columns, start, longest, 1)
        inside = (jnp.arange(longest) < 128) | (mp_index != 1 ^ flip)
        return jnp.where(inside[None, :, None], rows, 0).astype(bf16)

    kinds = [kind_rows(0)] + [
        lax.ppermute(kind_rows(flip), "mp", flip_perm(mp_count, flip)) for flip in (1, 2, 3)
    ]
    kinds = jnp.concatenate(kinds, axis=1)
    stat = lax.dot_general(
        kinds, kinds, (((1,), (1,)), ((0,), (0,))), preferred_element_type=f32
    )
    stats_own = lax.dynamic_index_in_dim(precond_stats, own_kind, 1, keepdims=False)
    bases_own = lax.dynamic_index_in_dim(rotation_bases, own_kind, 1, keepdims=False)
    stats_own = SHAMPOO_BETA * stats_own + (1 - SHAMPOO_BETA) * (clip_factor * clip_factor) * stat
    far_stats = lax.ppermute(stats_own, "mp", flip_perm(4, 2))
    stats_own, head_own = lax.optimization_barrier((stats_own, head_own))
    far_head = lax.ppermute(head_own, "mp", flip_perm(4, 2))
    basis_own, late_clip, far_head = lax.optimization_barrier(
        (renew_bases(stats_own, bases_own), clip_factor, far_head)
    )
    head_g = gather_mats(head_own, far_head, across, core).transpose(1, 0, 2)
    head_g = head_g.reshape(head_rows, -1)
    new_head_w, new_head_m, new_head_v = adamw(
        head_w, late_clip * head_g, head_m, head_v, LR_HEAD, WEIGHT_DECAY
    )
    new_proto_w, new_proto_m, new_proto_v = adamw(
        proto_w, late_clip * proto_g, proto_m, proto_v, LR_PROTO, WEIGHT_DECAY
    )
    new_teacher_head = TEACHER_MOM * teacher_head + (1 - TEACHER_MOM) * new_head_w
    new_teacher_proto = TEACHER_MOM * teacher_proto + (1 - TEACHER_MOM) * new_proto_w
    beside = (
        new_head_w, new_head_m, new_head_v, new_proto_w, new_proto_m, new_proto_v,
        new_teacher_head, new_teacher_proto,
    )
    far_bases = lax.ppermute(basis_own, "mp", flip_perm(4, 2))
    far_stats, far_bases, beside = lax.optimization_barrier((far_stats, far_bases, beside))
    new_bases = gather_mats(basis_own, far_bases, across, core)
    new_stats = gather_mats(stats_own, far_stats, across, core).transpose(1, 0, 2, 3)
    (
        new_head_w, new_head_m, new_head_v, new_proto_w, new_proto_m, new_proto_v,
        new_teacher_head, new_teacher_proto,
    ) = beside
    new_bases = new_bases.transpose(1, 0, 2, 3)
    col_ids = dp_index * col_width + jnp.arange(col_width)
    col_masks = jnp.stack(
        [((col_ids >= bounds[k]) & (col_ids < bounds[k + 1])).astype(f32) for k in range(4)]
    )
    grad_cols = clip_factor * block_g
    rotated = jnp.einsum("lkde,lcd,kc->lec", new_bases, grad_cols, col_masks, precision=precise)
    first_mom = ROT_ONE * block_m[:, :, 0] + (1 - ROT_ONE) * rotated
    second_mom = ROT_TWO * block_v[:, :, 0] + (1 - ROT_TWO) * rotated * rotated
    direction = adam_direction(first_mom, second_mom, ROT_ONE, ROT_TWO)
    turned_back = jnp.einsum("lkde,lec,kc->ldc", new_bases, direction, col_masks, precision=precise)
    master = block_w[:, :, 0]
    new_block_w = (master - LR_BLOCK * (turned_back + WEIGHT_DECAY * master))[:, :, None]
    new_norm, new_norm_m, new_norm_v = adamw(
        norm_params, clip_factor * norm_total, norm_m, norm_v, LR_NORM, 0.0
    )
    new_teacher_block = TEACHER_MOM * teacher_block + (1 - TEACHER_MOM) * new_block_w
    new_teacher_norm = TEACHER_MOM * teacher_norm + (1 - TEACHER_MOM) * new_norm
    new_center = CENTER_MOM * center + (1 - CENTER_MOM) * center_total / (2.0 * images)
    return (
        loss_total, grad_norm[0, 0], new_block_w, first_mom[:, :, None], second_mom[:, :, None],
        new_bases, new_stats, new_head_w, new_head_m, new_head_v,
        new_proto_w, new_proto_m, new_proto_v, new_norm, new_norm_m, new_norm_v,
        new_teacher_block, new_teacher_head, new_teacher_proto, new_teacher_norm, new_center,
    )


def solution(mesh):
    block, head, proto, rep = P(None, None, "mp", "dp"), P("dp", None), P("dp", "mp"), P()
    in_specs = (
        P(None, ("dp", "mp"), None), P(None, "dp"), rep, block, block, block, rep, rep,
        head, head, head, proto, proto, proto, rep, rep, rep, block, head, proto, rep, P("mp"),
    )
    out_specs = (
        rep, rep, block, block, block, rep, rep, head, head, head, proto, proto, proto,
        rep, rep, rep, block, head, proto, rep, P("mp"),
    )
    return jax.shard_map(shards, mesh=mesh, in_specs=in_specs, out_specs=out_specs, check_vma=False)
```

```python
import functools

import jax
import jax.numpy as jnp
from jax import lax
from jax.experimental import pallas as pl
from jax.experimental.pallas import tpu as pltpu
from jax.sharding import PartitionSpec as P

D = 384
HD = 64
HID = 2048
LAYERS = 2
SLOT_DEV = 2
GLOBAL_TOK = 197
LOCAL_TOK = 37
MAX_LOCAL = 10
IMG_ROWS = 768
STEP = 10
MICRO = 2
CROPS = 12
GLOBAL_PAD = 200
LOCAL_PAD = 40
CHUNK = 400
CLS = 16

precise = lax.Precision.HIGHEST
TAU_S = 0.1
TAU_T = 0.07
CLIP_NORM = 0.005
BETA_ONE = 0.9
BETA_TWO = 0.999
ROT_ONE = 0.95
ROT_TWO = 0.95
SHAMPOO_BETA = 0.95
ADAM_EPS = 1e-08
WEIGHT_DECAY = 0.04
LR_BLOCK = 0.05
LR_HEAD = 0.03
LR_PROTO = 0.1
LR_NORM = 0.2
TEACHER_MOM = 0.7
CENTER_MOM = 0.9
NN = (((1,), (0,)), ((), ()))
NT = (((1,), (1,)), ((), ()))
TN = (((0,), (0,)), ((), ()))
bf16 = jnp.bfloat16
f32 = jnp.float32
VMEM_LIMIT = 58 * 1024 * 1024


def mm(lhs, rhs, dims=NN, precision=None):
    return lax.dot_general(lhs, rhs, dims, precision=precision, preferred_element_type=f32)


def normalize(inputs):
    centred = inputs - jnp.mean(inputs, axis=-1, keepdims=True)
    spread = jnp.mean(centred * centred, axis=-1, keepdims=True)
    inv = lax.rsqrt(spread + 1e-06)
    return centred * inv, inv


def norm_rows(inputs, gain, bias):
    return normalize(inputs)[0] * gain + bias


def norm_back(inputs, gain, grad_out):
    unit, inv = normalize(inputs)
    scaled = grad_out * gain
    grad = inv * (
        scaled
        - jnp.mean(scaled, axis=-1, keepdims=True)
        - unit * jnp.mean(scaled * unit, axis=-1, keepdims=True)
    )
    return (
        grad,
        jnp.sum(grad_out * unit, axis=0, keepdims=True),
        jnp.sum(grad_out, axis=0, keepdims=True),
    )


def gelu_cdf(inputs):
    return 0.5 + 0.5 * lax.erf(inputs * (0.5**0.5))


def gelu_exact(inputs):
    return inputs * gelu_cdf(inputs)


def gelu_slope(inputs):
    return gelu_cdf(inputs) + inputs * (jnp.exp(-0.5 * inputs * inputs) * 0.3989422804014327)


def low_half(shape):
    return lax.broadcasted_iota(jnp.int32, shape, 1) < HD


def halves(array):
    low = low_half(array.shape)
    zero = jnp.zeros_like(array)
    return jnp.where(low, array, zero), jnp.where(low, zero, array)


def block_fwd_kernel(
    x_ref, wt_ref, gains_ref, seg_col_ref, seg_row_ref, slot_ref,
    out_ref, h1_ref, qkv_ref, o_ref, x2_ref,
):
    x = x_ref[...]
    h1 = norm_rows(x, gains_ref[0:1], gains_ref[1:2]).astype(bf16)
    h1_ref[...] = h1
    allowed = seg_col_ref[0] == seg_row_ref[0]

    def heads(group, att):
        qkv = mm(h1, wt_ref[group, 0:384], NT).astype(bf16)
        qkv_ref[group] = qkv
        keys, values = qkv[:, 128:256], qkv[:, 256:384]
        mixes = []
        for query in halves(qkv[:, 0:128]):
            expd = jnp.where(allowed, jnp.exp(mm(query, keys, NT) * HD ** (-0.5)), 0.0)
            prob = expd / jnp.sum(expd, axis=-1, keepdims=True)
            mixes.append(mm(prob.astype(bf16), values))
        mix = jnp.where(low_half(mixes[0].shape), mixes[0], mixes[1])
        mix = (mix * slot_ref[group]).astype(bf16)
        o_ref[group] = mix
        return att + mm(mix, wt_ref[group, 384:512])

    att = lax.fori_loop(0, wt_ref.shape[0], heads, jnp.zeros(x.shape, f32))
    x2 = x + att
    x2_ref[...] = x2
    h2 = norm_rows(x2, gains_ref[2:3], gains_ref[3:4]).astype(bf16)

    def units(group, total):
        hidden = gelu_exact(mm(h2, wt_ref[group, 512:896], NT)).astype(bf16)
        return total + mm(hidden, wt_ref[group, 896:1280])

    out_ref[...] = x2 + lax.fori_loop(0, wt_ref.shape[0], units, jnp.zeros(x.shape, f32))


def mlp_bwd_kernel(last, wt_ref, gains_ref, x2_ref, grad_ref, *refs):
    if last:
        partial_ref, _, dwt_ref, dx2_ref, dgains_ref = refs
    else:
        dwt_ref, dx2_ref = refs

    @pl.when(pl.program_id(0) == 0)
    def _():
        dwt_ref[...] = jnp.zeros_like(dwt_ref)
        if last:
            dgains_ref[...] = jnp.zeros_like(dgains_ref)

    grad = grad_ref[...]
    grad_low = grad.astype(bf16)
    x2 = x2_ref[...]
    h2 = norm_rows(x2, gains_ref[2:3], gains_ref[3:4]).astype(bf16)

    def units(group, total):
        up = mm(h2, wt_ref[group, 512:896], NT)
        cdf = gelu_cdf(up)
        hidden = (up * cdf).astype(bf16)
        slope = cdf + up * (jnp.exp(-0.5 * up * up) * 0.3989422804014327)
        grad_up = (mm(grad_low, wt_ref[group, 896:1280], NT) * slope).astype(bf16)
        dwt_ref[group, 512:896] += mm(grad_up, h2, TN)
        dwt_ref[group, 896:1280] += mm(hidden, grad_low, TN)
        return total + mm(grad_up, wt_ref[group, 512:896])

    start = partial_ref[...] if last else jnp.zeros(grad.shape, f32)
    grad_h2 = lax.fori_loop(0, wt_ref.shape[0], units, start)
    if last:
        grad_x2, gain_two, bias_two = norm_back(x2, gains_ref[2:3], grad_h2)
        dx2_ref[...] = grad + grad_x2
        dgains_ref[...] += jnp.concatenate([gain_two, bias_two], axis=0)
    else:
        dx2_ref[...] = grad_h2


def attention_bwd_kernel(
    last, wt_ref, gains_ref, seg_col_ref, seg_row_ref, slot_ref, h1_ref, qkv_ref, o_ref, dx2_ref,
    *refs,
):
    if last:
        x_ref, partial_ref, _, dwt_ref, dgains_ref = refs
    else:
        _, dwt_ref, dh1_ref = refs

    @pl.when(pl.program_id(0) == 0)
    def _():
        dwt_ref[...] = jnp.zeros_like(dwt_ref)
        if last:
            dgains_ref[...] = jnp.zeros_like(dgains_ref)

    grad_att = dx2_ref[...].astype(bf16)
    allowed = seg_col_ref[0] == seg_row_ref[0]
    h1 = h1_ref[...]

    def heads(group, total):
        grad_mix = mm(grad_att, wt_ref[group, 384:512], NT).astype(bf16)
        grad_mix = grad_mix * slot_ref[group].astype(bf16)
        dwt_ref[group, 384:512] += mm(o_ref[group], grad_att, TN)
        qkv = qkv_ref[group]
        keys, values = qkv[:, 128:256], qkv[:, 256:384]
        grad_values = jnp.zeros(values.shape, f32)
        grad_keys = jnp.zeros(values.shape, f32)
        grad_queries = []
        for query, gmix in zip(halves(qkv[:, 0:128]), halves(grad_mix)):
            expd = jnp.where(allowed, jnp.exp(mm(query, keys, NT) * HD ** (-0.5)), 0.0)
            prob = expd * (1.0 / jnp.sum(expd, axis=-1, keepdims=True))
            grad_values = grad_values + mm(prob.astype(bf16), gmix, TN)
            grad_prob = mm(gmix, values, NT)
            scored = prob * (grad_prob - jnp.sum(prob * grad_prob, axis=-1, keepdims=True))
            scored = scored.astype(bf16)
            grad_queries.append(mm(scored, keys))
            grad_keys = grad_keys + mm(scored, query, TN)
        low = low_half(grad_queries[0].shape)
        grad_query = jnp.where(low, grad_queries[0], grad_queries[1]) * HD ** (-0.5)
        grad_qkv = jnp.concatenate(
            [grad_query.astype(bf16), (grad_keys * HD ** (-0.5)).astype(bf16), grad_values.astype(bf16)],
            axis=1,
        )
        dwt_ref[group, 0:384] += mm(grad_qkv, h1, TN)
        return total + mm(grad_qkv, wt_ref[group, 0:384])

    start = partial_ref[...] if last else jnp.zeros(h1.shape, f32)
    grad_h1 = lax.fori_loop(0, wt_ref.shape[0], heads, start)
    if last:
        _, gain_one, bias_one = norm_back(x_ref[...], gains_ref[0:1], grad_h1)
        dgains_ref[...] += jnp.concatenate([gain_one, bias_one], axis=0)
    else:
        dh1_ref[...] = grad_h1


def whole_spec(shape):
    return pl.BlockSpec(shape, lambda *_: (0,) * len(shape))


def block_specs(groups, layer):
    row = pl.BlockSpec((CHUNK, D), lambda c: (c, 0))
    return dict(
        row=row,
        wt=pl.BlockSpec((groups, 1280, D), lambda c: (0, 0, layer)),
        gains=whole_spec((4, D)),
        seg_col=pl.BlockSpec((1, CHUNK, 1), lambda c: (c, 0, 0)),
        seg_row=pl.BlockSpec((1, 1, CHUNK), lambda c: (c, 0, 0)),
        slot=whole_spec((groups, 1, 128)),
        qkv=pl.BlockSpec((groups, CHUNK, 384), lambda c: (0, c, 0)),
        mix=pl.BlockSpec((groups, CHUNK, 128), lambda c: (0, c, 0)),
    )


def block_fwd(x, weights, layer, gains, seg_col, seg_row, slot):
    rows, groups = x.shape[0], weights.shape[0]
    s = block_specs(groups, layer)
    return pl.pallas_call(
        block_fwd_kernel,
        grid=(rows // CHUNK,),
        in_specs=[s["row"], s["wt"], s["gains"], s["seg_col"], s["seg_row"], s["slot"]],
        out_specs=[s["row"], s["row"], s["qkv"], s["mix"], s["row"]],
        out_shape=[
            jax.ShapeDtypeStruct((rows, D), f32),
            jax.ShapeDtypeStruct((rows, D), bf16),
            jax.ShapeDtypeStruct((groups, rows, 384), bf16),
            jax.ShapeDtypeStruct((groups, rows, 128), bf16),
            jax.ShapeDtypeStruct((rows, D), f32),
        ],
        compiler_params=pltpu.CompilerParams(vmem_limit_bytes=VMEM_LIMIT),
        cost_estimate=pl.CostEstimate(
            flops=rows * 30_000_000, bytes_accessed=8_000_000, transcendentals=rows * 4000
        ),
    )(x, weights, gains, seg_col, seg_row, slot)


def mlp_bwd(part, weights, layer, gains, x2, grad, last=()):
    rows, groups = x2.shape[0], weights.shape[0] // 2
    s = block_specs(groups, layer)
    half = pl.BlockSpec((groups, 1280, D), lambda c: (part, 0, layer))
    any_spec = [pl.BlockSpec(memory_space=pl.ANY)] if last else []
    args = (weights, gains, x2, grad, *last)
    return pl.pallas_call(
        functools.partial(mlp_bwd_kernel, bool(last)),
        grid=(rows // CHUNK,),
        in_specs=[half, s["gains"], s["row"], s["row"]] + [s["row"]] * len(last[:1]) + any_spec,
        out_specs=[pl.BlockSpec((groups, 1280, D), lambda c: (part, 0, 0)), s["row"]]
        + [whole_spec((2, D))] * len(last[:1]),
        out_shape=[
            jax.ShapeDtypeStruct((2 * groups, 1280, D), f32),
            jax.ShapeDtypeStruct((rows, D), f32),
        ]
        + [jax.ShapeDtypeStruct((2, D), f32)] * len(last[:1]),
        input_output_aliases={len(args) - 1: 0} if last else {},
        compiler_params=pltpu.CompilerParams(vmem_limit_bytes=VMEM_LIMIT),
        cost_estimate=pl.CostEstimate(
            flops=rows * 13_000_000, bytes_accessed=8_000_000, transcendentals=rows * 3000
        ),
    )(*args)


def attention_bwd(part, weights, layer, gains, seg_col, seg_row, slot, saved, grad_x2, dwt, last=()):
    h1, qkv, mix, _ = saved
    rows, groups = h1.shape[0], weights.shape[0] // 2
    s = block_specs(groups, layer)
    heads = pl.BlockSpec((groups, 512, D), lambda c: (part, 0, 0))
    in_specs = [
        pl.BlockSpec((groups, 512, D), lambda c: (part, 0, layer)),
        s["gains"], s["seg_col"], s["seg_row"],
        pl.BlockSpec((groups, 1, 128), lambda c: (part, 0, 0)),
        s["row"],
        pl.BlockSpec((groups, CHUNK, 384), lambda c: (part, c, 0)),
        pl.BlockSpec((groups, CHUNK, 128), lambda c: (part, c, 0)),
        s["row"],
    ] + [s["row"]] * len(last)
    args = (weights, gains, seg_col, seg_row, slot, h1, qkv, mix, grad_x2, *last, dwt)
    return pl.pallas_call(
        functools.partial(attention_bwd_kernel, bool(last)),
        grid=(rows // CHUNK,),
        in_specs=in_specs + [pl.BlockSpec(memory_space=pl.ANY)],
        out_specs=[heads, whole_spec((2, D)) if last else s["row"]],
        out_shape=[
            jax.ShapeDtypeStruct(dwt.shape, f32),
            jax.ShapeDtypeStruct((2, D) if last else (rows, D), f32),
        ],
        input_output_aliases={len(args) - 1: 0},
        compiler_params=pltpu.CompilerParams(vmem_limit_bytes=VMEM_LIMIT),
        cost_estimate=pl.CostEstimate(
            flops=rows * 19_000_000, bytes_accessed=8_000_000, transcendentals=rows * 3000
        ),
    )(*args)


def crop_starts(crops):
    return [
        crop * GLOBAL_PAD if crop < 2 else 2 * GLOBAL_PAD + (crop - 2) * LOCAL_PAD
        for crop in range(crops)
    ]


def take_cls(ref, crops):
    rows = [ref[start : start + 1, :] for start in crop_starts(crops)]
    return jnp.concatenate(rows + [jnp.zeros((CLS - crops, ref.shape[1]), f32)], axis=0)


def last_fwd_kernel(
    crops, x_ref, wt_ref, gains_ref, seg_cls_ref, seg_row_ref, slot_ref,
    out_ref, h1_ref, kv_ref, q_ref, o_ref, x2_ref,
):
    gain, bias = gains_ref[0:1], gains_ref[1:2]
    h1 = norm_rows(x_ref[...], gain, bias).astype(bf16)
    h1_ref[...] = h1
    x_cls = take_cls(x_ref, crops)
    h1_cls = norm_rows(x_cls, gain, bias).astype(bf16)
    allowed = seg_cls_ref[...] == seg_row_ref[...]

    def heads(group, att):
        kv = mm(h1, wt_ref[group, 128:384], NT).astype(bf16)
        kv_ref[group] = kv
        query = mm(h1_cls, wt_ref[group, 0:128], NT).astype(bf16)
        q_ref[group] = query
        both = jnp.concatenate(halves(query), axis=0)
        scores = mm(both, kv[:, 0:128], NT) * HD ** (-0.5)
        expd = jnp.where(allowed, jnp.exp(scores), 0.0)
        prob = expd / jnp.sum(expd, axis=-1, keepdims=True)
        mix = mm(prob.astype(bf16), kv[:, 128:256])
        mix = jnp.where(low_half((CLS, 128)), mix[0:CLS], mix[CLS:])
        mix = (mix * slot_ref[group]).astype(bf16)
        o_ref[group] = mix
        return att + mm(mix, wt_ref[group, 384:512])

    att = lax.fori_loop(0, wt_ref.shape[0], heads, jnp.zeros((CLS, D), f32))
    x2 = x_cls + att
    x2_ref[...] = x2
    h2 = norm_rows(x2, gains_ref[2:3], gains_ref[3:4]).astype(bf16)

    def units(group, total):
        hidden = gelu_exact(mm(h2, wt_ref[group, 512:896], NT)).astype(bf16)
        return total + mm(hidden, wt_ref[group, 896:1280])

    out_ref[...] = x2 + lax.fori_loop(0, wt_ref.shape[0], units, jnp.zeros((CLS, D), f32))


def last_bwd_kernel(
    crops, x_ref, wt_ref, gains_ref, seg_cls_ref, seg_row_ref, slot_ref,
    h1_ref, kv_ref, q_ref, o_ref, x2_ref, grad_ref,
    dwt_ref, dgains_ref, dx_ref,
):
    grad = grad_ref[...]
    grad_low = grad.astype(bf16)
    x2 = x2_ref[...]
    h2 = norm_rows(x2, gains_ref[2:3], gains_ref[3:4]).astype(bf16)
    groups = wt_ref.shape[0]

    def units(group, total):
        up = mm(h2, wt_ref[group, 512:896], NT)
        hidden = gelu_exact(up).astype(bf16)
        grad_up = (mm(grad_low, wt_ref[group, 896:1280], NT) * gelu_slope(up)).astype(bf16)
        dwt_ref[group, 512:896] = mm(grad_up, h2, TN)
        dwt_ref[group, 896:1280] = mm(hidden, grad_low, TN)
        return total + mm(grad_up, wt_ref[group, 512:896])

    grad_h2 = lax.fori_loop(0, groups, units, jnp.zeros((CLS, D), f32))
    grad_x2, gain_two, bias_two = norm_back(x2, gains_ref[2:3], grad_h2)
    grad_x2 = grad + grad_x2
    grad_att = grad_x2.astype(bf16)
    allowed = seg_cls_ref[...] == seg_row_ref[...]
    h1 = h1_ref[...]
    h1_cls = norm_rows(take_cls(x_ref, crops), gains_ref[0:1], gains_ref[1:2]).astype(bf16)

    def heads(group, carry):
        total, total_cls = carry
        grad_mix = mm(grad_att, wt_ref[group, 384:512], NT).astype(bf16)
        grad_mix = grad_mix * slot_ref[group].astype(bf16)
        dwt_ref[group, 384:512] = mm(o_ref[group], grad_att, TN)
        kv = kv_ref[group]
        keys, values = kv[:, 0:128], kv[:, 128:256]
        both = jnp.concatenate(halves(q_ref[group]), axis=0)
        gboth = jnp.concatenate(halves(grad_mix), axis=0)
        expd = jnp.where(allowed, jnp.exp(mm(both, keys, NT) * HD ** (-0.5)), 0.0)
        prob = expd / jnp.sum(expd, axis=-1, keepdims=True)
        grad_prob = mm(gboth, values, NT)
        scored = prob * (grad_prob - jnp.sum(prob * grad_prob, axis=-1, keepdims=True))
        scored = scored.astype(bf16)
        grad_values = mm(prob.astype(bf16), gboth, TN)
        grad_keys = mm(scored, both, TN) * HD ** (-0.5)
        grad_query = mm(scored, keys)
        low = low_half((CLS, 128))
        grad_query = jnp.where(low, grad_query[0:CLS], grad_query[CLS:]) * HD ** (-0.5)
        grad_query = grad_query.astype(bf16)
        grad_kv = jnp.concatenate([grad_keys.astype(bf16), grad_values.astype(bf16)], axis=1)
        dwt_ref[group, 0:128] = mm(grad_query, h1_cls, TN)
        dwt_ref[group, 128:384] = mm(grad_kv, h1, TN)
        return (
            total + mm(grad_kv, wt_ref[group, 128:384]),
            total_cls + mm(grad_query, wt_ref[group, 0:128]),
        )

    grad_h1, grad_cls = lax.fori_loop(
        0, groups, heads, (jnp.zeros(h1.shape, f32), jnp.zeros((CLS, D), f32))
    )
    dx_ref[...] = grad_h1
    starts = crop_starts(crops)
    for crop, start in enumerate(starts):
        dx_ref[start : start + 1, :] += grad_cls[crop : crop + 1, :]
    grad_x, gain_one, bias_one = norm_back(x_ref[...], gains_ref[0:1], dx_ref[...])
    dx_ref[...] = grad_x
    for crop, start in enumerate(starts):
        dx_ref[start : start + 1, :] += grad_x2[crop : crop + 1, :]
    dgains_ref[...] = jnp.concatenate([gain_one, bias_one, gain_two, bias_two], axis=0)


def last_in_specs(rows, groups, layer):
    return [
        whole_spec((rows, D)),
        pl.BlockSpec((groups, 1280, D), lambda i: (0, 0, layer)),
        whole_spec((4, D)),
        whole_spec((2 * CLS, 1)),
        whole_spec((1, rows)),
        whole_spec((groups, 1, 128)),
    ]


def last_saved(rows, groups):
    return [
        jax.ShapeDtypeStruct((rows, D), bf16),
        jax.ShapeDtypeStruct((groups, rows, 256), bf16),
        jax.ShapeDtypeStruct((groups, CLS, 128), bf16),
        jax.ShapeDtypeStruct((groups, CLS, 128), bf16),
        jax.ShapeDtypeStruct((CLS, D), f32),
    ]


def last_fwd(crops, x, weights, layer, gains, seg_cls, seg_row, slot):
    rows, groups = x.shape[0], weights.shape[0]
    out_shape = [jax.ShapeDtypeStruct((CLS, D), f32)] + last_saved(rows, groups)
    return pl.pallas_call(
        functools.partial(last_fwd_kernel, crops),
        grid=(1,),
        in_specs=last_in_specs(rows, groups, layer),
        out_specs=[whole_spec(a.shape) for a in out_shape],
        out_shape=out_shape,
        compiler_params=pltpu.CompilerParams(vmem_limit_bytes=VMEM_LIMIT),
        cost_estimate=pl.CostEstimate(
            flops=rows * 15_000_000, bytes_accessed=8_000_000, transcendentals=rows * 200
        ),
    )(x, weights, gains, seg_cls, seg_row, slot)


def last_bwd(crops, x, weights, layer, gains, seg_cls, seg_row, slot, saved, grad):
    rows, groups = x.shape[0], weights.shape[0]
    out_shape = [
        jax.ShapeDtypeStruct((groups, 1280, D), f32),
        jax.ShapeDtypeStruct((4, D), f32),
        jax.ShapeDtypeStruct((rows, D), f32),
    ]
    return pl.pallas_call(
        functools.partial(last_bwd_kernel, crops),
        grid=(1,),
        in_specs=last_in_specs(rows, groups, layer)
        + [whole_spec(a.shape) for a in last_saved(rows, groups)]
        + [whole_spec((CLS, D))],
        out_specs=[whole_spec(a.shape) for a in out_shape],
        out_shape=out_shape,
        compiler_params=pltpu.CompilerParams(vmem_limit_bytes=VMEM_LIMIT),
        cost_estimate=pl.CostEstimate(
            flops=rows * 20_000_000, bytes_accessed=16_000_000, transcendentals=rows * 400
        ),
    )(x, weights, gains, seg_cls, seg_row, slot, *saved, grad)


PANEL = 32


def panel_steps(panels):
    lanes = lax.broadcasted_iota(jnp.int32, (PANEL, 128), 1)
    ids = lax.broadcasted_iota(jnp.int32, (PANEL, 1), 0)
    panels = list(panels)
    pivots = [jnp.zeros((PANEL, 1), f32) for _ in panels]
    for step in range(PANEL):
        here = lanes == step
        for i, panel in enumerate(panels):
            row = panel[step : step + 1]
            pivot = row[:, step : step + 1]
            column = jnp.where(ids > step, panel[:, step : step + 1], 0.0)
            source = jnp.where(here[0:1], 1.0, row) * (1.0 / pivot)
            cleared = jnp.where(here & (ids > step), 0.0, panel)
            panels[i] = cleared - column * source
            pivots[i] = jnp.where(ids == step, pivot, pivots[i])
    return panels, pivots


def basis_kernel(stats_ref, bases_ref, out_ref, gram_ref, inverse_ref):
    mats = stats_ref.shape[0]
    lanes = lax.broadcasted_iota(jnp.int32, (128, 128), 1)
    rows = lax.broadcasted_iota(jnp.int32, (128, 128), 0)
    near_lanes, near_rows = lanes[:PANEL], rows[:PANEL]
    for mat in range(mats):
        out_ref[mat] = mm(stats_ref[mat], bases_ref[mat], precision=precise)
    for block in range(D // 128):
        low, high = block * 128, block * 128 + 128
        for mat in range(mats):
            part = out_ref[mat, :, low:high]
            gram_ref[mat] = mm(part, part, TN, precise)

        def panels(index, carry):
            first = pl.multiple_of(index * PANEL, PANEL)
            last = first + PANEL
            started = [
                pltpu.roll(gram_ref[mat, pl.ds(first, PANEL), :], 128 - first, 1)
                for mat in range(mats)
            ]
            for mat, (panel, pivots) in enumerate(zip(*panel_steps(started))):
                panel = pltpu.roll(panel, first, 1)
                own = near_lanes - first
                unit = jnp.where(own < near_rows, panel, jnp.where(own == near_rows, 1.0, 0.0))
                inverse_ref[mat, pl.ds(first, PANEL), :] = unit * lax.rsqrt(pivots)
                source = jnp.where(near_lanes < last, unit, panel)
                factors = jnp.where(near_lanes < last, 0.0, panel / pivots)
                gram = gram_ref[mat]
                gram = jnp.where((lanes >= first) & (lanes < last) & (rows >= last), 0.0, gram)
                gram_ref[mat] = gram - mm(factors, source, TN, precise)
            return carry

        lax.fori_loop(0, 128 // PANEL, panels, 0)
        for mat in range(mats):
            part = mm(out_ref[mat, :, low:high], inverse_ref[mat], NT, precise)
            out_ref[mat, :, low:high] = part
            if high < D:
                rest = out_ref[mat, :, high:]
                cross = mm(part, rest, TN, precise)
                out_ref[mat, :, high:] = rest - mm(part, cross, NN, precise)


def renew_bases(new_stats, bases):
    mats = new_stats.shape[0]
    return pl.pallas_call(
        basis_kernel,
        in_specs=[pl.BlockSpec(memory_space=pltpu.VMEM)] * 2,
        out_specs=pl.BlockSpec(memory_space=pltpu.VMEM),
        out_shape=jax.ShapeDtypeStruct((mats, D, D), f32),
        scratch_shapes=[pltpu.VMEM((mats, 128, 128), f32), pltpu.VMEM((mats, 128, 128), f32)],
        compiler_params=pltpu.CompilerParams(vmem_limit_bytes=VMEM_LIMIT),
        cost_estimate=pl.CostEstimate(
            flops=60_000_000_000, bytes_accessed=6_000_000, transcendentals=1000
        ),
    )(new_stats, bases)


def crop_pairs(r_t, r_s):
    rows = lax.broadcasted_iota(jnp.int32, (r_t, r_s), 0)
    crops = lax.broadcasted_iota(jnp.int32, (r_t, r_s), 1)
    first = (rows // 2) * CROPS
    return (crops >= first) & (crops < first + CROPS), rows % 2 == 0


def spread_pairs(values, same, even):
    first = jnp.where(same & even, 1.0, 0.0)
    second = jnp.where(same & ~even, 1.0, 0.0)
    return mm(values, first, NN, precise), mm(values, second, NN, precise)


def logits_kernel(
    zs_ref, zt_ref, ps_ref, pt_ref, center_ref, exp_s_ref, exp_t_ref, stats_ref, part_ref
):
    scaled_s = mm(ps_ref[...], zs_ref[...], (((0,), (1,)), ((), ()))) / TAU_S
    glob = mm(pt_ref[...], zt_ref[...], (((0,), (1,)), ((), ())))
    part_ref[...] = jnp.sum(glob, axis=1, keepdims=True)
    scaled_t = (glob - center_ref[...]) / TAU_T
    max_s = jnp.max(scaled_s, axis=0, keepdims=True)
    max_t = jnp.max(scaled_t, axis=0, keepdims=True)
    exp_s = jnp.exp(scaled_s - max_s)
    exp_t = jnp.exp(scaled_t - max_t)
    exp_s_ref[...] = exp_s
    exp_t_ref[...] = exp_t
    same, even = crop_pairs(exp_t.shape[1], exp_s.shape[1])
    cross = jnp.where(same, mm(exp_t, scaled_s, TN, precise), 0.0)
    stats_ref[...] = jnp.concatenate(
        [
            max_s,
            jnp.sum(exp_s, axis=0, keepdims=True),
            *spread_pairs(max_t, same, even),
            *spread_pairs(jnp.sum(exp_t, axis=0, keepdims=True), same, even),
            jnp.sum(jnp.where(even, cross, 0.0), axis=0, keepdims=True),
            jnp.sum(jnp.where(even, 0.0, cross), axis=0, keepdims=True),
        ],
        axis=0,
    )


def prototype_logits(z_s, z_t, proto_s, proto_t, center):
    cols, r_s, r_t = proto_s.shape[1], z_s.shape[0], z_t.shape[0]
    return pl.pallas_call(
        logits_kernel,
        in_specs=[pl.BlockSpec(memory_space=pltpu.VMEM)] * 5,
        out_specs=[pl.BlockSpec(memory_space=pltpu.VMEM)] * 4,
        out_shape=[
            jax.ShapeDtypeStruct((cols, r_s), f32),
            jax.ShapeDtypeStruct((cols, r_t), f32),
            jax.ShapeDtypeStruct((8, r_s), f32),
            jax.ShapeDtypeStruct((cols, 1), f32),
        ],
        compiler_params=pltpu.CompilerParams(vmem_limit_bytes=VMEM_LIMIT),
        cost_estimate=pl.CostEstimate(
            flops=8_000_000_000, bytes_accessed=8_000_000, transcendentals=1_000_000
        ),
    )(z_s, z_t, proto_s, proto_t, center)


def join_stats(every):
    tops = jnp.max(every, axis=0)

    def add_up(row, shrink):
        return jnp.sum(every[:, row : row + 1] * shrink, axis=0)

    shrink = [jnp.exp(every[:, row : row + 1] - tops[row : row + 1][None]) for row in (0, 2, 3)]
    sums = [add_up(4, shrink[1]), add_up(5, shrink[2]), add_up(6, shrink[1]), add_up(7, shrink[2])]
    return jnp.concatenate([tops[0:1], add_up(1, shrink[0]), tops[2:4], *sums], axis=0)


def loss_kernel(
    all_ref, own_ref, weight_ref, exp_s_ref, exp_t_ref, zs_ref, ps_ref, dz_ref, dproto_ref, loss_ref
):
    every, own = all_ref[...], own_ref[...]
    every = join_stats(every) if every.ndim == 3 else every
    top_s, total_s, top_0, top_1 = every[0:1], every[1:2], every[2:3], every[3:4]
    total_0, total_1, cross_0, cross_1 = every[4:5], every[5:6], every[6:7], every[7:8]
    weight_0, weight_1 = weight_ref[0:1], weight_ref[1:2]
    log_norm = jnp.log(total_s) + top_s
    loss = weight_0 * (log_norm - cross_0 / total_0) + weight_1 * (log_norm - cross_1 / total_1)
    loss_ref[...] = jnp.broadcast_to(jnp.sum(loss, axis=1, keepdims=True), loss_ref.shape)
    coef_s = (weight_0 + weight_1) / total_s * jnp.exp(own[0:1] - top_s)
    coef_0 = weight_0 / total_0 * jnp.exp(own[2:3] - top_0)
    coef_1 = weight_1 / total_1 * jnp.exp(own[3:4] - top_1)
    same, even = crop_pairs(exp_t_ref.shape[1], exp_s_ref.shape[1])
    mix = jnp.where(same, jnp.where(even, coef_0, coef_1), 0.0)
    target = mm(exp_t_ref[...], mix, NN, precise)
    grad = ((coef_s * exp_s_ref[...] - target) / TAU_S).astype(bf16)
    dz_ref[...] = mm(grad, ps_ref[...], (((0,), (1,)), ((), ())))
    dproto_ref[...] = mm(zs_ref[...], grad, (((0,), (1,)), ((), ())))


def loss_and_grads(every, own, weights, exp_s, exp_t, z_s, proto_s):
    return pl.pallas_call(
        loss_kernel,
        in_specs=[pl.BlockSpec(memory_space=pltpu.VMEM)] * 7,
        out_specs=[pl.BlockSpec(memory_space=pltpu.VMEM)] * 3,
        out_shape=[
            jax.ShapeDtypeStruct(z_s.shape, f32),
            jax.ShapeDtypeStruct(proto_s.shape, f32),
            jax.ShapeDtypeStruct((1, 128), f32),
        ],
        compiler_params=pltpu.CompilerParams(vmem_limit_bytes=VMEM_LIMIT),
        cost_estimate=pl.CostEstimate(
            flops=8_000_000_000, bytes_accessed=8_000_000, transcendentals=10_000
        ),
    )(every, own, weights, exp_s, exp_t, z_s, proto_s)


def flip_perm(count, bit):
    return [(i, i ^ bit) for i in range(count)]


def flips(axis):
    count = lax.axis_size(axis)
    bits, bit = [], 1
    while bit < count:
        bits.append(bit)
        bit *= 2
    return count, bits


def thirds(array):
    high = lax.optimization_barrier(array.astype(bf16))
    rest = array - high.astype(f32)
    middle = lax.optimization_barrier(rest.astype(bf16))
    return jnp.stack([high, middle, (rest - middle.astype(f32)).astype(bf16)])


def whole_of(parts):
    layers, count = parts.shape[:2]
    parts = parts.transpose(1, 0, 2, 3).reshape(count, 3, -1, parts.shape[-1]).astype(f32)
    return jnp.sum(parts[:, 0] + (parts[:, 1] + parts[:, 2]), axis=0)


def sum_over(array, axes):
    for axis in axes:
        count, bits = flips(axis)
        for bit in bits:
            array = array + lax.ppermute(array, axis, flip_perm(count, bit))
    return array


def shift_perm(count, step):
    return [(i, (i + step) % count) for i in range(count)]


def gather_over(array, axis):
    count = lax.axis_size(axis)
    if lax.axis_size("dp") > 8:
        return lax.all_gather(array, axis, axis=0)
    return lax.all_to_all(jnp.broadcast_to(array[None], (count, *array.shape)), axis, 0, 0)


def swap_pieces(pick, after=None):
    count = lax.axis_size("dp")
    me = lax.axis_index("dp")
    if count > 8:
        return [lax.all_to_all(jnp.stack([pick(i) for i in range(count)]), "dp", 0, 0)]
    picks = [pick(lax.rem(me + step, count)) for step in range(1, count)]
    if after is not None:
        picks, _ = lax.optimization_barrier((picks, after))
    got = [
        lax.ppermute(piece, "dp", shift_perm(count, step + 1)) for step, piece in enumerate(picks)
    ]
    return [pick(me), *got]


def swap_joined(pieces):
    if len(pieces) == 1:
        return pieces[0]
    count = lax.axis_size("dp")
    out = jnp.zeros((count, *pieces[0].shape), pieces[0].dtype)
    for step, piece in enumerate(pieces):
        out = put(out, piece, lax.rem(lax.axis_index("dp") + (count - step), count))
    return out


RING = (0, 2, 4, 6, 7, 5, 3, 1)


def unsigned(index):
    return lax.convert_element_type(index, jnp.uint32)


def put(out, piece, index):
    return lax.dynamic_update_index_in_dim(out, piece, unsigned(index), 0)


def ring_at(offset):
    count = len(RING)
    table = [RING[(RING.index(i) + offset) % count] for i in range(count)]
    return lax.dynamic_slice(
        jnp.array(table, jnp.uint32), (lax.axis_index("dp").astype(jnp.uint32),), (1,)
    )[0]


def ring_perm(step):
    count = len(RING)
    return [(RING[i], RING[(i + step) % count]) for i in range(count)]


def ring_gather(piece):
    count = lax.axis_size("dp")
    if count != len(RING):
        return lax.all_gather(piece, "dp", axis=0)
    out = put(jnp.zeros((count, *piece.shape), piece.dtype), piece, lax.axis_index("dp"))
    right = left = piece
    for step in range(1, count // 2):
        right = lax.ppermute(right, "dp", ring_perm(1))
        left = lax.ppermute(left, "dp", ring_perm(-1))
        out = put(out, right, ring_at(-step))
        out = put(out, left, ring_at(step))
    half = piece.shape[-2] // 2
    right = lax.ppermute(right[..., :half, :], "dp", ring_perm(1))
    left = lax.ppermute(left[..., half:, :], "dp", ring_perm(-1))
    return put(out, jnp.concatenate([right, left], axis=-2), ring_at(count // 2))


class RingScatter:
    steps = len(RING) // 2

    def __init__(self, parts):
        self.parts = parts
        self.ringed = lax.axis_size("dp") == len(RING)
        self.right = self.left = None
        if self.ringed:
            far = self.own(self.steps)
            self.send_right, self.send_left = far[0:1], far[1:2]

    def own(self, offset):
        return lax.dynamic_index_in_dim(self.parts, ring_at(offset), 1, keepdims=False)

    def step(self, index):
        if not self.ringed:
            return
        if index > 0:
            right, left = self.own(self.steps - index), self.own(index - self.steps)
            if index == 1:
                right = jnp.concatenate([right[0:1] + self.right, right[1:2]])
                left = jnp.concatenate([left[0:1], left[1:2] + self.left])
            else:
                right, left = right + self.right, left + self.left
            self.send_right, self.send_left = right, left
        self.right = lax.ppermute(self.send_right, "dp", ring_perm(1))
        self.left = lax.ppermute(self.send_left, "dp", ring_perm(-1))

    def tie(self, other):
        if self.ringed:
            other, self.right, self.left = lax.optimization_barrier((other, self.right, self.left))
        return other

    def total(self):
        if not self.ringed:
            return lax.psum_scatter(self.parts, "dp", scatter_dimension=1, tiled=True)[:, 0]
        return self.own(0) + self.right + self.left


def core_halves(grad, dp_count, core):
    parts = grad.reshape(2, 2, dp_count, -1, D)
    send = lax.dynamic_index_in_dim(parts, unsigned(1 - core), 1, keepdims=False)
    return send, lax.dynamic_index_in_dim(parts, unsigned(core), 1, keepdims=False)


def across_sum(parts, across):
    send = lax.dynamic_index_in_dim(parts, unsigned(1 - across), 0, keepdims=False)
    own = lax.dynamic_index_in_dim(parts, unsigned(across), 0, keepdims=False)
    return own + lax.ppermute(send, "mp", flip_perm(4, 2))


def gather_mats(own, far, across, core):
    pair = put(jnp.stack([own, own]), far, 1 - across)
    other = lax.ppermute(pair, "mp", flip_perm(4, 1))
    whole = jnp.zeros((2, 2, *own.shape), own.dtype)
    whole = lax.dynamic_update_index_in_dim(whole, pair, unsigned(core), 1)
    whole = lax.dynamic_update_index_in_dim(whole, other, unsigned(1 - core), 1)
    return whole.reshape(4, *own.shape)


def adam_direction(first_mom, second_mom, beta_one, beta_two):
    return (
        first_mom / (1 - beta_one**STEP) / (jnp.sqrt(second_mom / (1 - beta_two**STEP)) + ADAM_EPS)
    )


def adamw(weight, grad_in, first_mom, second_mom, rate, decay):
    first_mom = BETA_ONE * first_mom + (1 - BETA_ONE) * grad_in
    second_mom = BETA_TWO * second_mom + (1 - BETA_TWO) * grad_in * grad_in
    weight = weight - rate * (
        adam_direction(first_mom, second_mom, BETA_ONE, BETA_TWO) + decay * weight
    )
    return (weight, first_mom, second_mom)


def row_layout(crop_count):
    rows = jnp.arange(2 * CHUNK)
    is_global = rows < 2 * GLOBAL_PAD
    local = rows - 2 * GLOBAL_PAD
    crop = jnp.where(is_global, rows // GLOBAL_PAD, 2 + local // LOCAL_PAD)
    offset = jnp.where(is_global, rows % GLOBAL_PAD, local % LOCAL_PAD)
    real = offset < jnp.where(is_global, GLOBAL_TOK, LOCAL_TOK)
    source = jnp.where(
        is_global, crop * GLOBAL_TOK + offset, 2 * GLOBAL_TOK + (crop - 2) * LOCAL_TOK + offset
    )
    source = jnp.where(real, source, -1)
    segment = jnp.where(real & (crop < 2 + crop_count), crop, 1000 + rows)
    return source, segment.astype(jnp.int32)


def shards(
    tokens, crop_counts, slot_live, block_w, block_m, block_v, rotation_bases, precond_stats,
    head_w, head_m, head_v, proto_w, proto_m, proto_v, norm_params, norm_m, norm_v,
    teacher_block, teacher_head, teacher_proto, teacher_norm, center,
):
    mp_index = lax.axis_index("mp")
    dp_index = lax.axis_index("dp")
    mp_count = lax.axis_size("mp")
    dp_count = lax.axis_size("dp")
    col_width = block_w.shape[3]
    micro, place = mp_index % MICRO, mp_index // MICRO
    crop_count = crop_counts[micro, place]
    across, core = mp_index // 2, mp_index % 2
    own_t = [teacher_block[layer, :, 0].astype(bf16).T for layer in range(LAYERS)]
    own_s = [block_w[layer, :, 0].astype(bf16).T for layer in range(LAYERS)]
    weights = lax.all_gather(
        jnp.concatenate([*own_t, *own_s], axis=1), ("mp", "dp"), axis=0, tiled=True
    ).reshape(mp_count, -1, 2 * LAYERS * D)
    head_cols = head_w.shape[1] // mp_count
    proto_cols = proto_w.shape[1] // dp_count
    heads = jnp.concatenate(
        [
            lax.dynamic_slice_in_dim(part, unsigned(mp_index * head_cols), head_cols, 1)
            for part in (teacher_head, head_w)
        ],
        axis=1,
    ).astype(bf16)

    def pick_cols(i):
        return jnp.stack(
            [
                lax.dynamic_slice_in_dim(part, unsigned(i * proto_cols), proto_cols, 1).astype(bf16)
                for part in (teacher_proto, proto_w)
            ]
        )

    counts_own = jnp.stack([crop_counts[i % MICRO, i // MICRO] for i in range(mp_count)])
    counts = gather_over(counts_own[None], "dp").reshape(-1)
    other = lax.ppermute(
        lax.dynamic_index_in_dim(tokens, 1 - micro, 0, keepdims=False), "mp", flip_perm(mp_count, 1)
    )
    mine = lax.dynamic_index_in_dim(tokens, micro, 0, keepdims=False)
    first = micro == 0
    image = jnp.concatenate([jnp.where(first, mine, other), jnp.where(first, other, mine)], axis=0)
    source, segment = row_layout(crop_count)
    spread = (source[:, None] == jnp.arange(IMG_ROWS)[None, :]).astype(bf16)
    x0 = mm(spread, image)
    seg_col, seg_row = segment.reshape(2, CHUNK, 1), segment.reshape(2, 1, CHUNK)
    starts = crop_starts(CROPS)
    seg_cls = jnp.concatenate([segment[jnp.array(starts)], jnp.zeros((CLS - CROPS,), jnp.int32)])
    seg_cls = jnp.concatenate([seg_cls, seg_cls])[:, None]
    slot = jnp.repeat(slot_live.astype(f32).reshape(mp_count, SLOT_DEV), HD, axis=1)[:, None, :]
    protos = swap_joined(swap_pieces(pick_cols))
    center_own = lax.dynamic_slice_in_dim(center, unsigned(dp_index * proto_cols), proto_cols)
    center_own = center_own[:, None]
    crop_ids = jnp.arange(CROPS)
    pair_weight = (
        (crop_ids[None, None, :] != jnp.arange(2)[:, None, None])
        & (crop_ids[None, None, :] < 2 + counts[None, :, None])
    ).astype(f32) / (2.0 * counts.astype(f32) + 2.0)[None, :, None]
    pair_weight = pair_weight.reshape(2, -1)
    x0, weights, heads, protos, seg_col, seg_row, seg_cls, slot, center_own, pair_weight = (
        lax.optimization_barrier(
            (x0, weights, heads, protos, seg_col, seg_row, seg_cls, slot, center_own, pair_weight)
        )
    )
    heads = lax.all_gather(heads, "dp", axis=0, tiled=True)
    head_t, head_s = heads[:, :head_cols], heads[:, head_cols:]
    protos = protos.transpose(1, 0, 2, 3).reshape(2, -1, proto_cols)
    proto_t, proto_s = protos[0], protos[1]
    x0_t = x0[:CHUNK]
    x1_t = block_fwd(x0_t, weights, 0, teacher_norm[0:4], seg_col, seg_row, slot)[0]
    x1, *saved0 = block_fwd(x0, weights, 2, norm_params[0:4], seg_col, seg_row, slot)
    y_t = last_fwd(
        2, x1_t, weights, 1, teacher_norm[4:8], seg_cls, segment[None, :CHUNK], slot
    )[0]
    y_s, *saved1 = last_fwd(
        CROPS, x1, weights, 3, norm_params[4:8], seg_cls, segment[None], slot
    )
    y_all = lax.all_gather(jnp.concatenate([y_s[:CROPS], y_t[:4]], axis=0), "mp", axis=0)
    cls_s = y_all[:, :CROPS].reshape(mp_count * CROPS, D)
    cls_t = y_all[:, CROPS : CROPS + 2].reshape(mp_count * 2, D)
    n_s, n_t = cls_s.shape[0], cls_t.shape[0]
    h1_s, h2_s, h3_s = head_s[:D], head_s[D : D + HID], head_s[D + HID :]
    h1_t, h2_t, h3_t = head_t[:D], head_t[D : D + HID], head_t[D + HID :]
    gain_s, bias_s = norm_params[8:9], norm_params[9:10]
    feats_s = norm_rows(cls_s, gain_s, bias_s).astype(bf16)
    feats_t = norm_rows(cls_t, teacher_norm[8:9], teacher_norm[9:10]).astype(bf16)
    a1_s, a1_t = mm(feats_s, h1_s), mm(feats_t, h1_t)
    b1_own = jnp.concatenate([gelu_exact(a1_s), gelu_exact(a1_t)], axis=0).astype(bf16)
    b1 = lax.all_gather(b1_own, "mp", axis=1, tiled=True)
    a2_s, a2_t = mm(b1[:n_s], h2_s), mm(b1[n_s:], h2_t)
    b2_s = gelu_exact(a2_s).astype(bf16)
    b2_t = gelu_exact(a2_t).astype(bf16)
    third = sum_over(jnp.concatenate([mm(b2_s, h3_s, NT), mm(b2_t, h3_t, NT)], axis=0), ("mp",))
    inv = lax.rsqrt(jnp.sum(third * third, axis=-1, keepdims=True) + 1e-06)
    unit = (third * inv).astype(bf16)
    unit_all = gather_over(unit, "dp")
    z_s = unit_all[:, :n_s].reshape(dp_count * n_s, -1)
    z_t = unit_all[:, n_s:].reshape(dp_count * n_t, -1)
    images = dp_count * mp_count
    exp_s, exp_t, own_stats, center_part = prototype_logits(z_s, z_t, proto_s, proto_t, center_own)
    center_part = center_part.reshape(-1)
    all_stats = gather_over(own_stats, ("dp", "mp"))
    if dp_count > 8:
        all_stats = join_stats(all_stats)
    grad_unit_part, grad_proto, loss_total = loss_and_grads(
        all_stats, own_stats, pair_weight, exp_s, exp_t, z_s, proto_s
    )
    loss_total = loss_total[0, 0]
    grad_unit = lax.all_to_all(grad_unit_part.reshape(dp_count, n_s, -1), "dp", 0, 0)
    grad_unit = sum_over(jnp.sum(grad_unit, axis=0), ("mp",))
    third_s, inv_s = third[:n_s], inv[:n_s]
    along = jnp.sum(grad_unit * third_s, axis=-1, keepdims=True)
    grad_third = (inv_s * grad_unit - third_s * (inv_s * inv_s * inv_s * along)).astype(bf16)
    grad_a2 = (mm(grad_third, h3_s) * gelu_slope(a2_s)).astype(bf16)
    grad_b1 = mm(grad_a2, h2_s, NT).reshape(n_s, mp_count, head_cols).transpose(1, 0, 2)
    grad_b1 = jnp.sum(lax.all_to_all(grad_b1, "mp", 0, 0), axis=0)
    grad_a1 = (grad_b1 * gelu_slope(a1_s)).astype(bf16)
    grad_feats = sum_over(mm(grad_a1, h1_s, NT), ("mp",))
    grad_cls, head_gain, head_bias = norm_back(cls_s, gain_s, grad_feats)
    grad_y = lax.dynamic_slice_in_dim(grad_cls, mp_index * CROPS, CROPS, 0)
    grad_y = jnp.concatenate([grad_y, jnp.zeros((CLS - CROPS, D), f32)], axis=0)
    proto_square = jnp.sum(grad_proto * grad_proto)
    proto_rows = proto_w.shape[0]

    def pick_proto(i):
        return lax.dynamic_slice_in_dim(grad_proto, unsigned(i * proto_rows), proto_rows, 0)

    proto_g = swap_pieces(pick_proto)
    rows_left = jnp.concatenate([feats_s, b1[:n_s], grad_third], axis=1)
    head_rows = head_w.shape[0]

    right = lax.all_gather(jnp.concatenate([grad_a1, grad_a2, b2_s], axis=1), "dp", axis=0)
    right = right.reshape(dp_count * n_s, 3 * head_cols)
    dwt1, dgains1, grad_x1 = last_bwd(
        CROPS, x1, weights, 3, norm_params[4:8], seg_cls, segment[None], slot, saved1, grad_y
    )
    send1, own1 = core_halves(dwt1, dp_count, core)
    grad_x1, send1, proto_g = lax.optimization_barrier((grad_x1, send1, proto_g))
    got1 = lax.ppermute(send1, "mp", flip_perm(4, 1))
    mlp_args = (weights, 2, norm_params[0:4], saved0[3], grad_x1)
    dwt0, grad_h2 = mlp_bwd(0, *mlp_args)
    grad_h2, got1 = lax.optimization_barrier((grad_h2, got1))
    ring1 = RingScatter(own1 + got1)
    ring1.step(0)
    dwt0, grad_x2, dgains0b = mlp_bwd(1, *mlp_args, (grad_h2, dwt0))
    grad_x2 = ring1.tie(grad_x2)
    ring1.step(1)
    block_args = (weights, 2, norm_params[0:4], seg_col, seg_row, slot, saved0)
    grad_x2, rows_left = lax.optimization_barrier((grad_x2, rows_left))
    left = rows_left.reshape(n_s, dp_count, head_rows).transpose(1, 0, 2)
    left = lax.all_to_all(left, "dp", 0, 0).reshape(dp_count * n_s, head_rows)
    dwt0, grad_h1 = attention_bwd(0, *block_args, grad_x2, dwt0)
    grad_h1 = ring1.tie(grad_h1)
    ring1.step(2)
    dwt0, dgains0a = attention_bwd(1, *block_args, grad_x2, dwt0, (x0, grad_h1))
    send0, own0 = core_halves(dwt0, dp_count, core)
    send0, left, right = lax.optimization_barrier((ring1.tie(send0), left, right))
    stack_ids = dp_index * head_rows + jnp.arange(head_rows)[None, :]
    edges = (0, D, D + HID, D + HID + third.shape[1])
    head_own = sum(
        mm(
            jnp.where((stack_ids >= edges[i]) & (stack_ids < edges[i + 1]), left, 0).astype(bf16),
            right[:, i * head_cols : (i + 1) * head_cols],
            TN,
        )
        for i in range(3)
    )
    ring1.step(3)
    ring0 = RingScatter(own0 + lax.ppermute(send0, "mp", flip_perm(4, 1)))
    ring0.step(0)
    block_g1 = across_sum(ring1.total(), across)
    for index in range(1, RingScatter.steps):
        ring0.step(index)
    block_g = jnp.stack([across_sum(ring0.total(), across), block_g1])
    head_square = jnp.sum(head_own * head_own)
    center_total = gather_over(center_part, "dp").reshape(-1)
    head_first = (mp_index == 0).astype(f32)
    square = head_square + proto_square
    norm_part = jnp.concatenate(
        [
            dgains0a,
            dgains0b,
            dgains1,
            head_first * head_gain,
            head_first * head_bias,
            jnp.full((1, D), square),
            jnp.zeros((5, D), f32),
        ],
        axis=0,
    )
    norm_part = sum_over(norm_part, ("mp",))
    norm_rows_sent = thirds(norm_part).reshape(LAYERS, -1, D)
    columns = jnp.concatenate([block_g.astype(bf16), norm_rows_sent], axis=1)
    columns = ring_gather(columns).transpose(1, 0, 2, 3)
    norm_sum = whole_of(columns[:, :, col_width:])
    norm_total = norm_sum[:10]
    columns, proto_g = lax.optimization_barrier((columns, proto_g))
    proto_g = swap_joined(proto_g).transpose(1, 0, 2).reshape(proto_rows, -1)
    columns = columns[:, :, :col_width].reshape(LAYERS, dp_count * col_width, D)
    wide = columns.astype(f32)
    block_square = sum_over(jnp.full((1, 128), jnp.sum(wide * wide)), ("mp",))[:, :1]
    norm_square = jnp.sum(norm_total * norm_total, axis=(0, 1), keepdims=True)
    grad_norm = jnp.sqrt(norm_sum[10:11, :1] + block_square + norm_square)
    clip_factor = jnp.minimum(1.0, CLIP_NORM / (grad_norm + 1e-06))
    bounds = (0, 384, 512, 896, 1280)
    longest = 384

    own_kind = unsigned(mp_index)
    starts = jnp.array([[bounds[kind ^ flip] for flip in range(4)] for kind in range(4)], jnp.uint32)

    def kind_rows(flip):
        start = lax.dynamic_slice(starts, (own_kind, jnp.uint32(flip)), (1, 1))[0, 0]
        rows = lax.dynamic_slice_in_dim(columns, start, longest, 1)
        inside = (jnp.arange(longest) < 128) | (mp_index != 1 ^ flip)
        return jnp.where(inside[None, :, None], rows, 0).astype(bf16)

    kinds = [kind_rows(0)] + [
        lax.ppermute(kind_rows(flip), "mp", flip_perm(mp_count, flip)) for flip in (1, 2, 3)
    ]
    kinds = jnp.concatenate(kinds, axis=1)
    stat = lax.dot_general(
        kinds, kinds, (((1,), (1,)), ((0,), (0,))), preferred_element_type=f32
    )
    stats_own = lax.dynamic_index_in_dim(precond_stats, own_kind, 1, keepdims=False)
    bases_own = lax.dynamic_index_in_dim(rotation_bases, own_kind, 1, keepdims=False)
    stats_own = SHAMPOO_BETA * stats_own + (1 - SHAMPOO_BETA) * (clip_factor * clip_factor) * stat
    far_stats = lax.ppermute(stats_own, "mp", flip_perm(4, 2))
    stats_own, head_own = lax.optimization_barrier((stats_own, head_own))
    far_head = lax.ppermute(head_own, "mp", flip_perm(4, 2))
    basis_own, late_clip, far_head = lax.optimization_barrier(
        (renew_bases(stats_own, bases_own), clip_factor, far_head)
    )
    head_g = gather_mats(head_own, far_head, across, core).transpose(1, 0, 2)
    head_g = head_g.reshape(head_rows, -1)
    new_head_w, new_head_m, new_head_v = adamw(
        head_w, late_clip * head_g, head_m, head_v, LR_HEAD, WEIGHT_DECAY
    )
    new_proto_w, new_proto_m, new_proto_v = adamw(
        proto_w, late_clip * proto_g, proto_m, proto_v, LR_PROTO, WEIGHT_DECAY
    )
    new_teacher_head = TEACHER_MOM * teacher_head + (1 - TEACHER_MOM) * new_head_w
    new_teacher_proto = TEACHER_MOM * teacher_proto + (1 - TEACHER_MOM) * new_proto_w
    beside = (
        new_head_w, new_head_m, new_head_v, new_proto_w, new_proto_m, new_proto_v,
        new_teacher_head, new_teacher_proto,
    )
    far_bases = lax.ppermute(basis_own, "mp", flip_perm(4, 2))
    far_stats, far_bases, beside = lax.optimization_barrier((far_stats, far_bases, beside))
    new_bases = gather_mats(basis_own, far_bases, across, core)
    new_stats = gather_mats(stats_own, far_stats, across, core).transpose(1, 0, 2, 3)
    (
        new_head_w, new_head_m, new_head_v, new_proto_w, new_proto_m, new_proto_v,
        new_teacher_head, new_teacher_proto,
    ) = beside
    new_bases = new_bases.transpose(1, 0, 2, 3)
    col_ids = dp_index * col_width + jnp.arange(col_width)
    col_masks = jnp.stack(
        [((col_ids >= bounds[k]) & (col_ids < bounds[k + 1])).astype(f32) for k in range(4)]
    )
    grad_cols = clip_factor * block_g
    rotated = jnp.einsum("lkde,lcd,kc->lec", new_bases, grad_cols, col_masks, precision=precise)
    first_mom = ROT_ONE * block_m[:, :, 0] + (1 - ROT_ONE) * rotated
    second_mom = ROT_TWO * block_v[:, :, 0] + (1 - ROT_TWO) * rotated * rotated
    direction = adam_direction(first_mom, second_mom, ROT_ONE, ROT_TWO)
    turned_back = jnp.einsum("lkde,lec,kc->ldc", new_bases, direction, col_masks, precision=precise)
    master = block_w[:, :, 0]
    new_block_w = (master - LR_BLOCK * (turned_back + WEIGHT_DECAY * master))[:, :, None]
    new_norm, new_norm_m, new_norm_v = adamw(
        norm_params, clip_factor * norm_total, norm_m, norm_v, LR_NORM, 0.0
    )
    new_teacher_block = TEACHER_MOM * teacher_block + (1 - TEACHER_MOM) * new_block_w
    new_teacher_norm = TEACHER_MOM * teacher_norm + (1 - TEACHER_MOM) * new_norm
    new_center = CENTER_MOM * center + (1 - CENTER_MOM) * center_total / (2.0 * images)
    return (
        loss_total, grad_norm[0, 0], new_block_w, first_mom[:, :, None], second_mom[:, :, None],
        new_bases, new_stats, new_head_w, new_head_m, new_head_v,
        new_proto_w, new_proto_m, new_proto_v, new_norm, new_norm_m, new_norm_v,
        new_teacher_block, new_teacher_head, new_teacher_proto, new_teacher_norm, new_center,
    )


def solution(mesh):
    block, head, proto, rep = P(None, None, "mp", "dp"), P("dp", None), P("dp", "mp"), P()
    in_specs = (
        P(None, ("dp", "mp"), None), P(None, "dp"), rep, block, block, block, rep, rep,
        head, head, head, proto, proto, proto, rep, rep, rep, block, head, proto, rep, P("mp"),
    )
    out_specs = (
        rep, rep, block, block, block, rep, rep, head, head, head, proto, proto, proto,
        rep, rep, rep, block, head, proto, rep, P("mp"),
    )
    return jax.shard_map(shards, mesh=mesh, in_specs=in_specs, out_specs=out_specs, check_vma=False)
```

```python
import functools

import jax
import jax.numpy as jnp
from jax import lax
from jax.experimental import pallas as pl
from jax.experimental.pallas import tpu as pltpu
from jax.sharding import PartitionSpec as P

D = 384
HD = 64
HID = 2048
LAYERS = 2
SLOT_DEV = 2
GLOBAL_TOK = 197
LOCAL_TOK = 37
MAX_LOCAL = 10
IMG_ROWS = 768
STEP = 10
MICRO = 2
CROPS = 12
GLOBAL_PAD = 200
LOCAL_PAD = 40
CHUNK = 400
CLS = 16

precise = lax.Precision.HIGHEST
TAU_S = 0.1
TAU_T = 0.07
CLIP_NORM = 0.005
BETA_ONE = 0.9
BETA_TWO = 0.999
ROT_ONE = 0.95
ROT_TWO = 0.95
SHAMPOO_BETA = 0.95
ADAM_EPS = 1e-08
WEIGHT_DECAY = 0.04
LR_BLOCK = 0.05
LR_HEAD = 0.03
LR_PROTO = 0.1
LR_NORM = 0.2
TEACHER_MOM = 0.7
CENTER_MOM = 0.9
NN = (((1,), (0,)), ((), ()))
NT = (((1,), (1,)), ((), ()))
TN = (((0,), (0,)), ((), ()))
bf16 = jnp.bfloat16
f32 = jnp.float32
VMEM_LIMIT = 58 * 1024 * 1024


def mm(lhs, rhs, dims=NN, precision=None):
    return lax.dot_general(lhs, rhs, dims, precision=precision, preferred_element_type=f32)


def normalize(inputs):
    centred = inputs - jnp.mean(inputs, axis=-1, keepdims=True)
    spread = jnp.mean(centred * centred, axis=-1, keepdims=True)
    inv = lax.rsqrt(spread + 1e-06)
    return centred * inv, inv


def norm_rows(inputs, gain, bias):
    return normalize(inputs)[0] * gain + bias


def norm_back(inputs, gain, grad_out):
    unit, inv = normalize(inputs)
    scaled = grad_out * gain
    grad = inv * (
        scaled
        - jnp.mean(scaled, axis=-1, keepdims=True)
        - unit * jnp.mean(scaled * unit, axis=-1, keepdims=True)
    )
    return (
        grad,
        jnp.sum(grad_out * unit, axis=0, keepdims=True),
        jnp.sum(grad_out, axis=0, keepdims=True),
    )


def gelu_cdf(inputs):
    return 0.5 + 0.5 * lax.erf(inputs * (0.5**0.5))


def gelu_exact(inputs):
    return inputs * gelu_cdf(inputs)


def gelu_slope(inputs):
    return gelu_cdf(inputs) + inputs * (jnp.exp(-0.5 * inputs * inputs) * 0.3989422804014327)


def low_half(shape):
    return lax.broadcasted_iota(jnp.int32, shape, 1) < HD


def halves(array):
    low = low_half(array.shape)
    zero = jnp.zeros_like(array)
    return jnp.where(low, array, zero), jnp.where(low, zero, array)


def block_fwd_kernel(
    x_ref, wt_ref, gains_ref, seg_col_ref, seg_row_ref, slot_ref,
    out_ref, h1_ref, qkv_ref, o_ref, x2_ref,
):
    x = x_ref[...]
    h1 = norm_rows(x, gains_ref[0:1], gains_ref[1:2]).astype(bf16)
    h1_ref[...] = h1
    allowed = seg_col_ref[0] == seg_row_ref[0]

    def heads(group, att):
        qkv = mm(h1, wt_ref[group, 0:384], NT).astype(bf16)
        qkv_ref[group] = qkv
        keys, values = qkv[:, 128:256], qkv[:, 256:384]
        mixes = []
        for query in halves(qkv[:, 0:128]):
            expd = jnp.where(allowed, jnp.exp(mm(query, keys, NT) * HD ** (-0.5)), 0.0)
            prob = expd / jnp.sum(expd, axis=-1, keepdims=True)
            mixes.append(mm(prob.astype(bf16), values))
        mix = jnp.where(low_half(mixes[0].shape), mixes[0], mixes[1])
        mix = (mix * slot_ref[group]).astype(bf16)
        o_ref[group] = mix
        return att + mm(mix, wt_ref[group, 384:512])

    att = lax.fori_loop(0, wt_ref.shape[0], heads, jnp.zeros(x.shape, f32))
    x2 = x + att
    x2_ref[...] = x2
    h2 = norm_rows(x2, gains_ref[2:3], gains_ref[3:4]).astype(bf16)

    def units(group, total):
        hidden = gelu_exact(mm(h2, wt_ref[group, 512:896], NT)).astype(bf16)
        return total + mm(hidden, wt_ref[group, 896:1280])

    out_ref[...] = x2 + lax.fori_loop(0, wt_ref.shape[0], units, jnp.zeros(x.shape, f32))


def mlp_bwd_kernel(last, wt_ref, gains_ref, x2_ref, grad_ref, *refs):
    if last:
        partial_ref, _, dwt_ref, dx2_ref, dgains_ref = refs
    else:
        dwt_ref, dx2_ref = refs

    @pl.when(pl.program_id(0) == 0)
    def _():
        dwt_ref[...] = jnp.zeros_like(dwt_ref)
        if last:
            dgains_ref[...] = jnp.zeros_like(dgains_ref)

    grad = grad_ref[...]
    grad_low = grad.astype(bf16)
    x2 = x2_ref[...]
    h2 = norm_rows(x2, gains_ref[2:3], gains_ref[3:4]).astype(bf16)

    def units(group, total):
        up = mm(h2, wt_ref[group, 512:896], NT)
        cdf = gelu_cdf(up)
        hidden = (up * cdf).astype(bf16)
        slope = cdf + up * (jnp.exp(-0.5 * up * up) * 0.3989422804014327)
        grad_up = (mm(grad_low, wt_ref[group, 896:1280], NT) * slope).astype(bf16)
        dwt_ref[group, 512:896] += mm(grad_up, h2, TN)
        dwt_ref[group, 896:1280] += mm(hidden, grad_low, TN)
        return total + mm(grad_up, wt_ref[group, 512:896])

    start = partial_ref[...] if last else jnp.zeros(grad.shape, f32)
    grad_h2 = lax.fori_loop(0, wt_ref.shape[0], units, start)
    if last:
        grad_x2, gain_two, bias_two = norm_back(x2, gains_ref[2:3], grad_h2)
        dx2_ref[...] = grad + grad_x2
        dgains_ref[...] += jnp.concatenate([gain_two, bias_two], axis=0)
    else:
        dx2_ref[...] = grad_h2


def attention_bwd_kernel(
    last, wt_ref, gains_ref, seg_col_ref, seg_row_ref, slot_ref, h1_ref, qkv_ref, o_ref, dx2_ref,
    *refs,
):
    if last:
        x_ref, partial_ref, _, dwt_ref, dgains_ref = refs
    else:
        _, dwt_ref, dh1_ref = refs

    @pl.when(pl.program_id(0) == 0)
    def _():
        dwt_ref[...] = jnp.zeros_like(dwt_ref)
        if last:
            dgains_ref[...] = jnp.zeros_like(dgains_ref)

    grad_att = dx2_ref[...].astype(bf16)
    allowed = seg_col_ref[0] == seg_row_ref[0]
    h1 = h1_ref[...]

    def heads(group, total):
        grad_mix = mm(grad_att, wt_ref[group, 384:512], NT).astype(bf16)
        grad_mix = grad_mix * slot_ref[group].astype(bf16)
        dwt_ref[group, 384:512] += mm(o_ref[group], grad_att, TN)
        qkv = qkv_ref[group]
        keys, values = qkv[:, 128:256], qkv[:, 256:384]
        grad_values = jnp.zeros(values.shape, f32)
        grad_keys = jnp.zeros(values.shape, f32)
        grad_queries = []
        for query, gmix in zip(halves(qkv[:, 0:128]), halves(grad_mix)):
            expd = jnp.where(allowed, jnp.exp(mm(query, keys, NT) * HD ** (-0.5)), 0.0)
            prob = expd * (1.0 / jnp.sum(expd, axis=-1, keepdims=True))
            grad_values = grad_values + mm(prob.astype(bf16), gmix, TN)
            grad_prob = mm(gmix, values, NT)
            scored = prob * (grad_prob - jnp.sum(prob * grad_prob, axis=-1, keepdims=True))
            scored = scored.astype(bf16)
            grad_queries.append(mm(scored, keys))
            grad_keys = grad_keys + mm(scored, query, TN)
        low = low_half(grad_queries[0].shape)
        grad_query = jnp.where(low, grad_queries[0], grad_queries[1]) * HD ** (-0.5)
        grad_qkv = jnp.concatenate(
            [grad_query.astype(bf16), (grad_keys * HD ** (-0.5)).astype(bf16), grad_values.astype(bf16)],
            axis=1,
        )
        dwt_ref[group, 0:384] += mm(grad_qkv, h1, TN)
        return total + mm(grad_qkv, wt_ref[group, 0:384])

    start = partial_ref[...] if last else jnp.zeros(h1.shape, f32)
    grad_h1 = lax.fori_loop(0, wt_ref.shape[0], heads, start)
    if last:
        _, gain_one, bias_one = norm_back(x_ref[...], gains_ref[0:1], grad_h1)
        dgains_ref[...] += jnp.concatenate([gain_one, bias_one], axis=0)
    else:
        dh1_ref[...] = grad_h1


def whole_spec(shape):
    return pl.BlockSpec(shape, lambda *_: (0,) * len(shape))


def block_specs(groups, layer):
    row = pl.BlockSpec((CHUNK, D), lambda c: (c, 0))
    return dict(
        row=row,
        wt=pl.BlockSpec((groups, 1280, D), lambda c: (0, 0, layer)),
        gains=whole_spec((4, D)),
        seg_col=pl.BlockSpec((1, CHUNK, 1), lambda c: (c, 0, 0)),
        seg_row=pl.BlockSpec((1, 1, CHUNK), lambda c: (c, 0, 0)),
        slot=whole_spec((groups, 1, 128)),
        qkv=pl.BlockSpec((groups, CHUNK, 384), lambda c: (0, c, 0)),
        mix=pl.BlockSpec((groups, CHUNK, 128), lambda c: (0, c, 0)),
    )


def block_fwd(x, weights, layer, gains, seg_col, seg_row, slot):
    rows, groups = x.shape[0], weights.shape[0]
    s = block_specs(groups, layer)
    return pl.pallas_call(
        block_fwd_kernel,
        grid=(rows // CHUNK,),
        in_specs=[s["row"], s["wt"], s["gains"], s["seg_col"], s["seg_row"], s["slot"]],
        out_specs=[s["row"], s["row"], s["qkv"], s["mix"], s["row"]],
        out_shape=[
            jax.ShapeDtypeStruct((rows, D), f32),
            jax.ShapeDtypeStruct((rows, D), bf16),
            jax.ShapeDtypeStruct((groups, rows, 384), bf16),
            jax.ShapeDtypeStruct((groups, rows, 128), bf16),
            jax.ShapeDtypeStruct((rows, D), f32),
        ],
        compiler_params=pltpu.CompilerParams(vmem_limit_bytes=VMEM_LIMIT),
        cost_estimate=pl.CostEstimate(
            flops=rows * 30_000_000, bytes_accessed=8_000_000, transcendentals=rows * 4000
        ),
    )(x, weights, gains, seg_col, seg_row, slot)


def mlp_bwd(part, weights, layer, gains, x2, grad, last=()):
    rows, groups = x2.shape[0], weights.shape[0] // 2
    s = block_specs(groups, layer)
    half = pl.BlockSpec((groups, 1280, D), lambda c: (part, 0, layer))
    any_spec = [pl.BlockSpec(memory_space=pl.ANY)] if last else []
    args = (weights, gains, x2, grad, *last)
    return pl.pallas_call(
        functools.partial(mlp_bwd_kernel, bool(last)),
        grid=(rows // CHUNK,),
        in_specs=[half, s["gains"], s["row"], s["row"]] + [s["row"]] * len(last[:1]) + any_spec,
        out_specs=[pl.BlockSpec((groups, 1280, D), lambda c: (part, 0, 0)), s["row"]]
        + [whole_spec((2, D))] * len(last[:1]),
        out_shape=[
            jax.ShapeDtypeStruct((2 * groups, 1280, D), f32),
            jax.ShapeDtypeStruct((rows, D), f32),
        ]
        + [jax.ShapeDtypeStruct((2, D), f32)] * len(last[:1]),
        input_output_aliases={len(args) - 1: 0} if last else {},
        compiler_params=pltpu.CompilerParams(vmem_limit_bytes=VMEM_LIMIT),
        cost_estimate=pl.CostEstimate(
            flops=rows * 13_000_000, bytes_accessed=8_000_000, transcendentals=rows * 3000
        ),
    )(*args)


def attention_bwd(part, weights, layer, gains, seg_col, seg_row, slot, saved, grad_x2, dwt, last=()):
    h1, qkv, mix, _ = saved
    rows, groups = h1.shape[0], weights.shape[0] // 2
    s = block_specs(groups, layer)
    heads = pl.BlockSpec((groups, 512, D), lambda c: (part, 0, 0))
    in_specs = [
        pl.BlockSpec((groups, 512, D), lambda c: (part, 0, layer)),
        s["gains"], s["seg_col"], s["seg_row"],
        pl.BlockSpec((groups, 1, 128), lambda c: (part, 0, 0)),
        s["row"],
        pl.BlockSpec((groups, CHUNK, 384), lambda c: (part, c, 0)),
        pl.BlockSpec((groups, CHUNK, 128), lambda c: (part, c, 0)),
        s["row"],
    ] + [s["row"]] * len(last)
    args = (weights, gains, seg_col, seg_row, slot, h1, qkv, mix, grad_x2, *last, dwt)
    return pl.pallas_call(
        functools.partial(attention_bwd_kernel, bool(last)),
        grid=(rows // CHUNK,),
        in_specs=in_specs + [pl.BlockSpec(memory_space=pl.ANY)],
        out_specs=[heads, whole_spec((2, D)) if last else s["row"]],
        out_shape=[
            jax.ShapeDtypeStruct(dwt.shape, f32),
            jax.ShapeDtypeStruct((2, D) if last else (rows, D), f32),
        ],
        input_output_aliases={len(args) - 1: 0},
        compiler_params=pltpu.CompilerParams(vmem_limit_bytes=VMEM_LIMIT),
        cost_estimate=pl.CostEstimate(
            flops=rows * 19_000_000, bytes_accessed=8_000_000, transcendentals=rows * 3000
        ),
    )(*args)


def crop_starts(crops):
    return [
        crop * GLOBAL_PAD if crop < 2 else 2 * GLOBAL_PAD + (crop - 2) * LOCAL_PAD
        for crop in range(crops)
    ]


def take_cls(ref, crops):
    rows = [ref[start : start + 1, :] for start in crop_starts(crops)]
    return jnp.concatenate(rows + [jnp.zeros((CLS - crops, ref.shape[1]), f32)], axis=0)


def last_fwd_kernel(
    crops, x_ref, wt_ref, gains_ref, seg_cls_ref, seg_row_ref, slot_ref,
    out_ref, h1_ref, kv_ref, q_ref, o_ref, x2_ref,
):
    gain, bias = gains_ref[0:1], gains_ref[1:2]
    h1 = norm_rows(x_ref[...], gain, bias).astype(bf16)
    h1_ref[...] = h1
    x_cls = take_cls(x_ref, crops)
    h1_cls = norm_rows(x_cls, gain, bias).astype(bf16)
    allowed = seg_cls_ref[...] == seg_row_ref[...]

    def heads(group, att):
        kv = mm(h1, wt_ref[group, 128:384], NT).astype(bf16)
        kv_ref[group] = kv
        query = mm(h1_cls, wt_ref[group, 0:128], NT).astype(bf16)
        q_ref[group] = query
        both = jnp.concatenate(halves(query), axis=0)
        scores = mm(both, kv[:, 0:128], NT) * HD ** (-0.5)
        expd = jnp.where(allowed, jnp.exp(scores), 0.0)
        prob = expd / jnp.sum(expd, axis=-1, keepdims=True)
        mix = mm(prob.astype(bf16), kv[:, 128:256])
        mix = jnp.where(low_half((CLS, 128)), mix[0:CLS], mix[CLS:])
        mix = (mix * slot_ref[group]).astype(bf16)
        o_ref[group] = mix
        return att + mm(mix, wt_ref[group, 384:512])

    att = lax.fori_loop(0, wt_ref.shape[0], heads, jnp.zeros((CLS, D), f32))
    x2 = x_cls + att
    x2_ref[...] = x2
    h2 = norm_rows(x2, gains_ref[2:3], gains_ref[3:4]).astype(bf16)

    def units(group, total):
        hidden = gelu_exact(mm(h2, wt_ref[group, 512:896], NT)).astype(bf16)
        return total + mm(hidden, wt_ref[group, 896:1280])

    out_ref[...] = x2 + lax.fori_loop(0, wt_ref.shape[0], units, jnp.zeros((CLS, D), f32))


def last_bwd_kernel(
    crops, x_ref, wt_ref, gains_ref, seg_cls_ref, seg_row_ref, slot_ref,
    h1_ref, kv_ref, q_ref, o_ref, x2_ref, grad_ref,
    dwt_ref, dgains_ref, dx_ref,
):
    grad = grad_ref[...]
    grad_low = grad.astype(bf16)
    x2 = x2_ref[...]
    h2 = norm_rows(x2, gains_ref[2:3], gains_ref[3:4]).astype(bf16)
    groups = wt_ref.shape[0]

    def units(group, total):
        up = mm(h2, wt_ref[group, 512:896], NT)
        hidden = gelu_exact(up).astype(bf16)
        grad_up = (mm(grad_low, wt_ref[group, 896:1280], NT) * gelu_slope(up)).astype(bf16)
        dwt_ref[group, 512:896] = mm(grad_up, h2, TN)
        dwt_ref[group, 896:1280] = mm(hidden, grad_low, TN)
        return total + mm(grad_up, wt_ref[group, 512:896])

    grad_h2 = lax.fori_loop(0, groups, units, jnp.zeros((CLS, D), f32))
    grad_x2, gain_two, bias_two = norm_back(x2, gains_ref[2:3], grad_h2)
    grad_x2 = grad + grad_x2
    grad_att = grad_x2.astype(bf16)
    allowed = seg_cls_ref[...] == seg_row_ref[...]
    h1 = h1_ref[...]
    h1_cls = norm_rows(take_cls(x_ref, crops), gains_ref[0:1], gains_ref[1:2]).astype(bf16)

    def heads(group, carry):
        total, total_cls = carry
        grad_mix = mm(grad_att, wt_ref[group, 384:512], NT).astype(bf16)
        grad_mix = grad_mix * slot_ref[group].astype(bf16)
        dwt_ref[group, 384:512] = mm(o_ref[group], grad_att, TN)
        kv = kv_ref[group]
        keys, values = kv[:, 0:128], kv[:, 128:256]
        both = jnp.concatenate(halves(q_ref[group]), axis=0)
        gboth = jnp.concatenate(halves(grad_mix), axis=0)
        expd = jnp.where(allowed, jnp.exp(mm(both, keys, NT) * HD ** (-0.5)), 0.0)
        prob = expd / jnp.sum(expd, axis=-1, keepdims=True)
        grad_prob = mm(gboth, values, NT)
        scored = prob * (grad_prob - jnp.sum(prob * grad_prob, axis=-1, keepdims=True))
        scored = scored.astype(bf16)
        grad_values = mm(prob.astype(bf16), gboth, TN)
        grad_keys = mm(scored, both, TN) * HD ** (-0.5)
        grad_query = mm(scored, keys)
        low = low_half((CLS, 128))
        grad_query = jnp.where(low, grad_query[0:CLS], grad_query[CLS:]) * HD ** (-0.5)
        grad_query = grad_query.astype(bf16)
        grad_kv = jnp.concatenate([grad_keys.astype(bf16), grad_values.astype(bf16)], axis=1)
        dwt_ref[group, 0:128] = mm(grad_query, h1_cls, TN)
        dwt_ref[group, 128:384] = mm(grad_kv, h1, TN)
        return (
            total + mm(grad_kv, wt_ref[group, 128:384]),
            total_cls + mm(grad_query, wt_ref[group, 0:128]),
        )

    grad_h1, grad_cls = lax.fori_loop(
        0, groups, heads, (jnp.zeros(h1.shape, f32), jnp.zeros((CLS, D), f32))
    )
    dx_ref[...] = grad_h1
    starts = crop_starts(crops)
    for crop, start in enumerate(starts):
        dx_ref[start : start + 1, :] += grad_cls[crop : crop + 1, :]
    grad_x, gain_one, bias_one = norm_back(x_ref[...], gains_ref[0:1], dx_ref[...])
    dx_ref[...] = grad_x
    for crop, start in enumerate(starts):
        dx_ref[start : start + 1, :] += grad_x2[crop : crop + 1, :]
    dgains_ref[...] = jnp.concatenate([gain_one, bias_one, gain_two, bias_two], axis=0)


def last_in_specs(rows, groups, layer):
    return [
        whole_spec((rows, D)),
        pl.BlockSpec((groups, 1280, D), lambda i: (0, 0, layer)),
        whole_spec((4, D)),
        whole_spec((2 * CLS, 1)),
        whole_spec((1, rows)),
        whole_spec((groups, 1, 128)),
    ]


def last_saved(rows, groups):
    return [
        jax.ShapeDtypeStruct((rows, D), bf16),
        jax.ShapeDtypeStruct((groups, rows, 256), bf16),
        jax.ShapeDtypeStruct((groups, CLS, 128), bf16),
        jax.ShapeDtypeStruct((groups, CLS, 128), bf16),
        jax.ShapeDtypeStruct((CLS, D), f32),
    ]


def last_fwd(crops, x, weights, layer, gains, seg_cls, seg_row, slot):
    rows, groups = x.shape[0], weights.shape[0]
    out_shape = [jax.ShapeDtypeStruct((CLS, D), f32)] + last_saved(rows, groups)
    return pl.pallas_call(
        functools.partial(last_fwd_kernel, crops),
        grid=(1,),
        in_specs=last_in_specs(rows, groups, layer),
        out_specs=[whole_spec(a.shape) for a in out_shape],
        out_shape=out_shape,
        compiler_params=pltpu.CompilerParams(vmem_limit_bytes=VMEM_LIMIT),
        cost_estimate=pl.CostEstimate(
            flops=rows * 15_000_000, bytes_accessed=8_000_000, transcendentals=rows * 200
        ),
    )(x, weights, gains, seg_cls, seg_row, slot)


def last_bwd(crops, x, weights, layer, gains, seg_cls, seg_row, slot, saved, grad):
    rows, groups = x.shape[0], weights.shape[0]
    out_shape = [
        jax.ShapeDtypeStruct((groups, 1280, D), f32),
        jax.ShapeDtypeStruct((4, D), f32),
        jax.ShapeDtypeStruct((rows, D), f32),
    ]
    return pl.pallas_call(
        functools.partial(last_bwd_kernel, crops),
        grid=(1,),
        in_specs=last_in_specs(rows, groups, layer)
        + [whole_spec(a.shape) for a in last_saved(rows, groups)]
        + [whole_spec((CLS, D))],
        out_specs=[whole_spec(a.shape) for a in out_shape],
        out_shape=out_shape,
        compiler_params=pltpu.CompilerParams(vmem_limit_bytes=VMEM_LIMIT),
        cost_estimate=pl.CostEstimate(
            flops=rows * 20_000_000, bytes_accessed=16_000_000, transcendentals=rows * 400
        ),
    )(x, weights, gains, seg_cls, seg_row, slot, *saved, grad)


PANEL = 32


def panel_steps(panels):
    lanes = lax.broadcasted_iota(jnp.int32, (PANEL, 128), 1)
    ids = lax.broadcasted_iota(jnp.int32, (PANEL, 1), 0)
    panels = list(panels)
    pivots = [jnp.zeros((PANEL, 1), f32) for _ in panels]
    for step in range(PANEL):
        here = lanes == step
        for i, panel in enumerate(panels):
            row = panel[step : step + 1]
            pivot = row[:, step : step + 1]
            column = jnp.where(ids > step, panel[:, step : step + 1], 0.0)
            source = jnp.where(here[0:1], 1.0, row) * (1.0 / pivot)
            cleared = jnp.where(here & (ids > step), 0.0, panel)
            panels[i] = cleared - column * source
            pivots[i] = jnp.where(ids == step, pivot, pivots[i])
    return panels, pivots


def basis_kernel(stats_ref, bases_ref, out_ref, gram_ref, inverse_ref):
    mats = stats_ref.shape[0]
    lanes = lax.broadcasted_iota(jnp.int32, (128, 128), 1)
    rows = lax.broadcasted_iota(jnp.int32, (128, 128), 0)
    near_lanes, near_rows = lanes[:PANEL], rows[:PANEL]
    for mat in range(mats):
        out_ref[mat] = mm(stats_ref[mat], bases_ref[mat], precision=precise)
    for block in range(D // 128):
        low, high = block * 128, block * 128 + 128
        for mat in range(mats):
            part = out_ref[mat, :, low:high]
            gram_ref[mat] = mm(part, part, TN, precise)

        def panels(index, carry):
            first = pl.multiple_of(index * PANEL, PANEL)
            last = first + PANEL
            started = [
                pltpu.roll(gram_ref[mat, pl.ds(first, PANEL), :], 128 - first, 1)
                for mat in range(mats)
            ]
            for mat, (panel, pivots) in enumerate(zip(*panel_steps(started))):
                panel = pltpu.roll(panel, first, 1)
                own = near_lanes - first
                unit = jnp.where(own < near_rows, panel, jnp.where(own == near_rows, 1.0, 0.0))
                inverse_ref[mat, pl.ds(first, PANEL), :] = unit * lax.rsqrt(pivots)
                source = jnp.where(near_lanes < last, unit, panel)
                factors = jnp.where(near_lanes < last, 0.0, panel / pivots)
                gram = gram_ref[mat]
                gram = jnp.where((lanes >= first) & (lanes < last) & (rows >= last), 0.0, gram)
                gram_ref[mat] = gram - mm(factors, source, TN, precise)
            return carry

        lax.fori_loop(0, 128 // PANEL, panels, 0)
        for mat in range(mats):
            part = mm(out_ref[mat, :, low:high], inverse_ref[mat], NT, precise)
            out_ref[mat, :, low:high] = part
            if high < D:
                rest = out_ref[mat, :, high:]
                cross = mm(part, rest, TN, precise)
                out_ref[mat, :, high:] = rest - mm(part, cross, NN, precise)


def renew_bases(new_stats, bases):
    mats = new_stats.shape[0]
    return pl.pallas_call(
        basis_kernel,
        in_specs=[pl.BlockSpec(memory_space=pltpu.VMEM)] * 2,
        out_specs=pl.BlockSpec(memory_space=pltpu.VMEM),
        out_shape=jax.ShapeDtypeStruct((mats, D, D), f32),
        scratch_shapes=[pltpu.VMEM((mats, 128, 128), f32), pltpu.VMEM((mats, 128, 128), f32)],
        compiler_params=pltpu.CompilerParams(vmem_limit_bytes=VMEM_LIMIT),
        cost_estimate=pl.CostEstimate(
            flops=60_000_000_000, bytes_accessed=6_000_000, transcendentals=1000
        ),
    )(new_stats, bases)


def crop_pairs(r_t, r_s):
    rows = lax.broadcasted_iota(jnp.int32, (r_t, r_s), 0)
    crops = lax.broadcasted_iota(jnp.int32, (r_t, r_s), 1)
    first = (rows // 2) * CROPS
    return (crops >= first) & (crops < first + CROPS), rows % 2 == 0


def spread_pairs(values, same, even):
    first = jnp.where(same & even, 1.0, 0.0)
    second = jnp.where(same & ~even, 1.0, 0.0)
    return mm(values, first, NN, precise), mm(values, second, NN, precise)


def logits_kernel(
    zs_ref, zt_ref, ps_ref, pt_ref, center_ref, exp_s_ref, exp_t_ref, stats_ref, part_ref
):
    scaled_s = mm(ps_ref[...], zs_ref[...], (((0,), (1,)), ((), ()))) / TAU_S
    glob = mm(pt_ref[...], zt_ref[...], (((0,), (1,)), ((), ())))
    part_ref[...] = jnp.sum(glob, axis=1, keepdims=True)
    scaled_t = (glob - center_ref[...]) / TAU_T
    max_s = jnp.max(scaled_s, axis=0, keepdims=True)
    max_t = jnp.max(scaled_t, axis=0, keepdims=True)
    exp_s = jnp.exp(scaled_s - max_s)
    exp_t = jnp.exp(scaled_t - max_t)
    exp_s_ref[...] = exp_s
    exp_t_ref[...] = exp_t
    same, even = crop_pairs(exp_t.shape[1], exp_s.shape[1])
    cross = jnp.where(same, mm(exp_t, scaled_s, TN, precise), 0.0)
    stats_ref[...] = jnp.concatenate(
        [
            max_s,
            jnp.sum(exp_s, axis=0, keepdims=True),
            *spread_pairs(max_t, same, even),
            *spread_pairs(jnp.sum(exp_t, axis=0, keepdims=True), same, even),
            jnp.sum(jnp.where(even, cross, 0.0), axis=0, keepdims=True),
            jnp.sum(jnp.where(even, 0.0, cross), axis=0, keepdims=True),
        ],
        axis=0,
    )


def prototype_logits(z_s, z_t, proto_s, proto_t, center):
    cols, r_s, r_t = proto_s.shape[1], z_s.shape[0], z_t.shape[0]
    return pl.pallas_call(
        logits_kernel,
        in_specs=[pl.BlockSpec(memory_space=pltpu.VMEM)] * 5,
        out_specs=[pl.BlockSpec(memory_space=pltpu.VMEM)] * 4,
        out_shape=[
            jax.ShapeDtypeStruct((cols, r_s), f32),
            jax.ShapeDtypeStruct((cols, r_t), f32),
            jax.ShapeDtypeStruct((8, r_s), f32),
            jax.ShapeDtypeStruct((cols, 1), f32),
        ],
        compiler_params=pltpu.CompilerParams(vmem_limit_bytes=VMEM_LIMIT),
        cost_estimate=pl.CostEstimate(
            flops=8_000_000_000, bytes_accessed=8_000_000, transcendentals=1_000_000
        ),
    )(z_s, z_t, proto_s, proto_t, center)


def join_stats(every):
    tops = jnp.max(every, axis=0)

    def add_up(row, shrink):
        return jnp.sum(every[:, row : row + 1] * shrink, axis=0)

    shrink = [jnp.exp(every[:, row : row + 1] - tops[row : row + 1][None]) for row in (0, 2, 3)]
    sums = [add_up(4, shrink[1]), add_up(5, shrink[2]), add_up(6, shrink[1]), add_up(7, shrink[2])]
    return jnp.concatenate([tops[0:1], add_up(1, shrink[0]), tops[2:4], *sums], axis=0)


def loss_kernel(
    all_ref, own_ref, weight_ref, exp_s_ref, exp_t_ref, zs_ref, ps_ref, dz_ref, dproto_ref, loss_ref
):
    every, own = all_ref[...], own_ref[...]
    every = join_stats(every) if every.ndim == 3 else every
    top_s, total_s, top_0, top_1 = every[0:1], every[1:2], every[2:3], every[3:4]
    total_0, total_1, cross_0, cross_1 = every[4:5], every[5:6], every[6:7], every[7:8]
    weight_0, weight_1 = weight_ref[0:1], weight_ref[1:2]
    log_norm = jnp.log(total_s) + top_s
    loss = weight_0 * (log_norm - cross_0 / total_0) + weight_1 * (log_norm - cross_1 / total_1)
    loss_ref[...] = jnp.broadcast_to(jnp.sum(loss, axis=1, keepdims=True), loss_ref.shape)
    coef_s = (weight_0 + weight_1) / total_s * jnp.exp(own[0:1] - top_s)
    coef_0 = weight_0 / total_0 * jnp.exp(own[2:3] - top_0)
    coef_1 = weight_1 / total_1 * jnp.exp(own[3:4] - top_1)
    same, even = crop_pairs(exp_t_ref.shape[1], exp_s_ref.shape[1])
    mix = jnp.where(same, jnp.where(even, coef_0, coef_1), 0.0)
    target = mm(exp_t_ref[...], mix, NN, precise)
    grad = ((coef_s * exp_s_ref[...] - target) / TAU_S).astype(bf16)
    dz_ref[...] = mm(grad, ps_ref[...], (((0,), (1,)), ((), ())))
    dproto_ref[...] = mm(zs_ref[...], grad, (((0,), (1,)), ((), ())))


def loss_and_grads(every, own, weights, exp_s, exp_t, z_s, proto_s):
    return pl.pallas_call(
        loss_kernel,
        in_specs=[pl.BlockSpec(memory_space=pltpu.VMEM)] * 7,
        out_specs=[pl.BlockSpec(memory_space=pltpu.VMEM)] * 3,
        out_shape=[
            jax.ShapeDtypeStruct(z_s.shape, f32),
            jax.ShapeDtypeStruct(proto_s.shape, f32),
            jax.ShapeDtypeStruct((1, 128), f32),
        ],
        compiler_params=pltpu.CompilerParams(vmem_limit_bytes=VMEM_LIMIT),
        cost_estimate=pl.CostEstimate(
            flops=8_000_000_000, bytes_accessed=8_000_000, transcendentals=10_000
        ),
    )(every, own, weights, exp_s, exp_t, z_s, proto_s)


def flip_perm(count, bit):
    return [(i, i ^ bit) for i in range(count)]


def flips(axis):
    count = lax.axis_size(axis)
    bits, bit = [], 1
    while bit < count:
        bits.append(bit)
        bit *= 2
    return count, bits


def thirds(array):
    high = lax.optimization_barrier(array.astype(bf16))
    rest = array - high.astype(f32)
    middle = lax.optimization_barrier(rest.astype(bf16))
    return jnp.stack([high, middle, (rest - middle.astype(f32)).astype(bf16)])


def whole_of(parts):
    layers, count = parts.shape[:2]
    parts = parts.transpose(1, 0, 2, 3).reshape(count, 3, -1, parts.shape[-1]).astype(f32)
    return jnp.sum(parts[:, 0] + (parts[:, 1] + parts[:, 2]), axis=0)


def sum_over(array, axes):
    for axis in axes:
        count, bits = flips(axis)
        for bit in bits:
            array = array + lax.ppermute(array, axis, flip_perm(count, bit))
    return array


def shift_perm(count, step):
    return [(i, (i + step) % count) for i in range(count)]


def gather_over(array, axis):
    count = lax.axis_size(axis)
    if lax.axis_size("dp") > 8:
        return lax.all_gather(array, axis, axis=0)
    return lax.all_to_all(jnp.broadcast_to(array[None], (count, *array.shape)), axis, 0, 0)


def swap_pieces(pick, after=None):
    count = lax.axis_size("dp")
    me = lax.axis_index("dp")
    if count > 8:
        return [lax.all_to_all(jnp.stack([pick(i) for i in range(count)]), "dp", 0, 0)]
    picks = [pick(lax.rem(me + step, count)) for step in range(1, count)]
    if after is not None:
        picks, _ = lax.optimization_barrier((picks, after))
    got = [
        lax.ppermute(piece, "dp", shift_perm(count, step + 1)) for step, piece in enumerate(picks)
    ]
    return [pick(me), *got]


def swap_joined(pieces):
    if len(pieces) == 1:
        return pieces[0]
    count = lax.axis_size("dp")
    out = jnp.zeros((count, *pieces[0].shape), pieces[0].dtype)
    for step, piece in enumerate(pieces):
        out = put(out, piece, lax.rem(lax.axis_index("dp") + (count - step), count))
    return out


RING = (0, 2, 4, 6, 7, 5, 3, 1)


def unsigned(index):
    return lax.convert_element_type(index, jnp.uint32)


def put(out, piece, index):
    return lax.dynamic_update_index_in_dim(out, piece, unsigned(index), 0)


def ring_at(offset):
    count = len(RING)
    table = [RING[(RING.index(i) + offset) % count] for i in range(count)]
    return lax.dynamic_slice(
        jnp.array(table, jnp.uint32), (lax.axis_index("dp").astype(jnp.uint32),), (1,)
    )[0]


def ring_perm(step):
    count = len(RING)
    return [(RING[i], RING[(i + step) % count]) for i in range(count)]


def ring_gather(piece):
    count = lax.axis_size("dp")
    if count != len(RING):
        return lax.all_gather(piece, "dp", axis=0)
    out = put(jnp.zeros((count, *piece.shape), piece.dtype), piece, lax.axis_index("dp"))
    right = left = piece
    for step in range(1, count // 2):
        right = lax.ppermute(right, "dp", ring_perm(1))
        left = lax.ppermute(left, "dp", ring_perm(-1))
        out = put(out, right, ring_at(-step))
        out = put(out, left, ring_at(step))
    half = piece.shape[-2] // 2
    right = lax.ppermute(right[..., :half, :], "dp", ring_perm(1))
    left = lax.ppermute(left[..., half:, :], "dp", ring_perm(-1))
    return put(out, jnp.concatenate([right, left], axis=-2), ring_at(count // 2))


class RingScatter:
    steps = len(RING) // 2

    def __init__(self, parts):
        self.parts = parts
        self.ringed = lax.axis_size("dp") == len(RING)
        self.right = self.left = None
        if self.ringed:
            far = self.own(self.steps)
            self.send_right, self.send_left = far[0:1], far[1:2]

    def own(self, offset):
        return lax.dynamic_index_in_dim(self.parts, ring_at(offset), 1, keepdims=False)

    def step(self, index):
        if not self.ringed:
            return
        if index > 0:
            right, left = self.own(self.steps - index), self.own(index - self.steps)
            if index == 1:
                right = jnp.concatenate([right[0:1] + self.right, right[1:2]])
                left = jnp.concatenate([left[0:1], left[1:2] + self.left])
            else:
                right, left = right + self.right, left + self.left
            self.send_right, self.send_left = right, left
        if index < 2:
            self.send_right = self.send_right.astype(bf16)
            self.send_left = self.send_left.astype(bf16)
        self.right = lax.ppermute(self.send_right, "dp", ring_perm(1))
        self.left = lax.ppermute(self.send_left, "dp", ring_perm(-1))

    def tie(self, other):
        if self.ringed:
            other, self.right, self.left = lax.optimization_barrier((other, self.right, self.left))
        return other

    def total(self):
        if not self.ringed:
            return lax.psum_scatter(self.parts, "dp", scatter_dimension=1, tiled=True)[:, 0]
        return self.own(0) + self.right + self.left


def core_halves(grad, dp_count, core):
    parts = grad.reshape(2, 2, dp_count, -1, D)
    send = lax.dynamic_index_in_dim(parts, unsigned(1 - core), 1, keepdims=False)
    return send, lax.dynamic_index_in_dim(parts, unsigned(core), 1, keepdims=False)


def across_sum(parts, across):
    send = lax.dynamic_index_in_dim(parts, unsigned(1 - across), 0, keepdims=False)
    own = lax.dynamic_index_in_dim(parts, unsigned(across), 0, keepdims=False)
    return own + lax.ppermute(send, "mp", flip_perm(4, 2))


def gather_mats(own, far, across, core):
    pair = put(jnp.stack([own, own]), far, 1 - across)
    other = lax.ppermute(pair, "mp", flip_perm(4, 1))
    whole = jnp.zeros((2, 2, *own.shape), own.dtype)
    whole = lax.dynamic_update_index_in_dim(whole, pair, unsigned(core), 1)
    whole = lax.dynamic_update_index_in_dim(whole, other, unsigned(1 - core), 1)
    return whole.reshape(4, *own.shape)


def adam_direction(first_mom, second_mom, beta_one, beta_two):
    return (
        first_mom / (1 - beta_one**STEP) / (jnp.sqrt(second_mom / (1 - beta_two**STEP)) + ADAM_EPS)
    )


def adamw(weight, grad_in, first_mom, second_mom, rate, decay):
    first_mom = BETA_ONE * first_mom + (1 - BETA_ONE) * grad_in
    second_mom = BETA_TWO * second_mom + (1 - BETA_TWO) * grad_in * grad_in
    weight = weight - rate * (
        adam_direction(first_mom, second_mom, BETA_ONE, BETA_TWO) + decay * weight
    )
    return (weight, first_mom, second_mom)


def row_layout(crop_count):
    rows = jnp.arange(2 * CHUNK)
    is_global = rows < 2 * GLOBAL_PAD
    local = rows - 2 * GLOBAL_PAD
    crop = jnp.where(is_global, rows // GLOBAL_PAD, 2 + local // LOCAL_PAD)
    offset = jnp.where(is_global, rows % GLOBAL_PAD, local % LOCAL_PAD)
    real = offset < jnp.where(is_global, GLOBAL_TOK, LOCAL_TOK)
    source = jnp.where(
        is_global, crop * GLOBAL_TOK + offset, 2 * GLOBAL_TOK + (crop - 2) * LOCAL_TOK + offset
    )
    source = jnp.where(real, source, -1)
    segment = jnp.where(real & (crop < 2 + crop_count), crop, 1000 + rows)
    return source, segment.astype(jnp.int32)


def shards(
    tokens, crop_counts, slot_live, block_w, block_m, block_v, rotation_bases, precond_stats,
    head_w, head_m, head_v, proto_w, proto_m, proto_v, norm_params, norm_m, norm_v,
    teacher_block, teacher_head, teacher_proto, teacher_norm, center,
):
    mp_index = lax.axis_index("mp")
    dp_index = lax.axis_index("dp")
    mp_count = lax.axis_size("mp")
    dp_count = lax.axis_size("dp")
    col_width = block_w.shape[3]
    micro, place = mp_index % MICRO, mp_index // MICRO
    crop_count = crop_counts[micro, place]
    across, core = mp_index // 2, mp_index % 2
    own_t = [teacher_block[layer, :, 0].astype(bf16).T for layer in range(LAYERS)]
    own_s = [block_w[layer, :, 0].astype(bf16).T for layer in range(LAYERS)]
    weights = lax.all_gather(
        jnp.concatenate([*own_t, *own_s], axis=1), ("mp", "dp"), axis=0, tiled=True
    ).reshape(mp_count, -1, 2 * LAYERS * D)
    head_cols = head_w.shape[1] // mp_count
    proto_cols = proto_w.shape[1] // dp_count
    heads = jnp.concatenate(
        [
            lax.dynamic_slice_in_dim(part, unsigned(mp_index * head_cols), head_cols, 1)
            for part in (teacher_head, head_w)
        ],
        axis=1,
    ).astype(bf16)

    def pick_cols(i):
        return jnp.stack(
            [
                lax.dynamic_slice_in_dim(part, unsigned(i * proto_cols), proto_cols, 1).astype(bf16)
                for part in (teacher_proto, proto_w)
            ]
        )

    counts_own = jnp.stack([crop_counts[i % MICRO, i // MICRO] for i in range(mp_count)])
    counts = gather_over(counts_own[None], "dp").reshape(-1)
    other = lax.ppermute(
        lax.dynamic_index_in_dim(tokens, 1 - micro, 0, keepdims=False), "mp", flip_perm(mp_count, 1)
    )
    mine = lax.dynamic_index_in_dim(tokens, micro, 0, keepdims=False)
    first = micro == 0
    image = jnp.concatenate([jnp.where(first, mine, other), jnp.where(first, other, mine)], axis=0)
    source, segment = row_layout(crop_count)
    spread = (source[:, None] == jnp.arange(IMG_ROWS)[None, :]).astype(bf16)
    x0 = mm(spread, image)
    seg_col, seg_row = segment.reshape(2, CHUNK, 1), segment.reshape(2, 1, CHUNK)
    starts = crop_starts(CROPS)
    seg_cls = jnp.concatenate([segment[jnp.array(starts)], jnp.zeros((CLS - CROPS,), jnp.int32)])
    seg_cls = jnp.concatenate([seg_cls, seg_cls])[:, None]
    slot = jnp.repeat(slot_live.astype(f32).reshape(mp_count, SLOT_DEV), HD, axis=1)[:, None, :]
    protos = swap_joined(swap_pieces(pick_cols))
    center_own = lax.dynamic_slice_in_dim(center, unsigned(dp_index * proto_cols), proto_cols)
    center_own = center_own[:, None]
    crop_ids = jnp.arange(CROPS)
    pair_weight = (
        (crop_ids[None, None, :] != jnp.arange(2)[:, None, None])
        & (crop_ids[None, None, :] < 2 + counts[None, :, None])
    ).astype(f32) / (2.0 * counts.astype(f32) + 2.0)[None, :, None]
    pair_weight = pair_weight.reshape(2, -1)
    x0, weights, heads, protos, seg_col, seg_row, seg_cls, slot, center_own, pair_weight = (
        lax.optimization_barrier(
            (x0, weights, heads, protos, seg_col, seg_row, seg_cls, slot, center_own, pair_weight)
        )
    )
    heads = lax.all_gather(heads, "dp", axis=0, tiled=True)
    head_t, head_s = heads[:, :head_cols], heads[:, head_cols:]
    protos = protos.transpose(1, 0, 2, 3).reshape(2, -1, proto_cols)
    proto_t, proto_s = protos[0], protos[1]
    x0_t = x0[:CHUNK]
    x1_t = block_fwd(x0_t, weights, 0, teacher_norm[0:4], seg_col, seg_row, slot)[0]
    x1, *saved0 = block_fwd(x0, weights, 2, norm_params[0:4], seg_col, seg_row, slot)
    y_t = last_fwd(
        2, x1_t, weights, 1, teacher_norm[4:8], seg_cls, segment[None, :CHUNK], slot
    )[0]
    y_s, *saved1 = last_fwd(
        CROPS, x1, weights, 3, norm_params[4:8], seg_cls, segment[None], slot
    )
    y_all = lax.all_gather(jnp.concatenate([y_s[:CROPS], y_t[:4]], axis=0), "mp", axis=0)
    cls_s = y_all[:, :CROPS].reshape(mp_count * CROPS, D)
    cls_t = y_all[:, CROPS : CROPS + 2].reshape(mp_count * 2, D)
    n_s, n_t = cls_s.shape[0], cls_t.shape[0]
    h1_s, h2_s, h3_s = head_s[:D], head_s[D : D + HID], head_s[D + HID :]
    h1_t, h2_t, h3_t = head_t[:D], head_t[D : D + HID], head_t[D + HID :]
    gain_s, bias_s = norm_params[8:9], norm_params[9:10]
    feats_s = norm_rows(cls_s, gain_s, bias_s).astype(bf16)
    feats_t = norm_rows(cls_t, teacher_norm[8:9], teacher_norm[9:10]).astype(bf16)
    a1_s, a1_t = mm(feats_s, h1_s), mm(feats_t, h1_t)
    b1_own = jnp.concatenate([gelu_exact(a1_s), gelu_exact(a1_t)], axis=0).astype(bf16)
    b1 = lax.all_gather(b1_own, "mp", axis=1, tiled=True)
    a2_s, a2_t = mm(b1[:n_s], h2_s), mm(b1[n_s:], h2_t)
    b2_s = gelu_exact(a2_s).astype(bf16)
    b2_t = gelu_exact(a2_t).astype(bf16)
    third = sum_over(jnp.concatenate([mm(b2_s, h3_s, NT), mm(b2_t, h3_t, NT)], axis=0), ("mp",))
    inv = lax.rsqrt(jnp.sum(third * third, axis=-1, keepdims=True) + 1e-06)
    unit = (third * inv).astype(bf16)
    unit_all = gather_over(unit, "dp")
    z_s = unit_all[:, :n_s].reshape(dp_count * n_s, -1)
    z_t = unit_all[:, n_s:].reshape(dp_count * n_t, -1)
    images = dp_count * mp_count
    exp_s, exp_t, own_stats, center_part = prototype_logits(z_s, z_t, proto_s, proto_t, center_own)
    center_part = center_part.reshape(-1)
    all_stats = gather_over(own_stats, ("dp", "mp"))
    if dp_count > 8:
        all_stats = join_stats(all_stats)
    grad_unit_part, grad_proto, loss_total = loss_and_grads(
        all_stats, own_stats, pair_weight, exp_s, exp_t, z_s, proto_s
    )
    loss_total = loss_total[0, 0]
    grad_unit = lax.all_to_all(grad_unit_part.reshape(dp_count, n_s, -1), "dp", 0, 0)
    grad_unit = sum_over(jnp.sum(grad_unit, axis=0), ("mp",))
    third_s, inv_s = third[:n_s], inv[:n_s]
    along = jnp.sum(grad_unit * third_s, axis=-1, keepdims=True)
    grad_third = (inv_s * grad_unit - third_s * (inv_s * inv_s * inv_s * along)).astype(bf16)
    grad_a2 = (mm(grad_third, h3_s) * gelu_slope(a2_s)).astype(bf16)
    grad_b1 = mm(grad_a2, h2_s, NT).reshape(n_s, mp_count, head_cols).transpose(1, 0, 2)
    grad_b1 = jnp.sum(lax.all_to_all(grad_b1, "mp", 0, 0), axis=0)
    grad_a1 = (grad_b1 * gelu_slope(a1_s)).astype(bf16)
    grad_feats = sum_over(mm(grad_a1, h1_s, NT), ("mp",))
    grad_cls, head_gain, head_bias = norm_back(cls_s, gain_s, grad_feats)
    grad_y = lax.dynamic_slice_in_dim(grad_cls, mp_index * CROPS, CROPS, 0)
    grad_y = jnp.concatenate([grad_y, jnp.zeros((CLS - CROPS, D), f32)], axis=0)
    proto_square = jnp.sum(grad_proto * grad_proto)
    proto_rows = proto_w.shape[0]

    def pick_proto(i):
        return lax.dynamic_slice_in_dim(grad_proto, unsigned(i * proto_rows), proto_rows, 0)

    proto_g = swap_pieces(pick_proto)
    rows_left = jnp.concatenate([feats_s, b1[:n_s], grad_third], axis=1)
    head_rows = head_w.shape[0]

    right = lax.all_gather(jnp.concatenate([grad_a1, grad_a2, b2_s], axis=1), "dp", axis=0)
    right = right.reshape(dp_count * n_s, 3 * head_cols)
    dwt1, dgains1, grad_x1 = last_bwd(
        CROPS, x1, weights, 3, norm_params[4:8], seg_cls, segment[None], slot, saved1, grad_y
    )
    send1, own1 = core_halves(dwt1, dp_count, core)
    grad_x1, send1, proto_g = lax.optimization_barrier((grad_x1, send1, proto_g))
    got1 = lax.ppermute(send1, "mp", flip_perm(4, 1))
    mlp_args = (weights, 2, norm_params[0:4], saved0[3], grad_x1)
    dwt0, grad_h2 = mlp_bwd(0, *mlp_args)
    grad_h2, got1 = lax.optimization_barrier((grad_h2, got1))
    ring1 = RingScatter(own1 + got1)
    ring1.step(0)
    dwt0, grad_x2, dgains0b = mlp_bwd(1, *mlp_args, (grad_h2, dwt0))
    grad_x2 = ring1.tie(grad_x2)
    ring1.step(1)
    block_args = (weights, 2, norm_params[0:4], seg_col, seg_row, slot, saved0)
    grad_x2, rows_left = lax.optimization_barrier((grad_x2, rows_left))
    left = rows_left.reshape(n_s, dp_count, head_rows).transpose(1, 0, 2)
    left = lax.all_to_all(left, "dp", 0, 0).reshape(dp_count * n_s, head_rows)
    dwt0, grad_h1 = attention_bwd(0, *block_args, grad_x2, dwt0)
    grad_h1 = ring1.tie(grad_h1)
    ring1.step(2)
    dwt0, dgains0a = attention_bwd(1, *block_args, grad_x2, dwt0, (x0, grad_h1))
    send0, own0 = core_halves(dwt0, dp_count, core)
    send0, left, right = lax.optimization_barrier((ring1.tie(send0), left, right))
    stack_ids = dp_index * head_rows + jnp.arange(head_rows)[None, :]
    edges = (0, D, D + HID, D + HID + third.shape[1])
    head_own = sum(
        mm(
            jnp.where((stack_ids >= edges[i]) & (stack_ids < edges[i + 1]), left, 0).astype(bf16),
            right[:, i * head_cols : (i + 1) * head_cols],
            TN,
        )
        for i in range(3)
    )
    ring1.step(3)
    ring0 = RingScatter(own0 + lax.ppermute(send0, "mp", flip_perm(4, 1)))
    ring0.step(0)
    block_g1 = across_sum(ring1.total(), across)
    for index in range(1, RingScatter.steps):
        ring0.step(index)
    block_g = jnp.stack([across_sum(ring0.total(), across), block_g1])
    head_square = jnp.sum(head_own * head_own)
    center_total = gather_over(center_part, "dp").reshape(-1)
    head_first = (mp_index == 0).astype(f32)
    square = head_square + proto_square
    norm_part = jnp.concatenate(
        [
            dgains0a,
            dgains0b,
            dgains1,
            head_first * head_gain,
            head_first * head_bias,
            jnp.full((1, D), square),
            jnp.zeros((5, D), f32),
        ],
        axis=0,
    )
    norm_part = sum_over(norm_part, ("mp",))
    norm_rows_sent = thirds(norm_part).reshape(LAYERS, -1, D)
    columns = jnp.concatenate([block_g.astype(bf16), norm_rows_sent], axis=1)
    columns = ring_gather(columns).transpose(1, 0, 2, 3)
    norm_sum = whole_of(columns[:, :, col_width:])
    norm_total = norm_sum[:10]
    columns, proto_g = lax.optimization_barrier((columns, proto_g))
    proto_g = swap_joined(proto_g).transpose(1, 0, 2).reshape(proto_rows, -1)
    columns = columns[:, :, :col_width].reshape(LAYERS, dp_count * col_width, D)
    wide = columns.astype(f32)
    block_square = sum_over(jnp.full((1, 128), jnp.sum(wide * wide)), ("mp",))[:, :1]
    norm_square = jnp.sum(norm_total * norm_total, axis=(0, 1), keepdims=True)
    grad_norm = jnp.sqrt(norm_sum[10:11, :1] + block_square + norm_square)
    clip_factor = jnp.minimum(1.0, CLIP_NORM / (grad_norm + 1e-06))
    bounds = (0, 384, 512, 896, 1280)
    longest = 384

    own_kind = unsigned(mp_index)
    starts = jnp.array([[bounds[kind ^ flip] for flip in range(4)] for kind in range(4)], jnp.uint32)

    def kind_rows(flip):
        start = lax.dynamic_slice(starts, (own_kind, jnp.uint32(flip)), (1, 1))[0, 0]
        rows = lax.dynamic_slice_in_dim(columns, start, longest, 1)
        inside = (jnp.arange(longest) < 128) | (mp_index != 1 ^ flip)
        return jnp.where(inside[None, :, None], rows, 0).astype(bf16)

    kinds = [kind_rows(0)] + [
        lax.ppermute(kind_rows(flip), "mp", flip_perm(mp_count, flip)) for flip in (1, 2, 3)
    ]
    kinds = jnp.concatenate(kinds, axis=1)
    stat = lax.dot_general(
        kinds, kinds, (((1,), (1,)), ((0,), (0,))), preferred_element_type=f32
    )
    stats_own = lax.dynamic_index_in_dim(precond_stats, own_kind, 1, keepdims=False)
    bases_own = lax.dynamic_index_in_dim(rotation_bases, own_kind, 1, keepdims=False)
    stats_own = SHAMPOO_BETA * stats_own + (1 - SHAMPOO_BETA) * (clip_factor * clip_factor) * stat
    far_stats = lax.ppermute(stats_own, "mp", flip_perm(4, 2))
    stats_own, head_own = lax.optimization_barrier((stats_own, head_own))
    far_head = lax.ppermute(head_own, "mp", flip_perm(4, 2))
    basis_own, late_clip, far_head = lax.optimization_barrier(
        (renew_bases(stats_own, bases_own), clip_factor, far_head)
    )
    head_g = gather_mats(head_own, far_head, across, core).transpose(1, 0, 2)
    head_g = head_g.reshape(head_rows, -1)
    new_head_w, new_head_m, new_head_v = adamw(
        head_w, late_clip * head_g, head_m, head_v, LR_HEAD, WEIGHT_DECAY
    )
    new_proto_w, new_proto_m, new_proto_v = adamw(
        proto_w, late_clip * proto_g, proto_m, proto_v, LR_PROTO, WEIGHT_DECAY
    )
    new_teacher_head = TEACHER_MOM * teacher_head + (1 - TEACHER_MOM) * new_head_w
    new_teacher_proto = TEACHER_MOM * teacher_proto + (1 - TEACHER_MOM) * new_proto_w
    beside = (
        new_head_w, new_head_m, new_head_v, new_proto_w, new_proto_m, new_proto_v,
        new_teacher_head, new_teacher_proto,
    )
    far_bases = lax.ppermute(basis_own, "mp", flip_perm(4, 2))
    far_stats, far_bases, beside = lax.optimization_barrier((far_stats, far_bases, beside))
    new_bases = gather_mats(basis_own, far_bases, across, core)
    new_stats = gather_mats(stats_own, far_stats, across, core).transpose(1, 0, 2, 3)
    (
        new_head_w, new_head_m, new_head_v, new_proto_w, new_proto_m, new_proto_v,
        new_teacher_head, new_teacher_proto,
    ) = beside
    new_bases = new_bases.transpose(1, 0, 2, 3)
    col_ids = dp_index * col_width + jnp.arange(col_width)
    col_masks = jnp.stack(
        [((col_ids >= bounds[k]) & (col_ids < bounds[k + 1])).astype(f32) for k in range(4)]
    )
    grad_cols = clip_factor * block_g
    rotated = jnp.einsum("lkde,lcd,kc->lec", new_bases, grad_cols, col_masks, precision=precise)
    first_mom = ROT_ONE * block_m[:, :, 0] + (1 - ROT_ONE) * rotated
    second_mom = ROT_TWO * block_v[:, :, 0] + (1 - ROT_TWO) * rotated * rotated
    direction = adam_direction(first_mom, second_mom, ROT_ONE, ROT_TWO)
    turned_back = jnp.einsum("lkde,lec,kc->ldc", new_bases, direction, col_masks, precision=precise)
    master = block_w[:, :, 0]
    new_block_w = (master - LR_BLOCK * (turned_back + WEIGHT_DECAY * master))[:, :, None]
    new_norm, new_norm_m, new_norm_v = adamw(
        norm_params, clip_factor * norm_total, norm_m, norm_v, LR_NORM, 0.0
    )
    new_teacher_block = TEACHER_MOM * teacher_block + (1 - TEACHER_MOM) * new_block_w
    new_teacher_norm = TEACHER_MOM * teacher_norm + (1 - TEACHER_MOM) * new_norm
    new_center = CENTER_MOM * center + (1 - CENTER_MOM) * center_total / (2.0 * images)
    return (
        loss_total, grad_norm[0, 0], new_block_w, first_mom[:, :, None], second_mom[:, :, None],
        new_bases, new_stats, new_head_w, new_head_m, new_head_v,
        new_proto_w, new_proto_m, new_proto_v, new_norm, new_norm_m, new_norm_v,
        new_teacher_block, new_teacher_head, new_teacher_proto, new_teacher_norm, new_center,
    )


def solution(mesh):
    block, head, proto, rep = P(None, None, "mp", "dp"), P("dp", None), P("dp", "mp"), P()
    in_specs = (
        P(None, ("dp", "mp"), None), P(None, "dp"), rep, block, block, block, rep, rep,
        head, head, head, proto, proto, proto, rep, rep, rep, block, head, proto, rep, P("mp"),
    )
    out_specs = (
        rep, rep, block, block, block, rep, rep, head, head, head, proto, proto, proto,
        rep, rep, rep, block, head, proto, rep, P("mp"),
    )
    return jax.shard_map(shards, mesh=mesh, in_specs=in_specs, out_specs=out_specs, check_vma=False)
```

```python
import functools

import jax
import jax.numpy as jnp
from jax import lax
from jax.experimental import pallas as pl
from jax.experimental.pallas import tpu as pltpu
from jax.sharding import PartitionSpec as P

D = 384
HD = 64
HID = 2048
LAYERS = 2
SLOT_DEV = 2
GLOBAL_TOK = 197
LOCAL_TOK = 37
MAX_LOCAL = 10
IMG_ROWS = 768
STEP = 10
MICRO = 2
CROPS = 12
GLOBAL_PAD = 200
LOCAL_PAD = 40
CHUNK = 400
CLS = 16

precise = lax.Precision.HIGHEST
TAU_S = 0.1
TAU_T = 0.07
CLIP_NORM = 0.005
BETA_ONE = 0.9
BETA_TWO = 0.999
ROT_ONE = 0.95
ROT_TWO = 0.95
SHAMPOO_BETA = 0.95
ADAM_EPS = 1e-08
WEIGHT_DECAY = 0.04
LR_BLOCK = 0.05
LR_HEAD = 0.03
LR_PROTO = 0.1
LR_NORM = 0.2
TEACHER_MOM = 0.7
CENTER_MOM = 0.9
NN = (((1,), (0,)), ((), ()))
NT = (((1,), (1,)), ((), ()))
TN = (((0,), (0,)), ((), ()))
bf16 = jnp.bfloat16
f32 = jnp.float32
VMEM_LIMIT = 58 * 1024 * 1024


def mm(lhs, rhs, dims=NN, precision=None):
    return lax.dot_general(lhs, rhs, dims, precision=precision, preferred_element_type=f32)


def normalize(inputs):
    centred = inputs - jnp.mean(inputs, axis=-1, keepdims=True)
    spread = jnp.mean(centred * centred, axis=-1, keepdims=True)
    inv = lax.rsqrt(spread + 1e-06)
    return centred * inv, inv


def norm_rows(inputs, gain, bias):
    return normalize(inputs)[0] * gain + bias


def norm_back(inputs, gain, grad_out):
    unit, inv = normalize(inputs)
    scaled = grad_out * gain
    grad = inv * (
        scaled
        - jnp.mean(scaled, axis=-1, keepdims=True)
        - unit * jnp.mean(scaled * unit, axis=-1, keepdims=True)
    )
    return (
        grad,
        jnp.sum(grad_out * unit, axis=0, keepdims=True),
        jnp.sum(grad_out, axis=0, keepdims=True),
    )


def gelu_cdf(inputs):
    return 0.5 + 0.5 * lax.erf(inputs * (0.5**0.5))


def gelu_exact(inputs):
    return inputs * gelu_cdf(inputs)


def gelu_slope(inputs):
    return gelu_cdf(inputs) + inputs * (jnp.exp(-0.5 * inputs * inputs) * 0.3989422804014327)


def low_half(shape):
    return lax.broadcasted_iota(jnp.int32, shape, 1) < HD


def halves(array):
    low = low_half(array.shape)
    zero = jnp.zeros_like(array)
    return jnp.where(low, array, zero), jnp.where(low, zero, array)


def block_fwd_kernel(
    x_ref, wt_ref, gains_ref, seg_col_ref, seg_row_ref, slot_ref,
    out_ref, h1_ref, qkv_ref, o_ref, x2_ref,
):
    x = x_ref[...]
    h1 = norm_rows(x, gains_ref[0:1], gains_ref[1:2]).astype(bf16)
    h1_ref[...] = h1
    allowed = seg_col_ref[0] == seg_row_ref[0]

    def heads(group, att):
        qkv = mm(h1, wt_ref[group, 0:384], NT).astype(bf16)
        qkv_ref[group] = qkv
        keys, values = qkv[:, 128:256], qkv[:, 256:384]
        mixes = []
        for query in halves(qkv[:, 0:128]):
            expd = jnp.where(allowed, jnp.exp(mm(query, keys, NT) * HD ** (-0.5)), 0.0)
            prob = expd / jnp.sum(expd, axis=-1, keepdims=True)
            mixes.append(mm(prob.astype(bf16), values))
        mix = jnp.where(low_half(mixes[0].shape), mixes[0], mixes[1])
        mix = (mix * slot_ref[group]).astype(bf16)
        o_ref[group] = mix
        return att + mm(mix, wt_ref[group, 384:512])

    att = lax.fori_loop(0, wt_ref.shape[0], heads, jnp.zeros(x.shape, f32))
    x2 = x + att
    x2_ref[...] = x2
    h2 = norm_rows(x2, gains_ref[2:3], gains_ref[3:4]).astype(bf16)

    def units(group, total):
        hidden = gelu_exact(mm(h2, wt_ref[group, 512:896], NT)).astype(bf16)
        return total + mm(hidden, wt_ref[group, 896:1280])

    out_ref[...] = x2 + lax.fori_loop(0, wt_ref.shape[0], units, jnp.zeros(x.shape, f32))


def mlp_bwd_kernel(last, wt_ref, gains_ref, x2_ref, grad_ref, *refs):
    if last:
        partial_ref, _, dwt_ref, dx2_ref, dgains_ref = refs
    else:
        dwt_ref, dx2_ref = refs

    @pl.when(pl.program_id(0) == 0)
    def _():
        dwt_ref[...] = jnp.zeros_like(dwt_ref)
        if last:
            dgains_ref[...] = jnp.zeros_like(dgains_ref)

    grad = grad_ref[...]
    grad_low = grad.astype(bf16)
    x2 = x2_ref[...]
    h2 = norm_rows(x2, gains_ref[2:3], gains_ref[3:4]).astype(bf16)

    def units(group, total):
        up = mm(h2, wt_ref[group, 512:896], NT)
        cdf = gelu_cdf(up)
        hidden = (up * cdf).astype(bf16)
        slope = cdf + up * (jnp.exp(-0.5 * up * up) * 0.3989422804014327)
        grad_up = (mm(grad_low, wt_ref[group, 896:1280], NT) * slope).astype(bf16)
        dwt_ref[group, 512:896] += mm(grad_up, h2, TN)
        dwt_ref[group, 896:1280] += mm(hidden, grad_low, TN)
        return total + mm(grad_up, wt_ref[group, 512:896])

    start = partial_ref[...] if last else jnp.zeros(grad.shape, f32)
    grad_h2 = lax.fori_loop(0, wt_ref.shape[0], units, start)
    if last:
        grad_x2, gain_two, bias_two = norm_back(x2, gains_ref[2:3], grad_h2)
        dx2_ref[...] = grad + grad_x2
        dgains_ref[...] += jnp.concatenate([gain_two, bias_two], axis=0)
    else:
        dx2_ref[...] = grad_h2


def attention_bwd_kernel(
    last, wt_ref, gains_ref, seg_col_ref, seg_row_ref, slot_ref, h1_ref, qkv_ref, o_ref, dx2_ref,
    *refs,
):
    if last:
        x_ref, partial_ref, _, dwt_ref, dgains_ref = refs
    else:
        _, dwt_ref, dh1_ref = refs

    @pl.when(pl.program_id(0) == 0)
    def _():
        dwt_ref[...] = jnp.zeros_like(dwt_ref)
        if last:
            dgains_ref[...] = jnp.zeros_like(dgains_ref)

    grad_att = dx2_ref[...].astype(bf16)
    allowed = seg_col_ref[0] == seg_row_ref[0]
    h1 = h1_ref[...]

    def heads(group, total):
        grad_mix = mm(grad_att, wt_ref[group, 384:512], NT).astype(bf16)
        grad_mix = grad_mix * slot_ref[group].astype(bf16)
        dwt_ref[group, 384:512] += mm(o_ref[group], grad_att, TN)
        qkv = qkv_ref[group]
        keys, values = qkv[:, 128:256], qkv[:, 256:384]
        grad_values = jnp.zeros(values.shape, f32)
        grad_keys = jnp.zeros(values.shape, f32)
        grad_queries = []
        for query, gmix in zip(halves(qkv[:, 0:128]), halves(grad_mix)):
            expd = jnp.where(allowed, jnp.exp(mm(query, keys, NT) * HD ** (-0.5)), 0.0)
            prob = expd * (1.0 / jnp.sum(expd, axis=-1, keepdims=True))
            grad_values = grad_values + mm(prob.astype(bf16), gmix, TN)
            grad_prob = mm(gmix, values, NT)
            scored = prob * (grad_prob - jnp.sum(prob * grad_prob, axis=-1, keepdims=True))
            scored = scored.astype(bf16)
            grad_queries.append(mm(scored, keys))
            grad_keys = grad_keys + mm(scored, query, TN)
        low = low_half(grad_queries[0].shape)
        grad_query = jnp.where(low, grad_queries[0], grad_queries[1]) * HD ** (-0.5)
        grad_qkv = jnp.concatenate(
            [grad_query.astype(bf16), (grad_keys * HD ** (-0.5)).astype(bf16), grad_values.astype(bf16)],
            axis=1,
        )
        dwt_ref[group, 0:384] += mm(grad_qkv, h1, TN)
        return total + mm(grad_qkv, wt_ref[group, 0:384])

    start = partial_ref[...] if last else jnp.zeros(h1.shape, f32)
    grad_h1 = lax.fori_loop(0, wt_ref.shape[0], heads, start)
    if last:
        _, gain_one, bias_one = norm_back(x_ref[...], gains_ref[0:1], grad_h1)
        dgains_ref[...] += jnp.concatenate([gain_one, bias_one], axis=0)
    else:
        dh1_ref[...] = grad_h1


def whole_spec(shape):
    return pl.BlockSpec(shape, lambda *_: (0,) * len(shape))


def block_specs(groups, layer):
    row = pl.BlockSpec((CHUNK, D), lambda c: (c, 0))
    return dict(
        row=row,
        wt=pl.BlockSpec((groups, 1280, D), lambda c: (0, 0, layer)),
        gains=whole_spec((4, D)),
        seg_col=pl.BlockSpec((1, CHUNK, 1), lambda c: (c, 0, 0)),
        seg_row=pl.BlockSpec((1, 1, CHUNK), lambda c: (c, 0, 0)),
        slot=whole_spec((groups, 1, 128)),
        qkv=pl.BlockSpec((groups, CHUNK, 384), lambda c: (0, c, 0)),
        mix=pl.BlockSpec((groups, CHUNK, 128), lambda c: (0, c, 0)),
    )


def block_fwd(x, weights, layer, gains, seg_col, seg_row, slot):
    rows, groups = x.shape[0], weights.shape[0]
    s = block_specs(groups, layer)
    return pl.pallas_call(
        block_fwd_kernel,
        grid=(rows // CHUNK,),
        in_specs=[s["row"], s["wt"], s["gains"], s["seg_col"], s["seg_row"], s["slot"]],
        out_specs=[s["row"], s["row"], s["qkv"], s["mix"], s["row"]],
        out_shape=[
            jax.ShapeDtypeStruct((rows, D), f32),
            jax.ShapeDtypeStruct((rows, D), bf16),
            jax.ShapeDtypeStruct((groups, rows, 384), bf16),
            jax.ShapeDtypeStruct((groups, rows, 128), bf16),
            jax.ShapeDtypeStruct((rows, D), f32),
        ],
        compiler_params=pltpu.CompilerParams(vmem_limit_bytes=VMEM_LIMIT),
        cost_estimate=pl.CostEstimate(
            flops=rows * 30_000_000, bytes_accessed=8_000_000, transcendentals=rows * 4000
        ),
    )(x, weights, gains, seg_col, seg_row, slot)


def mlp_bwd(part, weights, layer, gains, x2, grad, last=()):
    rows, groups = x2.shape[0], weights.shape[0] // 2
    s = block_specs(groups, layer)
    half = pl.BlockSpec((groups, 1280, D), lambda c: (part, 0, layer))
    any_spec = [pl.BlockSpec(memory_space=pl.ANY)] if last else []
    args = (weights, gains, x2, grad, *last)
    return pl.pallas_call(
        functools.partial(mlp_bwd_kernel, bool(last)),
        grid=(rows // CHUNK,),
        in_specs=[half, s["gains"], s["row"], s["row"]] + [s["row"]] * len(last[:1]) + any_spec,
        out_specs=[pl.BlockSpec((groups, 1280, D), lambda c: (part, 0, 0)), s["row"]]
        + [whole_spec((2, D))] * len(last[:1]),
        out_shape=[
            jax.ShapeDtypeStruct((2 * groups, 1280, D), f32),
            jax.ShapeDtypeStruct((rows, D), f32),
        ]
        + [jax.ShapeDtypeStruct((2, D), f32)] * len(last[:1]),
        input_output_aliases={len(args) - 1: 0} if last else {},
        compiler_params=pltpu.CompilerParams(vmem_limit_bytes=VMEM_LIMIT),
        cost_estimate=pl.CostEstimate(
            flops=rows * 13_000_000, bytes_accessed=8_000_000, transcendentals=rows * 3000
        ),
    )(*args)


def attention_bwd(part, weights, layer, gains, seg_col, seg_row, slot, saved, grad_x2, dwt, last=()):
    h1, qkv, mix, _ = saved
    rows, groups = h1.shape[0], weights.shape[0] // 2
    s = block_specs(groups, layer)
    heads = pl.BlockSpec((groups, 512, D), lambda c: (part, 0, 0))
    in_specs = [
        pl.BlockSpec((groups, 512, D), lambda c: (part, 0, layer)),
        s["gains"], s["seg_col"], s["seg_row"],
        pl.BlockSpec((groups, 1, 128), lambda c: (part, 0, 0)),
        s["row"],
        pl.BlockSpec((groups, CHUNK, 384), lambda c: (part, c, 0)),
        pl.BlockSpec((groups, CHUNK, 128), lambda c: (part, c, 0)),
        s["row"],
    ] + [s["row"]] * len(last)
    args = (weights, gains, seg_col, seg_row, slot, h1, qkv, mix, grad_x2, *last, dwt)
    return pl.pallas_call(
        functools.partial(attention_bwd_kernel, bool(last)),
        grid=(rows // CHUNK,),
        in_specs=in_specs + [pl.BlockSpec(memory_space=pl.ANY)],
        out_specs=[heads, whole_spec((2, D)) if last else s["row"]],
        out_shape=[
            jax.ShapeDtypeStruct(dwt.shape, f32),
            jax.ShapeDtypeStruct((2, D) if last else (rows, D), f32),
        ],
        input_output_aliases={len(args) - 1: 0},
        compiler_params=pltpu.CompilerParams(vmem_limit_bytes=VMEM_LIMIT),
        cost_estimate=pl.CostEstimate(
            flops=rows * 19_000_000, bytes_accessed=8_000_000, transcendentals=rows * 3000
        ),
    )(*args)


def crop_starts(crops):
    return [
        crop * GLOBAL_PAD if crop < 2 else 2 * GLOBAL_PAD + (crop - 2) * LOCAL_PAD
        for crop in range(crops)
    ]


def take_cls(ref, crops):
    rows = [ref[start : start + 1, :] for start in crop_starts(crops)]
    return jnp.concatenate(rows + [jnp.zeros((CLS - crops, ref.shape[1]), f32)], axis=0)


def last_fwd_kernel(
    crops, x_ref, wt_ref, gains_ref, seg_cls_ref, seg_row_ref, slot_ref,
    out_ref, h1_ref, kv_ref, q_ref, o_ref, x2_ref,
):
    gain, bias = gains_ref[0:1], gains_ref[1:2]
    h1 = norm_rows(x_ref[...], gain, bias).astype(bf16)
    h1_ref[...] = h1
    x_cls = take_cls(x_ref, crops)
    h1_cls = norm_rows(x_cls, gain, bias).astype(bf16)
    allowed = seg_cls_ref[...] == seg_row_ref[...]

    def heads(group, att):
        kv = mm(h1, wt_ref[group, 128:384], NT).astype(bf16)
        kv_ref[group] = kv
        query = mm(h1_cls, wt_ref[group, 0:128], NT).astype(bf16)
        q_ref[group] = query
        both = jnp.concatenate(halves(query), axis=0)
        scores = mm(both, kv[:, 0:128], NT) * HD ** (-0.5)
        expd = jnp.where(allowed, jnp.exp(scores), 0.0)
        prob = expd / jnp.sum(expd, axis=-1, keepdims=True)
        mix = mm(prob.astype(bf16), kv[:, 128:256])
        mix = jnp.where(low_half((CLS, 128)), mix[0:CLS], mix[CLS:])
        mix = (mix * slot_ref[group]).astype(bf16)
        o_ref[group] = mix
        return att + mm(mix, wt_ref[group, 384:512])

    att = lax.fori_loop(0, wt_ref.shape[0], heads, jnp.zeros((CLS, D), f32))
    x2 = x_cls + att
    x2_ref[...] = x2
    h2 = norm_rows(x2, gains_ref[2:3], gains_ref[3:4]).astype(bf16)

    def units(group, total):
        hidden = gelu_exact(mm(h2, wt_ref[group, 512:896], NT)).astype(bf16)
        return total + mm(hidden, wt_ref[group, 896:1280])

    out_ref[...] = x2 + lax.fori_loop(0, wt_ref.shape[0], units, jnp.zeros((CLS, D), f32))


def last_bwd_kernel(
    crops, x_ref, wt_ref, gains_ref, seg_cls_ref, seg_row_ref, slot_ref,
    h1_ref, kv_ref, q_ref, o_ref, x2_ref, grad_ref,
    dwt_ref, dgains_ref, dx_ref,
):
    grad = grad_ref[...]
    grad_low = grad.astype(bf16)
    x2 = x2_ref[...]
    h2 = norm_rows(x2, gains_ref[2:3], gains_ref[3:4]).astype(bf16)
    groups = wt_ref.shape[0]

    def units(group, total):
        up = mm(h2, wt_ref[group, 512:896], NT)
        hidden = gelu_exact(up).astype(bf16)
        grad_up = (mm(grad_low, wt_ref[group, 896:1280], NT) * gelu_slope(up)).astype(bf16)
        dwt_ref[group, 512:896] = mm(grad_up, h2, TN)
        dwt_ref[group, 896:1280] = mm(hidden, grad_low, TN)
        return total + mm(grad_up, wt_ref[group, 512:896])

    grad_h2 = lax.fori_loop(0, groups, units, jnp.zeros((CLS, D), f32))
    grad_x2, gain_two, bias_two = norm_back(x2, gains_ref[2:3], grad_h2)
    grad_x2 = grad + grad_x2
    grad_att = grad_x2.astype(bf16)
    allowed = seg_cls_ref[...] == seg_row_ref[...]
    h1 = h1_ref[...]
    h1_cls = norm_rows(take_cls(x_ref, crops), gains_ref[0:1], gains_ref[1:2]).astype(bf16)

    def heads(group, carry):
        total, total_cls = carry
        grad_mix = mm(grad_att, wt_ref[group, 384:512], NT).astype(bf16)
        grad_mix = grad_mix * slot_ref[group].astype(bf16)
        dwt_ref[group, 384:512] = mm(o_ref[group], grad_att, TN)
        kv = kv_ref[group]
        keys, values = kv[:, 0:128], kv[:, 128:256]
        both = jnp.concatenate(halves(q_ref[group]), axis=0)
        gboth = jnp.concatenate(halves(grad_mix), axis=0)
        expd = jnp.where(allowed, jnp.exp(mm(both, keys, NT) * HD ** (-0.5)), 0.0)
        prob = expd / jnp.sum(expd, axis=-1, keepdims=True)
        grad_prob = mm(gboth, values, NT)
        scored = prob * (grad_prob - jnp.sum(prob * grad_prob, axis=-1, keepdims=True))
        scored = scored.astype(bf16)
        grad_values = mm(prob.astype(bf16), gboth, TN)
        grad_keys = mm(scored, both, TN) * HD ** (-0.5)
        grad_query = mm(scored, keys)
        low = low_half((CLS, 128))
        grad_query = jnp.where(low, grad_query[0:CLS], grad_query[CLS:]) * HD ** (-0.5)
        grad_query = grad_query.astype(bf16)
        grad_kv = jnp.concatenate([grad_keys.astype(bf16), grad_values.astype(bf16)], axis=1)
        dwt_ref[group, 0:128] = mm(grad_query, h1_cls, TN)
        dwt_ref[group, 128:384] = mm(grad_kv, h1, TN)
        return (
            total + mm(grad_kv, wt_ref[group, 128:384]),
            total_cls + mm(grad_query, wt_ref[group, 0:128]),
        )

    grad_h1, grad_cls = lax.fori_loop(
        0, groups, heads, (jnp.zeros(h1.shape, f32), jnp.zeros((CLS, D), f32))
    )
    dx_ref[...] = grad_h1
    starts = crop_starts(crops)
    for crop, start in enumerate(starts):
        dx_ref[start : start + 1, :] += grad_cls[crop : crop + 1, :]
    grad_x, gain_one, bias_one = norm_back(x_ref[...], gains_ref[0:1], dx_ref[...])
    dx_ref[...] = grad_x
    for crop, start in enumerate(starts):
        dx_ref[start : start + 1, :] += grad_x2[crop : crop + 1, :]
    dgains_ref[...] = jnp.concatenate([gain_one, bias_one, gain_two, bias_two], axis=0)


def last_in_specs(rows, groups, layer):
    return [
        whole_spec((rows, D)),
        pl.BlockSpec((groups, 1280, D), lambda i: (0, 0, layer)),
        whole_spec((4, D)),
        whole_spec((2 * CLS, 1)),
        whole_spec((1, rows)),
        whole_spec((groups, 1, 128)),
    ]


def last_saved(rows, groups):
    return [
        jax.ShapeDtypeStruct((rows, D), bf16),
        jax.ShapeDtypeStruct((groups, rows, 256), bf16),
        jax.ShapeDtypeStruct((groups, CLS, 128), bf16),
        jax.ShapeDtypeStruct((groups, CLS, 128), bf16),
        jax.ShapeDtypeStruct((CLS, D), f32),
    ]


def last_fwd(crops, x, weights, layer, gains, seg_cls, seg_row, slot):
    rows, groups = x.shape[0], weights.shape[0]
    out_shape = [jax.ShapeDtypeStruct((CLS, D), f32)] + last_saved(rows, groups)
    return pl.pallas_call(
        functools.partial(last_fwd_kernel, crops),
        grid=(1,),
        in_specs=last_in_specs(rows, groups, layer),
        out_specs=[whole_spec(a.shape) for a in out_shape],
        out_shape=out_shape,
        compiler_params=pltpu.CompilerParams(vmem_limit_bytes=VMEM_LIMIT),
        cost_estimate=pl.CostEstimate(
            flops=rows * 15_000_000, bytes_accessed=8_000_000, transcendentals=rows * 200
        ),
    )(x, weights, gains, seg_cls, seg_row, slot)


def last_bwd(crops, x, weights, layer, gains, seg_cls, seg_row, slot, saved, grad):
    rows, groups = x.shape[0], weights.shape[0]
    out_shape = [
        jax.ShapeDtypeStruct((groups, 1280, D), f32),
        jax.ShapeDtypeStruct((4, D), f32),
        jax.ShapeDtypeStruct((rows, D), f32),
    ]
    return pl.pallas_call(
        functools.partial(last_bwd_kernel, crops),
        grid=(1,),
        in_specs=last_in_specs(rows, groups, layer)
        + [whole_spec(a.shape) for a in last_saved(rows, groups)]
        + [whole_spec((CLS, D))],
        out_specs=[whole_spec(a.shape) for a in out_shape],
        out_shape=out_shape,
        compiler_params=pltpu.CompilerParams(vmem_limit_bytes=VMEM_LIMIT),
        cost_estimate=pl.CostEstimate(
            flops=rows * 20_000_000, bytes_accessed=16_000_000, transcendentals=rows * 400
        ),
    )(x, weights, gains, seg_cls, seg_row, slot, *saved, grad)


PANEL = 32


def panel_steps(panels):
    lanes = lax.broadcasted_iota(jnp.int32, (PANEL, 128), 1)
    ids = lax.broadcasted_iota(jnp.int32, (PANEL, 1), 0)
    panels = list(panels)
    pivots = [jnp.zeros((PANEL, 1), f32) for _ in panels]
    for step in range(PANEL):
        here = lanes == step
        for i, panel in enumerate(panels):
            row = panel[step : step + 1]
            pivot = row[:, step : step + 1]
            column = jnp.where(ids > step, panel[:, step : step + 1], 0.0)
            source = jnp.where(here[0:1], 1.0, row) * (1.0 / pivot)
            cleared = jnp.where(here & (ids > step), 0.0, panel)
            panels[i] = cleared - column * source
            pivots[i] = jnp.where(ids == step, pivot, pivots[i])
    return panels, pivots


def basis_kernel(stats_ref, bases_ref, out_ref, gram_ref, inverse_ref):
    mats = stats_ref.shape[0]
    lanes = lax.broadcasted_iota(jnp.int32, (128, 128), 1)
    rows = lax.broadcasted_iota(jnp.int32, (128, 128), 0)
    near_lanes, near_rows = lanes[:PANEL], rows[:PANEL]
    for mat in range(mats):
        out_ref[mat] = mm(stats_ref[mat], bases_ref[mat], precision=precise)
    for block in range(D // 128):
        low, high = block * 128, block * 128 + 128
        for mat in range(mats):
            part = out_ref[mat, :, low:high]
            gram_ref[mat] = mm(part, part, TN, precise)

        def panels(index, carry):
            first = pl.multiple_of(index * PANEL, PANEL)
            last = first + PANEL
            started = [
                pltpu.roll(gram_ref[mat, pl.ds(first, PANEL), :], 128 - first, 1)
                for mat in range(mats)
            ]
            for mat, (panel, pivots) in enumerate(zip(*panel_steps(started))):
                panel = pltpu.roll(panel, first, 1)
                own = near_lanes - first
                unit = jnp.where(own < near_rows, panel, jnp.where(own == near_rows, 1.0, 0.0))
                inverse_ref[mat, pl.ds(first, PANEL), :] = unit * lax.rsqrt(pivots)
                source = jnp.where(near_lanes < last, unit, panel)
                factors = jnp.where(near_lanes < last, 0.0, panel / pivots)
                gram = gram_ref[mat]
                gram = jnp.where((lanes >= first) & (lanes < last) & (rows >= last), 0.0, gram)
                gram_ref[mat] = gram - mm(factors, source, TN, precise)
            return carry

        lax.fori_loop(0, 128 // PANEL, panels, 0)
        for mat in range(mats):
            part = mm(out_ref[mat, :, low:high], inverse_ref[mat], NT, precise)
            out_ref[mat, :, low:high] = part
            if high < D:
                rest = out_ref[mat, :, high:]
                cross = mm(part, rest, TN, precise)
                out_ref[mat, :, high:] = rest - mm(part, cross, NN, precise)


def renew_bases(new_stats, bases):
    mats = new_stats.shape[0]
    return pl.pallas_call(
        basis_kernel,
        in_specs=[pl.BlockSpec(memory_space=pltpu.VMEM)] * 2,
        out_specs=pl.BlockSpec(memory_space=pltpu.VMEM),
        out_shape=jax.ShapeDtypeStruct((mats, D, D), f32),
        scratch_shapes=[pltpu.VMEM((mats, 128, 128), f32), pltpu.VMEM((mats, 128, 128), f32)],
        compiler_params=pltpu.CompilerParams(vmem_limit_bytes=VMEM_LIMIT),
        cost_estimate=pl.CostEstimate(
            flops=60_000_000_000, bytes_accessed=6_000_000, transcendentals=1000
        ),
    )(new_stats, bases)


def crop_pairs(r_t, r_s):
    rows = lax.broadcasted_iota(jnp.int32, (r_t, r_s), 0)
    crops = lax.broadcasted_iota(jnp.int32, (r_t, r_s), 1)
    first = (rows // 2) * CROPS
    return (crops >= first) & (crops < first + CROPS), rows % 2 == 0


def spread_pairs(values, same, even):
    first = jnp.where(same & even, 1.0, 0.0)
    second = jnp.where(same & ~even, 1.0, 0.0)
    return mm(values, first, NN, precise), mm(values, second, NN, precise)


def logits_kernel(
    zs_ref, zt_ref, ps_ref, pt_ref, center_ref, exp_s_ref, exp_t_ref, stats_ref, part_ref
):
    scaled_s = mm(ps_ref[...], zs_ref[...], (((0,), (1,)), ((), ()))) / TAU_S
    glob = mm(pt_ref[...], zt_ref[...], (((0,), (1,)), ((), ())))
    part_ref[...] = jnp.sum(glob, axis=1, keepdims=True)
    scaled_t = (glob - center_ref[...]) / TAU_T
    max_s = jnp.max(scaled_s, axis=0, keepdims=True)
    max_t = jnp.max(scaled_t, axis=0, keepdims=True)
    exp_s = jnp.exp(scaled_s - max_s)
    exp_t = jnp.exp(scaled_t - max_t)
    exp_s_ref[...] = exp_s
    exp_t_ref[...] = exp_t
    same, even = crop_pairs(exp_t.shape[1], exp_s.shape[1])
    cross = jnp.where(same, mm(exp_t, scaled_s, TN, precise), 0.0)
    stats_ref[...] = jnp.concatenate(
        [
            max_s,
            jnp.sum(exp_s, axis=0, keepdims=True),
            *spread_pairs(max_t, same, even),
            *spread_pairs(jnp.sum(exp_t, axis=0, keepdims=True), same, even),
            jnp.sum(jnp.where(even, cross, 0.0), axis=0, keepdims=True),
            jnp.sum(jnp.where(even, 0.0, cross), axis=0, keepdims=True),
        ],
        axis=0,
    )


def prototype_logits(z_s, z_t, proto_s, proto_t, center):
    cols, r_s, r_t = proto_s.shape[1], z_s.shape[0], z_t.shape[0]
    return pl.pallas_call(
        logits_kernel,
        in_specs=[pl.BlockSpec(memory_space=pltpu.VMEM)] * 5,
        out_specs=[pl.BlockSpec(memory_space=pltpu.VMEM)] * 4,
        out_shape=[
            jax.ShapeDtypeStruct((cols, r_s), f32),
            jax.ShapeDtypeStruct((cols, r_t), f32),
            jax.ShapeDtypeStruct((8, r_s), f32),
            jax.ShapeDtypeStruct((cols, 1), f32),
        ],
        compiler_params=pltpu.CompilerParams(vmem_limit_bytes=VMEM_LIMIT),
        cost_estimate=pl.CostEstimate(
            flops=8_000_000_000, bytes_accessed=8_000_000, transcendentals=1_000_000
        ),
    )(z_s, z_t, proto_s, proto_t, center)


def join_stats(every):
    tops = jnp.max(every, axis=0)

    def add_up(row, shrink):
        return jnp.sum(every[:, row : row + 1] * shrink, axis=0)

    shrink = [jnp.exp(every[:, row : row + 1] - tops[row : row + 1][None]) for row in (0, 2, 3)]
    sums = [add_up(4, shrink[1]), add_up(5, shrink[2]), add_up(6, shrink[1]), add_up(7, shrink[2])]
    return jnp.concatenate([tops[0:1], add_up(1, shrink[0]), tops[2:4], *sums], axis=0)


def loss_kernel(
    all_ref, own_ref, weight_ref, exp_s_ref, exp_t_ref, zs_ref, ps_ref, dz_ref, dproto_ref, loss_ref
):
    every, own = all_ref[...], own_ref[...]
    every = join_stats(every) if every.ndim == 3 else every
    top_s, total_s, top_0, top_1 = every[0:1], every[1:2], every[2:3], every[3:4]
    total_0, total_1, cross_0, cross_1 = every[4:5], every[5:6], every[6:7], every[7:8]
    weight_0, weight_1 = weight_ref[0:1], weight_ref[1:2]
    log_norm = jnp.log(total_s) + top_s
    loss = weight_0 * (log_norm - cross_0 / total_0) + weight_1 * (log_norm - cross_1 / total_1)
    loss_ref[...] = jnp.broadcast_to(jnp.sum(loss, axis=1, keepdims=True), loss_ref.shape)
    coef_s = (weight_0 + weight_1) / total_s * jnp.exp(own[0:1] - top_s)
    coef_0 = weight_0 / total_0 * jnp.exp(own[2:3] - top_0)
    coef_1 = weight_1 / total_1 * jnp.exp(own[3:4] - top_1)
    same, even = crop_pairs(exp_t_ref.shape[1], exp_s_ref.shape[1])
    mix = jnp.where(same, jnp.where(even, coef_0, coef_1), 0.0)
    target = mm(exp_t_ref[...], mix, NN, precise)
    grad = ((coef_s * exp_s_ref[...] - target) / TAU_S).astype(bf16)
    dz_ref[...] = mm(grad, ps_ref[...], (((0,), (1,)), ((), ())))
    dproto_ref[...] = mm(zs_ref[...], grad, (((0,), (1,)), ((), ())))


def loss_and_grads(every, own, weights, exp_s, exp_t, z_s, proto_s):
    return pl.pallas_call(
        loss_kernel,
        in_specs=[pl.BlockSpec(memory_space=pltpu.VMEM)] * 7,
        out_specs=[pl.BlockSpec(memory_space=pltpu.VMEM)] * 3,
        out_shape=[
            jax.ShapeDtypeStruct(z_s.shape, f32),
            jax.ShapeDtypeStruct(proto_s.shape, f32),
            jax.ShapeDtypeStruct((1, 128), f32),
        ],
        compiler_params=pltpu.CompilerParams(vmem_limit_bytes=VMEM_LIMIT),
        cost_estimate=pl.CostEstimate(
            flops=8_000_000_000, bytes_accessed=8_000_000, transcendentals=10_000
        ),
    )(every, own, weights, exp_s, exp_t, z_s, proto_s)


def flip_perm(count, bit):
    return [(i, i ^ bit) for i in range(count)]


def flips(axis):
    count = lax.axis_size(axis)
    bits, bit = [], 1
    while bit < count:
        bits.append(bit)
        bit *= 2
    return count, bits


def thirds(array):
    high = lax.optimization_barrier(array.astype(bf16))
    rest = array - high.astype(f32)
    middle = lax.optimization_barrier(rest.astype(bf16))
    return jnp.stack([high, middle, (rest - middle.astype(f32)).astype(bf16)])


def whole_of(parts):
    layers, count = parts.shape[:2]
    parts = parts.transpose(1, 0, 2, 3).reshape(count, 3, -1, parts.shape[-1]).astype(f32)
    return jnp.sum(parts[:, 0] + (parts[:, 1] + parts[:, 2]), axis=0)


def sum_over(array, axes):
    for axis in axes:
        count, bits = flips(axis)
        for bit in bits:
            array = array + lax.ppermute(array, axis, flip_perm(count, bit))
    return array


def shift_perm(count, step):
    return [(i, (i + step) % count) for i in range(count)]


def gather_over(array, axis):
    count = lax.axis_size(axis)
    if lax.axis_size("dp") > 8:
        return lax.all_gather(array, axis, axis=0)
    return lax.all_to_all(jnp.broadcast_to(array[None], (count, *array.shape)), axis, 0, 0)


def swap_pieces(pick, after=None):
    count = lax.axis_size("dp")
    me = lax.axis_index("dp")
    if count > 8:
        return [lax.all_to_all(jnp.stack([pick(i) for i in range(count)]), "dp", 0, 0)]
    picks = [pick(lax.rem(me + step, count)) for step in range(1, count)]
    if after is not None:
        picks, _ = lax.optimization_barrier((picks, after))
    got = [
        lax.ppermute(piece, "dp", shift_perm(count, step + 1)) for step, piece in enumerate(picks)
    ]
    return [pick(me), *got]


def swap_joined(pieces):
    if len(pieces) == 1:
        return pieces[0]
    count = lax.axis_size("dp")
    out = jnp.zeros((count, *pieces[0].shape), pieces[0].dtype)
    for step, piece in enumerate(pieces):
        out = put(out, piece, lax.rem(lax.axis_index("dp") + (count - step), count))
    return out


RING = (0, 2, 4, 6, 7, 5, 3, 1)


def unsigned(index):
    return lax.convert_element_type(index, jnp.uint32)


def put(out, piece, index):
    return lax.dynamic_update_index_in_dim(out, piece, unsigned(index), 0)


def ring_at(offset):
    count = len(RING)
    table = [RING[(RING.index(i) + offset) % count] for i in range(count)]
    return lax.dynamic_slice(
        jnp.array(table, jnp.uint32), (lax.axis_index("dp").astype(jnp.uint32),), (1,)
    )[0]


def ring_perm(step):
    count = len(RING)
    return [(RING[i], RING[(i + step) % count]) for i in range(count)]


def ring_gather(piece):
    count = lax.axis_size("dp")
    if count != len(RING):
        return lax.all_gather(piece, "dp", axis=0)
    out = put(jnp.zeros((count, *piece.shape), piece.dtype), piece, lax.axis_index("dp"))
    right = left = piece
    for step in range(1, count // 2):
        right = lax.ppermute(right, "dp", ring_perm(1))
        left = lax.ppermute(left, "dp", ring_perm(-1))
        out = put(out, right, ring_at(-step))
        out = put(out, left, ring_at(step))
    half = piece.shape[-2] // 2
    right = lax.ppermute(right[..., :half, :], "dp", ring_perm(1))
    left = lax.ppermute(left[..., half:, :], "dp", ring_perm(-1))
    return put(out, jnp.concatenate([right, left], axis=-2), ring_at(count // 2))


class RingScatter:
    steps = len(RING) // 2

    def __init__(self, parts):
        self.parts = parts
        self.ringed = lax.axis_size("dp") == len(RING)
        self.right = self.left = None
        if self.ringed:
            far = self.own(self.steps)
            self.send_right, self.send_left = far[0:1], far[1:2]

    def own(self, offset):
        return lax.dynamic_index_in_dim(self.parts, ring_at(offset), 1, keepdims=False)

    def step(self, index):
        if not self.ringed:
            return
        if index > 0:
            right, left = self.own(self.steps - index), self.own(index - self.steps)
            if index == 1:
                right = jnp.concatenate([right[0:1] + self.right, right[1:2]])
                left = jnp.concatenate([left[0:1], left[1:2] + self.left])
            else:
                right, left = right + self.right, left + self.left
            self.send_right, self.send_left = right, left
        if index < 3:
            self.send_right = self.send_right.astype(bf16)
            self.send_left = self.send_left.astype(bf16)
        self.right = lax.ppermute(self.send_right, "dp", ring_perm(1))
        self.left = lax.ppermute(self.send_left, "dp", ring_perm(-1))

    def tie(self, other):
        if self.ringed:
            other, self.right, self.left = lax.optimization_barrier((other, self.right, self.left))
        return other

    def total(self):
        if not self.ringed:
            return lax.psum_scatter(self.parts, "dp", scatter_dimension=1, tiled=True)[:, 0]
        return self.own(0) + self.right + self.left


def core_halves(grad, dp_count, core):
    parts = grad.reshape(2, 2, dp_count, -1, D)
    send = lax.dynamic_index_in_dim(parts, unsigned(1 - core), 1, keepdims=False)
    return send, lax.dynamic_index_in_dim(parts, unsigned(core), 1, keepdims=False)


def across_sum(parts, across):
    send = lax.dynamic_index_in_dim(parts, unsigned(1 - across), 0, keepdims=False)
    own = lax.dynamic_index_in_dim(parts, unsigned(across), 0, keepdims=False)
    return own + lax.ppermute(send, "mp", flip_perm(4, 2))


def gather_mats(own, far, across, core):
    pair = put(jnp.stack([own, own]), far, 1 - across)
    other = lax.ppermute(pair, "mp", flip_perm(4, 1))
    whole = jnp.zeros((2, 2, *own.shape), own.dtype)
    whole = lax.dynamic_update_index_in_dim(whole, pair, unsigned(core), 1)
    whole = lax.dynamic_update_index_in_dim(whole, other, unsigned(1 - core), 1)
    return whole.reshape(4, *own.shape)


def adam_direction(first_mom, second_mom, beta_one, beta_two):
    return (
        first_mom / (1 - beta_one**STEP) / (jnp.sqrt(second_mom / (1 - beta_two**STEP)) + ADAM_EPS)
    )


def adamw(weight, grad_in, first_mom, second_mom, rate, decay):
    first_mom = BETA_ONE * first_mom + (1 - BETA_ONE) * grad_in
    second_mom = BETA_TWO * second_mom + (1 - BETA_TWO) * grad_in * grad_in
    weight = weight - rate * (
        adam_direction(first_mom, second_mom, BETA_ONE, BETA_TWO) + decay * weight
    )
    return (weight, first_mom, second_mom)


def row_layout(crop_count):
    rows = jnp.arange(2 * CHUNK)
    is_global = rows < 2 * GLOBAL_PAD
    local = rows - 2 * GLOBAL_PAD
    crop = jnp.where(is_global, rows // GLOBAL_PAD, 2 + local // LOCAL_PAD)
    offset = jnp.where(is_global, rows % GLOBAL_PAD, local % LOCAL_PAD)
    real = offset < jnp.where(is_global, GLOBAL_TOK, LOCAL_TOK)
    source = jnp.where(
        is_global, crop * GLOBAL_TOK + offset, 2 * GLOBAL_TOK + (crop - 2) * LOCAL_TOK + offset
    )
    source = jnp.where(real, source, -1)
    segment = jnp.where(real & (crop < 2 + crop_count), crop, 1000 + rows)
    return source, segment.astype(jnp.int32)


def shards(
    tokens, crop_counts, slot_live, block_w, block_m, block_v, rotation_bases, precond_stats,
    head_w, head_m, head_v, proto_w, proto_m, proto_v, norm_params, norm_m, norm_v,
    teacher_block, teacher_head, teacher_proto, teacher_norm, center,
):
    mp_index = lax.axis_index("mp")
    dp_index = lax.axis_index("dp")
    mp_count = lax.axis_size("mp")
    dp_count = lax.axis_size("dp")
    col_width = block_w.shape[3]
    micro, place = mp_index % MICRO, mp_index // MICRO
    crop_count = crop_counts[micro, place]
    across, core = mp_index // 2, mp_index % 2
    own_t = [teacher_block[layer, :, 0].astype(bf16).T for layer in range(LAYERS)]
    own_s = [block_w[layer, :, 0].astype(bf16).T for layer in range(LAYERS)]
    weights = lax.all_gather(
        jnp.concatenate([*own_t, *own_s], axis=1), ("mp", "dp"), axis=0, tiled=True
    ).reshape(mp_count, -1, 2 * LAYERS * D)
    head_cols = head_w.shape[1] // mp_count
    proto_cols = proto_w.shape[1] // dp_count
    heads = jnp.concatenate(
        [
            lax.dynamic_slice_in_dim(part, unsigned(mp_index * head_cols), head_cols, 1)
            for part in (teacher_head, head_w)
        ],
        axis=1,
    ).astype(bf16)

    def pick_cols(i):
        return jnp.stack(
            [
                lax.dynamic_slice_in_dim(part, unsigned(i * proto_cols), proto_cols, 1).astype(bf16)
                for part in (teacher_proto, proto_w)
            ]
        )

    counts_own = jnp.stack([crop_counts[i % MICRO, i // MICRO] for i in range(mp_count)])
    counts = gather_over(counts_own[None], "dp").reshape(-1)
    other = lax.ppermute(
        lax.dynamic_index_in_dim(tokens, 1 - micro, 0, keepdims=False), "mp", flip_perm(mp_count, 1)
    )
    mine = lax.dynamic_index_in_dim(tokens, micro, 0, keepdims=False)
    first = micro == 0
    image = jnp.concatenate([jnp.where(first, mine, other), jnp.where(first, other, mine)], axis=0)
    source, segment = row_layout(crop_count)
    spread = (source[:, None] == jnp.arange(IMG_ROWS)[None, :]).astype(bf16)
    x0 = mm(spread, image)
    seg_col, seg_row = segment.reshape(2, CHUNK, 1), segment.reshape(2, 1, CHUNK)
    starts = crop_starts(CROPS)
    seg_cls = jnp.concatenate([segment[jnp.array(starts)], jnp.zeros((CLS - CROPS,), jnp.int32)])
    seg_cls = jnp.concatenate([seg_cls, seg_cls])[:, None]
    slot = jnp.repeat(slot_live.astype(f32).reshape(mp_count, SLOT_DEV), HD, axis=1)[:, None, :]
    protos = swap_joined(swap_pieces(pick_cols))
    center_own = lax.dynamic_slice_in_dim(center, unsigned(dp_index * proto_cols), proto_cols)
    center_own = center_own[:, None]
    crop_ids = jnp.arange(CROPS)
    pair_weight = (
        (crop_ids[None, None, :] != jnp.arange(2)[:, None, None])
        & (crop_ids[None, None, :] < 2 + counts[None, :, None])
    ).astype(f32) / (2.0 * counts.astype(f32) + 2.0)[None, :, None]
    pair_weight = pair_weight.reshape(2, -1)
    x0, weights, heads, protos, seg_col, seg_row, seg_cls, slot, center_own, pair_weight = (
        lax.optimization_barrier(
            (x0, weights, heads, protos, seg_col, seg_row, seg_cls, slot, center_own, pair_weight)
        )
    )
    heads = lax.all_gather(heads, "dp", axis=0, tiled=True)
    head_t, head_s = heads[:, :head_cols], heads[:, head_cols:]
    protos = protos.transpose(1, 0, 2, 3).reshape(2, -1, proto_cols)
    proto_t, proto_s = protos[0], protos[1]
    x0_t = x0[:CHUNK]
    x1_t = block_fwd(x0_t, weights, 0, teacher_norm[0:4], seg_col, seg_row, slot)[0]
    x1, *saved0 = block_fwd(x0, weights, 2, norm_params[0:4], seg_col, seg_row, slot)
    y_t = last_fwd(
        2, x1_t, weights, 1, teacher_norm[4:8], seg_cls, segment[None, :CHUNK], slot
    )[0]
    y_s, *saved1 = last_fwd(
        CROPS, x1, weights, 3, norm_params[4:8], seg_cls, segment[None], slot
    )
    y_all = lax.all_gather(jnp.concatenate([y_s[:CROPS], y_t[:4]], axis=0), "mp", axis=0)
    cls_s = y_all[:, :CROPS].reshape(mp_count * CROPS, D)
    cls_t = y_all[:, CROPS : CROPS + 2].reshape(mp_count * 2, D)
    n_s, n_t = cls_s.shape[0], cls_t.shape[0]
    h1_s, h2_s, h3_s = head_s[:D], head_s[D : D + HID], head_s[D + HID :]
    h1_t, h2_t, h3_t = head_t[:D], head_t[D : D + HID], head_t[D + HID :]
    gain_s, bias_s = norm_params[8:9], norm_params[9:10]
    feats_s = norm_rows(cls_s, gain_s, bias_s).astype(bf16)
    feats_t = norm_rows(cls_t, teacher_norm[8:9], teacher_norm[9:10]).astype(bf16)
    a1_s, a1_t = mm(feats_s, h1_s), mm(feats_t, h1_t)
    b1_own = jnp.concatenate([gelu_exact(a1_s), gelu_exact(a1_t)], axis=0).astype(bf16)
    b1 = lax.all_gather(b1_own, "mp", axis=1, tiled=True)
    a2_s, a2_t = mm(b1[:n_s], h2_s), mm(b1[n_s:], h2_t)
    b2_s = gelu_exact(a2_s).astype(bf16)
    b2_t = gelu_exact(a2_t).astype(bf16)
    third = sum_over(jnp.concatenate([mm(b2_s, h3_s, NT), mm(b2_t, h3_t, NT)], axis=0), ("mp",))
    inv = lax.rsqrt(jnp.sum(third * third, axis=-1, keepdims=True) + 1e-06)
    unit = (third * inv).astype(bf16)
    unit_all = gather_over(unit, "dp")
    z_s = unit_all[:, :n_s].reshape(dp_count * n_s, -1)
    z_t = unit_all[:, n_s:].reshape(dp_count * n_t, -1)
    images = dp_count * mp_count
    exp_s, exp_t, own_stats, center_part = prototype_logits(z_s, z_t, proto_s, proto_t, center_own)
    center_part = center_part.reshape(-1)
    all_stats = gather_over(own_stats, ("dp", "mp"))
    if dp_count > 8:
        all_stats = join_stats(all_stats)
    grad_unit_part, grad_proto, loss_total = loss_and_grads(
        all_stats, own_stats, pair_weight, exp_s, exp_t, z_s, proto_s
    )
    loss_total = loss_total[0, 0]
    grad_unit = lax.all_to_all(grad_unit_part.reshape(dp_count, n_s, -1), "dp", 0, 0)
    grad_unit = sum_over(jnp.sum(grad_unit, axis=0), ("mp",))
    third_s, inv_s = third[:n_s], inv[:n_s]
    along = jnp.sum(grad_unit * third_s, axis=-1, keepdims=True)
    grad_third = (inv_s * grad_unit - third_s * (inv_s * inv_s * inv_s * along)).astype(bf16)
    grad_a2 = (mm(grad_third, h3_s) * gelu_slope(a2_s)).astype(bf16)
    grad_b1 = mm(grad_a2, h2_s, NT).reshape(n_s, mp_count, head_cols).transpose(1, 0, 2)
    grad_b1 = jnp.sum(lax.all_to_all(grad_b1, "mp", 0, 0), axis=0)
    grad_a1 = (grad_b1 * gelu_slope(a1_s)).astype(bf16)
    grad_feats = sum_over(mm(grad_a1, h1_s, NT), ("mp",))
    grad_cls, head_gain, head_bias = norm_back(cls_s, gain_s, grad_feats)
    grad_y = lax.dynamic_slice_in_dim(grad_cls, mp_index * CROPS, CROPS, 0)
    grad_y = jnp.concatenate([grad_y, jnp.zeros((CLS - CROPS, D), f32)], axis=0)
    proto_square = jnp.sum(grad_proto * grad_proto)
    proto_rows = proto_w.shape[0]

    def pick_proto(i):
        return lax.dynamic_slice_in_dim(grad_proto, unsigned(i * proto_rows), proto_rows, 0)

    proto_g = swap_pieces(pick_proto)
    rows_left = jnp.concatenate([feats_s, b1[:n_s], grad_third], axis=1)
    head_rows = head_w.shape[0]

    right = lax.all_gather(jnp.concatenate([grad_a1, grad_a2, b2_s], axis=1), "dp", axis=0)
    right = right.reshape(dp_count * n_s, 3 * head_cols)
    dwt1, dgains1, grad_x1 = last_bwd(
        CROPS, x1, weights, 3, norm_params[4:8], seg_cls, segment[None], slot, saved1, grad_y
    )
    send1, own1 = core_halves(dwt1, dp_count, core)
    grad_x1, send1, proto_g = lax.optimization_barrier((grad_x1, send1, proto_g))
    got1 = lax.ppermute(send1, "mp", flip_perm(4, 1))
    mlp_args = (weights, 2, norm_params[0:4], saved0[3], grad_x1)
    dwt0, grad_h2 = mlp_bwd(0, *mlp_args)
    grad_h2, got1 = lax.optimization_barrier((grad_h2, got1))
    ring1 = RingScatter(own1 + got1)
    ring1.step(0)
    dwt0, grad_x2, dgains0b = mlp_bwd(1, *mlp_args, (grad_h2, dwt0))
    grad_x2 = ring1.tie(grad_x2)
    ring1.step(1)
    block_args = (weights, 2, norm_params[0:4], seg_col, seg_row, slot, saved0)
    grad_x2, rows_left = lax.optimization_barrier((grad_x2, rows_left))
    left = rows_left.reshape(n_s, dp_count, head_rows).transpose(1, 0, 2)
    left = lax.all_to_all(left, "dp", 0, 0).reshape(dp_count * n_s, head_rows)
    dwt0, grad_h1 = attention_bwd(0, *block_args, grad_x2, dwt0)
    grad_h1 = ring1.tie(grad_h1)
    ring1.step(2)
    dwt0, dgains0a = attention_bwd(1, *block_args, grad_x2, dwt0, (x0, grad_h1))
    send0, own0 = core_halves(dwt0, dp_count, core)
    send0, left, right = lax.optimization_barrier((ring1.tie(send0), left, right))
    stack_ids = dp_index * head_rows + jnp.arange(head_rows)[None, :]
    edges = (0, D, D + HID, D + HID + third.shape[1])
    head_own = sum(
        mm(
            jnp.where((stack_ids >= edges[i]) & (stack_ids < edges[i + 1]), left, 0).astype(bf16),
            right[:, i * head_cols : (i + 1) * head_cols],
            TN,
        )
        for i in range(3)
    )
    ring1.step(3)
    ring0 = RingScatter(own0 + lax.ppermute(send0, "mp", flip_perm(4, 1)))
    ring0.step(0)
    block_g1 = across_sum(ring1.total(), across)
    for index in range(1, RingScatter.steps):
        ring0.step(index)
    block_g = jnp.stack([across_sum(ring0.total(), across), block_g1])
    head_square = jnp.sum(head_own * head_own)
    center_total = gather_over(center_part, "dp").reshape(-1)
    head_first = (mp_index == 0).astype(f32)
    square = head_square + proto_square
    norm_part = jnp.concatenate(
        [
            dgains0a,
            dgains0b,
            dgains1,
            head_first * head_gain,
            head_first * head_bias,
            jnp.full((1, D), square),
            jnp.zeros((5, D), f32),
        ],
        axis=0,
    )
    norm_part = sum_over(norm_part, ("mp",))
    norm_rows_sent = thirds(norm_part).reshape(LAYERS, -1, D)
    columns = jnp.concatenate([block_g.astype(bf16), norm_rows_sent], axis=1)
    columns = ring_gather(columns).transpose(1, 0, 2, 3)
    norm_sum = whole_of(columns[:, :, col_width:])
    norm_total = norm_sum[:10]
    columns, proto_g = lax.optimization_barrier((columns, proto_g))
    proto_g = swap_joined(proto_g).transpose(1, 0, 2).reshape(proto_rows, -1)
    columns = columns[:, :, :col_width].reshape(LAYERS, dp_count * col_width, D)
    wide = columns.astype(f32)
    block_square = sum_over(jnp.full((1, 128), jnp.sum(wide * wide)), ("mp",))[:, :1]
    norm_square = jnp.sum(norm_total * norm_total, axis=(0, 1), keepdims=True)
    grad_norm = jnp.sqrt(norm_sum[10:11, :1] + block_square + norm_square)
    clip_factor = jnp.minimum(1.0, CLIP_NORM / (grad_norm + 1e-06))
    bounds = (0, 384, 512, 896, 1280)
    longest = 384

    own_kind = unsigned(mp_index)
    starts = jnp.array([[bounds[kind ^ flip] for flip in range(4)] for kind in range(4)], jnp.uint32)

    def kind_rows(flip):
        start = lax.dynamic_slice(starts, (own_kind, jnp.uint32(flip)), (1, 1))[0, 0]
        rows = lax.dynamic_slice_in_dim(columns, start, longest, 1)
        inside = (jnp.arange(longest) < 128) | (mp_index != 1 ^ flip)
        return jnp.where(inside[None, :, None], rows, 0).astype(bf16)

    kinds = [kind_rows(0)] + [
        lax.ppermute(kind_rows(flip), "mp", flip_perm(mp_count, flip)) for flip in (1, 2, 3)
    ]
    kinds = jnp.concatenate(kinds, axis=1)
    stat = lax.dot_general(
        kinds, kinds, (((1,), (1,)), ((0,), (0,))), preferred_element_type=f32
    )
    stats_own = lax.dynamic_index_in_dim(precond_stats, own_kind, 1, keepdims=False)
    bases_own = lax.dynamic_index_in_dim(rotation_bases, own_kind, 1, keepdims=False)
    stats_own = SHAMPOO_BETA * stats_own + (1 - SHAMPOO_BETA) * (clip_factor * clip_factor) * stat
    far_stats = lax.ppermute(stats_own, "mp", flip_perm(4, 2))
    stats_own, head_own = lax.optimization_barrier((stats_own, head_own))
    far_head = lax.ppermute(head_own, "mp", flip_perm(4, 2))
    basis_own, late_clip, far_head = lax.optimization_barrier(
        (renew_bases(stats_own, bases_own), clip_factor, far_head)
    )
    head_g = gather_mats(head_own, far_head, across, core).transpose(1, 0, 2)
    head_g = head_g.reshape(head_rows, -1)
    new_head_w, new_head_m, new_head_v = adamw(
        head_w, late_clip * head_g, head_m, head_v, LR_HEAD, WEIGHT_DECAY
    )
    new_proto_w, new_proto_m, new_proto_v = adamw(
        proto_w, late_clip * proto_g, proto_m, proto_v, LR_PROTO, WEIGHT_DECAY
    )
    new_teacher_head = TEACHER_MOM * teacher_head + (1 - TEACHER_MOM) * new_head_w
    new_teacher_proto = TEACHER_MOM * teacher_proto + (1 - TEACHER_MOM) * new_proto_w
    beside = (
        new_head_w, new_head_m, new_head_v, new_proto_w, new_proto_m, new_proto_v,
        new_teacher_head, new_teacher_proto,
    )
    far_bases = lax.ppermute(basis_own, "mp", flip_perm(4, 2))
    far_stats, far_bases, beside = lax.optimization_barrier((far_stats, far_bases, beside))
    new_bases = gather_mats(basis_own, far_bases, across, core)
    new_stats = gather_mats(stats_own, far_stats, across, core).transpose(1, 0, 2, 3)
    (
        new_head_w, new_head_m, new_head_v, new_proto_w, new_proto_m, new_proto_v,
        new_teacher_head, new_teacher_proto,
    ) = beside
    new_bases = new_bases.transpose(1, 0, 2, 3)
    col_ids = dp_index * col_width + jnp.arange(col_width)
    col_masks = jnp.stack(
        [((col_ids >= bounds[k]) & (col_ids < bounds[k + 1])).astype(f32) for k in range(4)]
    )
    grad_cols = clip_factor * block_g
    rotated = jnp.einsum("lkde,lcd,kc->lec", new_bases, grad_cols, col_masks, precision=precise)
    first_mom = ROT_ONE * block_m[:, :, 0] + (1 - ROT_ONE) * rotated
    second_mom = ROT_TWO * block_v[:, :, 0] + (1 - ROT_TWO) * rotated * rotated
    direction = adam_direction(first_mom, second_mom, ROT_ONE, ROT_TWO)
    turned_back = jnp.einsum("lkde,lec,kc->ldc", new_bases, direction, col_masks, precision=precise)
    master = block_w[:, :, 0]
    new_block_w = (master - LR_BLOCK * (turned_back + WEIGHT_DECAY * master))[:, :, None]
    new_norm, new_norm_m, new_norm_v = adamw(
        norm_params, clip_factor * norm_total, norm_m, norm_v, LR_NORM, 0.0
    )
    new_teacher_block = TEACHER_MOM * teacher_block + (1 - TEACHER_MOM) * new_block_w
    new_teacher_norm = TEACHER_MOM * teacher_norm + (1 - TEACHER_MOM) * new_norm
    new_center = CENTER_MOM * center + (1 - CENTER_MOM) * center_total / (2.0 * images)
    return (
        loss_total, grad_norm[0, 0], new_block_w, first_mom[:, :, None], second_mom[:, :, None],
        new_bases, new_stats, new_head_w, new_head_m, new_head_v,
        new_proto_w, new_proto_m, new_proto_v, new_norm, new_norm_m, new_norm_v,
        new_teacher_block, new_teacher_head, new_teacher_proto, new_teacher_norm, new_center,
    )


def solution(mesh):
    block, head, proto, rep = P(None, None, "mp", "dp"), P("dp", None), P("dp", "mp"), P()
    in_specs = (
        P(None, ("dp", "mp"), None), P(None, "dp"), rep, block, block, block, rep, rep,
        head, head, head, proto, proto, proto, rep, rep, rep, block, head, proto, rep, P("mp"),
    )
    out_specs = (
        rep, rep, block, block, block, rep, rep, head, head, head, proto, proto, proto,
        rep, rep, rep, block, head, proto, rep, P("mp"),
    )
    return jax.shard_map(shards, mesh=mesh, in_specs=in_specs, out_specs=out_specs, check_vma=False)
```
